128 devices in a mesh: dp: 4 (over z), seq: 4 (over y), expert: 8 (over x, core).
Axes of the slice: x: 4, y: 4, z: 4, core: 2. Of those that a mesh axis runs over, the one named last changes fastest.
Arguments:
- tokens: bfloat16 [8, 2048, 1024], P('expert', ('dp', 'seq')), may hold values from -6 to 6
- cotangent: bfloat16 [8, 2048, 1024], P('expert', ('dp', 'seq')), may hold values from -6 to 6
- doc_lengths: int32 [8, 4], P('expert'), may hold values from 1 to 2044, as said below
- routes: int32 [8, 2048, 8], P('expert', ('dp', 'seq')), may hold values from 0 to 31, all different within a row
- route_rank: int32 [8, 2048], P('expert', ('dp', 'seq')), may hold values from 0 to 127, as said below
- w_qkv: bfloat16 [1024, 2048], P(('dp', 'seq')), may hold values from -0.1875 to 0.1875
- w_o: bfloat16 [1024, 1024], P(('dp', 'seq')), may hold values from -1.5 to 1.5
- norm_gains: bfloat16 [3, 1024], P(None, ('dp', 'seq')), may hold values from 0.5 to 1.5
- key_gain: bfloat16 [512], P(('dp', 'seq')), may hold values from 0.5 to 1.5
- w_router: bfloat16 [1024, 32], P(('dp', 'seq')), may hold values from -0.09375 to 0.09375
- w_in: bfloat16 [32, 1024, 2, 512], P('expert', ('dp', 'seq')), may hold values from -0.1875 to 0.1875
- w_out: bfloat16 [32, 512, 1024], P('expert', ('dp', 'seq')), may hold values from -1 to 1
Outputs:
- output: bfloat16 [8, 2048, 1024], P('expert', ('dp', 'seq'))
- input_grad: float32 [8, 2048, 1024], P('expert', ('dp', 'seq'))
- grad_qkv: float32 [1024, 2048], P(('dp', 'seq'))
- grad_o: float32 [1024, 1024], P(('dp', 'seq'))
- grad_norm_gains: float32 [3, 1024], P(None, ('dp', 'seq'))
- grad_key_gain: float32 [512], P(('dp', 'seq'))
- grad_router: float32 [1024, 32], P(('dp', 'seq'))
- grad_in: float32 [32, 1024, 2, 512], P('expert', ('dp', 'seq'))
- grad_out: float32 [32, 512, 1024], P('expert', ('dp', 'seq'))
The draws below stay inside these ranges and needn't reach their ends.
Inputs may be any that keep to these rules, and one draw needn't show every extreme that they name: `routes`: each row names 8 different experts. `doc_lengths`: the 4 documents of a row lie end to end from the sequence's first position; their sum is below 2048, and the positions after it are padding. `route_rank`: within each aligned block of 128 positions of a sequence every number from 0 to 127 stands once.
All inputs are finite; a program needn't handle non-finite values.
Results may differ from the reference program's by a relative error of at most 0.025.
Values may be sent and summed in bfloat16 or wider, within the bound.
No kernel may reach another device: no remote copies, remote signals or barrier semaphores. Data moves between devices by JAX's collectives and lax.ppermute only.
A program may use at most 192 MiB of HBM per device.

```python
import jax
import jax.numpy as jnp
from jax import lax

D = 1024
HEADS = 16
KV_HEADS = 8
HEAD_DIM = 64
FFE = 512
TOPK = 8
TOK_DEV = 128
NDOCS = 4
HALF = 512
EXPERTS = 32
SEQLEN = 2048
SEQS = 8
CAP = 40
KVW = 512
QKVW = 2048


def draw_doc_lengths(key, part):
    key = jax.random.fold_in(key, 11)
    pick_key, short_key, padding_key = jax.random.split(key, 3)
    limit = SEQLEN // 16
    shorts = jax.random.randint(short_key, (SEQS, NDOCS), 1, limit)
    padding = jax.random.randint(padding_key, (SEQS, 1), 1, limit)
    longest = jax.random.randint(pick_key, (SEQS, 1), 0, NDOCS)
    is_long = jnp.arange(NDOCS)[None, :] == longest
    others = jnp.sum(jnp.where(is_long, 0, shorts), axis=1, keepdims=True)
    return jnp.where(is_long, SEQLEN - padding - others, shorts).astype(jnp.int32)


def draw_route_rank(key, part):
    key = jax.random.fold_in(key, 12)
    block_keys = jax.random.split(key, SEQS * SEQLEN // TOK_DEV)
    ranking = jax.vmap(lambda single: jax.random.permutation(single, TOK_DEV))(block_keys)
    return ranking.reshape(SEQS, SEQLEN).astype(jnp.int32)


def level_of(stream_key, extent, cuts, least, high):
    loudness = 1.0
    for position, parts in cuts:
        draws = jax.random.uniform(jax.random.fold_in(jax.random.fold_in(stream_key, 6), position), (parts,), jnp.float32, least / len(cuts), high / len(cuts))
        loudness = loudness * jnp.repeat(jnp.exp(draws), extent[position] // parts).reshape((-1,) + (1,) * (len(extent) - 1 - position))
    return loudness


def picks_of(rng, rows, count, top, lift):
    order = jax.random.permutation(jax.random.fold_in(rng, 1), count)
    boost = order
    for power in range(3):
        boost = boost * boost // count
    boost = boost * lift // count
    lots = jax.random.randint(jax.random.fold_in(rng, 2), (rows, count), 0, 4096) + boost
    fixed_rows = jax.random.permutation(jax.random.fold_in(rng, 3), rows)[jnp.arange(count) % rows]
    lots = jnp.where(jnp.arange(rows)[:, None] == fixed_rows[None, :], 1 << 14, lots)
    priority = lots * count + jnp.arange(count)
    return lax.top_k(priority.astype(jnp.int32), top)[1].astype(jnp.int32)


def noise(key, extent, deviation, reach, cuts=(), kind=jnp.bfloat16):
    array = jax.random.normal(key, extent, jnp.float32) * deviation
    if len(cuts) > 0:
        array = level_of(key, extent, cuts, -0.22, 0.18) * array
    return jnp.clip(array, min=-reach, max=reach).astype(kind)


def setup_inputs(seed: int = 0) -> dict:
    arg_keys = jax.random.split(jax.random.key(seed), 13)
    return {
        "tokens": noise(arg_keys[0], (SEQS, SEQLEN, D), 1.0, 6.0, ((0, 8), (1, 16))),
        "cotangent": noise(arg_keys[1], (SEQS, SEQLEN, D), 1.0, 6.0, ((0, 8), (1, 16))),
        "doc_lengths": draw_doc_lengths(jax.random.fold_in(arg_keys[12], 71), 0),
        "routes": picks_of(arg_keys[3], SEQS * SEQLEN, EXPERTS, TOPK, 2048).reshape((SEQS, SEQLEN, TOPK)),
        "route_rank": draw_route_rank(jax.random.fold_in(arg_keys[12], 71), 0),
        "w_qkv": noise(arg_keys[5], (D, QKVW), D ** -0.5, 0.1875, ((0, 16),)),
        "w_o": noise(arg_keys[6], (D, D), (D // 64) ** -0.5, 1.5, ((0, 16),)),
        "norm_gains": jnp.clip(1.0 + 0.1 * jax.random.normal(arg_keys[7], (3, D), jnp.float32), 0.5, 1.5).astype(jnp.bfloat16),
        "key_gain": jnp.clip(1.0 + 0.1 * jax.random.normal(arg_keys[8], (KVW,), jnp.float32), 0.5, 1.5).astype(jnp.bfloat16),
        "w_router": noise(arg_keys[9], (D, EXPERTS), (4 * D) ** -0.5, 0.09375, ((0, 16),)),
        "w_in": noise(arg_keys[10], (EXPERTS, D, 2, FFE), D ** -0.5, 0.1875, ((0, 8), (1, 16))),
        "w_out": noise(arg_keys[11], (EXPERTS, FFE, D), (FFE // 16) ** -0.5, 1.0, ((0, 8), (1, 16))),
    }


epsilon = 1e-05
highest = lax.Precision.HIGHEST

@jax.custom_vjp
def low(v):
    return lax.optimization_barrier(v.astype(jnp.bfloat16)).astype(jnp.float32)

@jax.custom_vjp
def low_back(v):
    return v

def low_keep(v):
    return (low(v), None)

def low_pass(kept, grad):
    return (grad,)

def back_keep(v):
    return (v, None)

def back_low(kept, grad):
    return (low(grad),)
low.defvjp(low_keep, low_pass)
low_back.defvjp(back_keep, back_low)

def norm_rows(matrix, gain_row):
    return matrix * lax.rsqrt(lax.optimization_barrier(jnp.mean(matrix * matrix, axis=-1, keepdims=True)) + epsilon) * gain_row

def rotate(heads_rows, positions):
    half_dim = heads_rows.shape[-1] // 2
    frequency = 10000.0 ** (-jnp.arange(half_dim, dtype=jnp.float32) / half_dim)
    angles = positions.astype(jnp.float32)[:, None] * frequency[None, :]
    cosine = jnp.cos(angles)[:, None, :]
    sine = jnp.sin(angles)[:, None, :]
    front = heads_rows[..., :half_dim]
    behind = heads_rows[..., half_dim:]
    return jnp.concatenate([front * cosine - behind * sine, behind * cosine + front * sine], axis=-1)

def documents(lengths, places):
    ends = jnp.cumsum(lengths).astype(jnp.int32)
    doc_ids = lax.optimization_barrier(jnp.sum((places[:, None] >= ends[None, :]).astype(jnp.int32), axis=1)).astype(jnp.int32)
    starts = jnp.concatenate([jnp.zeros((1,), jnp.int32), ends])
    marks = jnp.arange(starts.shape[0], dtype=jnp.int32)
    begins = lax.optimization_barrier(jnp.sum(jnp.where(doc_ids[:, None] == marks[None, :], starts[None, :], 0), axis=1)).astype(jnp.int32)
    return (doc_ids, places - begins)

def window_attention(queries, keys_all, values_all, doc_ids):
    seq_length = queries.shape[0]
    block_rows = min(512, seq_length)
    groups_per = HEADS // KV_HEADS
    window_rows = block_rows + 2 * HALF
    grouped = queries.reshape(seq_length // block_rows, block_rows, KV_HEADS, groups_per, HEAD_DIM)
    keys_pad = jnp.pad(keys_all, ((HALF, HALF), (0, 0), (0, 0)))
    values_pad = jnp.pad(values_all, ((HALF, HALF), (0, 0), (0, 0)))
    docs_pad = jnp.pad(doc_ids, (HALF, HALF), constant_values=-1)
    score_scale = HEAD_DIM ** (-0.5)
    offsets = jnp.arange(window_rows, dtype=jnp.int32)[None, :] - HALF - jnp.arange(block_rows, dtype=jnp.int32)[:, None]
    in_window = (offsets >= -HALF) & (offsets < HALF)

    def one_block(block_index):
        begin_row = (block_index * block_rows).astype(jnp.int32)
        query_block = grouped[block_index]
        key_block = lax.dynamic_slice_in_dim(keys_pad, begin_row, window_rows, 0)
        value_block = lax.dynamic_slice_in_dim(values_pad, begin_row, window_rows, 0)
        query_docs = lax.dynamic_slice_in_dim(doc_ids, begin_row, block_rows, 0)
        key_docs = lax.dynamic_slice_in_dim(docs_pad, begin_row, window_rows, 0)
        allowed = in_window & (query_docs[:, None] == key_docs[None, :])
        scores = jnp.einsum('qkgd,mkd->kgqm', query_block, key_block, precision=highest) * score_scale
        scores = low_back(scores)
        scores = jnp.where(allowed[None, None], scores, -1e+30)
        largest = lax.optimization_barrier(jnp.max(scores, axis=-1, keepdims=True))
        weights = jnp.exp(scores - largest)
        probs = low(weights / lax.optimization_barrier(jnp.sum(weights, axis=-1, keepdims=True)))
        mixed = jnp.einsum('kgqm,mkd->qkgd', probs, value_block, precision=highest)
        return mixed.reshape(block_rows, HEADS * HEAD_DIM)
    blocks_out = lax.map(jax.checkpoint(one_block), jnp.arange(seq_length // block_rows, dtype=jnp.int32))
    return blocks_out.reshape(seq_length, HEADS * HEAD_DIM)

def experts_mix(normed, chosen_ids, ranking, w_router, w_in, w_out):
    seq_length = normed.shape[0]
    stretch_total = seq_length // TOK_DEV
    logits = jnp.dot(normed, w_router, precision=highest)
    picked = chosen_ids[:, :, None] == jnp.arange(EXPERTS, dtype=jnp.int32)[None, None, :]
    chosen = lax.optimization_barrier(jnp.sum(jnp.where(picked, logits[:, None, :], 0.0), axis=2))
    gates = jax.nn.softmax(chosen, axis=1)
    used = lax.optimization_barrier(jnp.sum(picked.astype(jnp.float32), axis=1)).reshape(stretch_total, TOK_DEV, EXPERTS)
    ordering = ranking.reshape(stretch_total, TOK_DEV)
    earlier = (ordering[:, None, :] < ordering[:, :, None]).astype(jnp.float32)
    before = jnp.einsum('ctu,cue->cte', earlier, used, precision=highest).reshape(seq_length, 1, EXPERTS)
    ahead_count = lax.optimization_barrier(jnp.sum(jnp.where(picked, before, 0.0), axis=2)).astype(jnp.int32)
    kept = ahead_count < CAP
    target = jnp.where(kept, chosen_ids * CAP + ahead_count, EXPERTS * CAP).reshape(stretch_total, TOK_DEV * TOPK)
    owners = jnp.repeat(jnp.arange(TOK_DEV, dtype=jnp.int32), TOPK)
    stretch_rows = jnp.arange(stretch_total, dtype=jnp.int32)[:, None]
    token_of = jnp.zeros((stretch_total, EXPERTS * CAP + 1), jnp.int32).at[stretch_rows, target].set(owners[None, :] + stretch_rows * TOK_DEV)
    filled = jnp.zeros((stretch_total, EXPERTS * CAP + 1), jnp.float32).at[stretch_rows, target].set(1.0)
    slot_rows = normed[token_of[:, :-1]] * filled[:, :-1, None]
    slot_rows = slot_rows.reshape(stretch_total, EXPERTS, CAP, D).transpose(1, 0, 2, 3).reshape(EXPERTS, stretch_total * CAP, D)
    slot_rows = low_back(slot_rows)
    both = low_back(jnp.einsum('erd,edf->erf', slot_rows, w_in.reshape(EXPERTS, D, 2 * FFE), precision=highest))
    hidden = low(jax.nn.silu(both[..., :FFE]) * both[..., FFE:])
    result = low(low_back(jnp.einsum('erf,efd->erd', hidden, w_out, precision=highest)))
    flat_rows = result.reshape(EXPERTS * stretch_total * CAP, D)
    stretch_of = (jnp.arange(seq_length, dtype=jnp.int32) // TOK_DEV)[:, None]
    where_row = (chosen_ids * stretch_total + stretch_of) * CAP + jnp.minimum(ahead_count, CAP - 1)
    taken = flat_rows[where_row]
    weight = gates * kept.astype(jnp.float32)
    return lax.optimization_barrier(jnp.sum(weight[:, :, None] * taken, axis=1))

def layer(inputs, lengths, chosen_ids, ranking, w_qkv, w_o, norm_gains, key_gain, w_router, w_in, w_out):
    seq_length = inputs.shape[0]
    places = jnp.arange(seq_length, dtype=jnp.int32)
    doc_ids, positions = documents(lengths, places)
    first_low = low(norm_rows(inputs, norm_gains[0]))
    projected = low_back(jnp.dot(first_low, w_qkv, precision=highest))
    queries = norm_rows(projected[:, :D], norm_gains[2]).reshape(seq_length, HEADS, HEAD_DIM)
    keys_all = norm_rows(projected[:, D:D + KVW], key_gain).reshape(seq_length, KV_HEADS, HEAD_DIM)
    values_all = projected[:, D + KVW:].reshape(seq_length, KV_HEADS, HEAD_DIM)
    queries = low(low_back(rotate(queries, positions)))
    keys_all = low(low_back(rotate(keys_all, positions)))
    values_all = low(low_back(values_all))
    attended = low(low_back(window_attention(queries, keys_all, values_all, doc_ids)))
    middle = inputs + low_back(jnp.dot(attended, w_o, precision=highest))
    second_low = low(norm_rows(middle, norm_gains[1]))
    return middle + experts_mix(second_low, chosen_ids, ranking, w_router, w_in, w_out)

def reference(tokens, cotangent, doc_lengths, routes, route_rank, w_qkv, w_o, norm_gains, key_gain, w_router, w_in, w_out):

    def forward(inputs, qkv_weight, out_weight, gain_rows, key_gain_row, router_weight, in_weight, down_weight):

        def step(carried, item):
            seq_rows, lengths, chosen_ids, ranking = item
            return (carried, layer(seq_rows, lengths, chosen_ids, ranking, qkv_weight, out_weight, gain_rows, key_gain_row, router_weight, in_weight, down_weight))
        _, result = lax.scan(jax.checkpoint(step), jnp.zeros((), jnp.float32), (inputs, doc_lengths, routes, route_rank))
        return result
    result, pullback = jax.vjp(forward, tokens.astype(jnp.float32), w_qkv.astype(jnp.float32), w_o.astype(jnp.float32), norm_gains.astype(jnp.float32), key_gain.astype(jnp.float32), w_router.astype(jnp.float32), w_in.astype(jnp.float32), w_out.astype(jnp.float32))
    grads = pullback(cotangent.astype(jnp.float32))
    return (result.astype(jnp.bfloat16), grads[0], grads[1], grads[2], grads[3], grads[4], grads[5], grads[6], grads[7])
```

```python
import jax
import jax.numpy as jnp
from jax import lax
from jax.sharding import PartitionSpec as P

HEADS = 16
KV_HEADS = 8
HEAD_DIM = 64
TOPK = 8
HALF = 512
CAP = 40

GROUP = ("dp", "seq")
ALL = ("dp", "seq", "expert")
epsilon = 1e-05
highest = lax.Precision.HIGHEST
bf16 = jnp.bfloat16
f32 = jnp.float32


def swap(array, axis):
    return lax.all_to_all(array, axis, split_axis=0, concat_axis=0, tiled=True)


def spread(array, axis, ways):
    return swap(jnp.broadcast_to(array[None], (ways,) + array.shape), axis)


def halo(array):
    size = lax.axis_size("dp")
    up = [(i, i + 1) for i in range(size - 1)]
    down = [(i + 1, i) for i in range(size - 1)]
    return lax.ppermute(array, "dp", up), lax.ppermute(array, "dp", down)


def turn(array, cosine, sine):
    rows, width = array.shape
    heads = array.reshape(rows, width // HEAD_DIM, HEAD_DIM)
    front, behind = heads[..., :32], heads[..., 32:]
    c, s = cosine[:, None, :], sine[:, None, :]
    return jnp.concatenate([front * c - behind * s, behind * c + front * s], axis=-1).reshape(rows, width)


def documents(lengths, places):
    ends = jnp.cumsum(lengths)
    ids = jnp.sum((places[:, None] >= ends[None, :]).astype(jnp.int32), axis=1)
    starts = jnp.concatenate([jnp.zeros((1,), jnp.int32), ends])
    marks = jnp.arange(starts.shape[0], dtype=jnp.int32)
    begins = jnp.sum(jnp.where(ids[:, None] == marks[None, :], starts[None, :], 0), axis=1)
    return ids, places - begins


def dot(a, b, dims, **kw):
    return lax.dot_general(a, b, ((dims[0], dims[1]), ((), ())), preferred_element_type=f32, **kw)


def shards(tokens, cotangent, doc_lengths, routes, route_rank, w_qkv, w_o, norm_gains, key_gain, w_router, w_in, w_out):
    D = 1024
    KVW = 512
    d_index = lax.axis_index("dp")
    s_index = lax.axis_index("seq")
    e_index = lax.axis_index("expert")
    lengths = doc_lengths[0]
    tok_own = tokens[0]
    w_send = jnp.concatenate(
        [
            w_qkv[:, :1024].reshape(64, 4, 256),
            w_qkv[:, 1024:1536].reshape(64, 4, 128),
            w_qkv[:, 1536:].reshape(64, 4, 128),
        ],
        axis=2,
    ).transpose(1, 0, 2)
    extra = jnp.zeros((64, 128), bf16)
    extra = extra.at[:, :32].set(w_router).at[:, 32:35].set(norm_gains.T).at[:32, 35].set(key_gain)
    w_send = jnp.concatenate([w_send, jnp.broadcast_to(extra[None], (4, 64, 128))], axis=2)
    w_send = jnp.broadcast_to(w_send[None], (4, 4, 64, 640)).reshape(16, 64, 640)
    w_got = swap(w_send, GROUP)
    w_cols = w_got[:, :, :512].reshape(1024, 512)
    extras = w_got[:, :, 512:].reshape(1024, 128)
    router = extras[:, :32]
    gain_rows = extras[:, 32:35].T.astype(f32)
    key_full = extras[:, 35].reshape(16, 64)[:, :32].reshape(512).astype(f32)
    span_tokens = spread(tok_own, "seq", 4).reshape(512, D)
    moe_shard = jnp.concatenate([w_in.reshape(4, 64, 1024), w_out], axis=1)
    moe_all = lax.all_gather(moe_shard, GROUP, axis=0, tiled=False)
    out_full = spread(w_o, GROUP, 16).reshape(1024, 1024)
    info = jnp.concatenate([routes[0].T, route_rank], axis=0)
    infos = spread(info, "expert", 8)
    upstream_all = spread(cotangent[0], "expert", 8)

    ext_places = d_index * 512 - HALF + jnp.arange(1536, dtype=jnp.int32)
    ids, positions = documents(lengths, ext_places)
    ext_docs = jnp.where((ext_places >= 0) & (ext_places < 2048), ids, -1)
    own_docs = ext_docs[HALF : HALF + 512]
    frequency = 10000.0 ** (-jnp.arange(32, dtype=f32) / 32)
    angles = positions.astype(f32)[:, None] * frequency[None, :]
    cosine, sine = jnp.cos(angles), jnp.sin(angles)

    span = span_tokens.astype(f32)
    first_inverse = lax.rsqrt(jnp.mean(span * span, axis=-1, keepdims=True) + epsilon)
    first_low = (span * first_inverse * gain_rows[0]).astype(bf16)
    projected = dot(first_low, w_cols, ((1,), (0,)))
    q_raw, k_raw, v_raw = projected[:, :256], projected[:, 256:384], projected[:, 384:]
    kv_low = projected[:, 256:].astype(bf16)
    part = jnp.concatenate(
        [jnp.sum(q_raw * q_raw, axis=1).reshape(4, 128), jnp.sum(k_raw * k_raw, axis=1).reshape(4, 128)], axis=0
    )
    kv_before, kv_after = halo(kv_low)
    parts = spread(part, GROUP, 16).reshape(4, 4, 8, 128)
    sums = jnp.sum(parts, axis=1)
    q_sum = lax.dynamic_index_in_dim(sums, d_index, 0, keepdims=False)[:4].reshape(512)
    k_pad = jnp.pad(sums[:, 4:], ((1, 1), (0, 0), (0, 0)))
    k_sum = lax.dynamic_slice_in_dim(k_pad, d_index, 3, 0).reshape(1536)
    q_inverse = lax.rsqrt(q_sum / 1024 + epsilon)[:, None]
    k_inverse = lax.rsqrt(k_sum / 512 + epsilon)[:, None]
    q_gain = lax.dynamic_slice_in_dim(gain_rows[2], s_index * 256, 256, 0)
    k_gain = lax.dynamic_slice_in_dim(key_full, s_index * 128, 128, 0)
    kv_ext = jnp.concatenate([kv_before, kv_low, kv_after], axis=0)
    q_unit = q_raw * q_inverse
    own_cos, own_sin = cosine[HALF : HALF + 512], sine[HALF : HALF + 512]
    queries = turn(q_unit * q_gain, own_cos, own_sin).astype(bf16)
    keys = turn(kv_ext[:, :128].astype(f32) * k_inverse * k_gain, cosine, sine).astype(bf16)
    values = kv_ext[:, 128:].reshape(1536, 2, 64)
    queries_g = queries.reshape(512, 2, 2, 64)
    keys_g = keys.reshape(1536, 2, 64)
    offsets = jnp.arange(1536, dtype=jnp.int32)[None, :] - HALF - jnp.arange(512, dtype=jnp.int32)[:, None]
    allowed = (offsets >= -HALF) & (offsets < HALF) & (own_docs[:, None] == ext_docs[None, :])

    def get_scores():
        scores = jnp.einsum("qkgd,mkd->kgqm", queries_g, keys_g, preferred_element_type=f32) * 0.125
        return jnp.where(allowed[None, None], scores, -1e30)

    scores = get_scores()
    largest = jnp.max(scores, axis=-1, keepdims=True)
    weights = jnp.exp(scores - largest)
    totals = jnp.sum(weights, axis=-1, keepdims=True)
    probs = (weights / totals).astype(bf16)
    mixed = jnp.einsum("kgqm,mkd->qkgd", probs, values, preferred_element_type=f32)
    attended = mixed.reshape(512, 256).astype(bf16)
    log_totals = largest + jnp.log(totals)
    attn_span = spread(attended, "seq", 4)
    attn_rows = lax.dynamic_slice_in_dim(attn_span, s_index * 128, 128, 1).transpose(1, 0, 2).reshape(128, 1024)
    residual = tok_own.astype(f32)
    middle = residual + dot(attn_rows, out_full, ((1,), (0,)))
    second_inverse = lax.rsqrt(jnp.mean(middle * middle, axis=-1, keepdims=True) + epsilon)
    second_unit = middle * second_inverse
    second_low = (second_unit * gain_rows[1]).astype(bf16)
    normed_all = spread(second_low, "expert", 8)

    def routing(route_t, rank):
        used = jnp.any(route_t[None] == jnp.arange(32, dtype=jnp.int32)[:, None, None], axis=1)
        earlier = (rank[:, None] < rank[None, :]).astype(bf16)
        before = dot(used.astype(bf16), earlier, ((1,), (0,)))
        return used, before.astype(jnp.int32)

    used_all, before_all = jax.vmap(routing)(infos[:, :8], infos[:, 8])
    pos_all = jnp.where(used_all & (before_all < CAP), before_all, -1)
    pos_mine = lax.dynamic_slice_in_dim(pos_all, e_index * 4, 4, 1)
    place = (pos_mine[:, :, None, :] == jnp.arange(CAP, dtype=jnp.int32)[None, None, :, None]).astype(bf16)
    logits_all = jnp.einsum("jtd,de->jte", normed_all, router, preferred_element_type=f32)

    def gates_of(logits, used_t):
        masked = jnp.where(used_t, logits, -1e30)
        top = jnp.max(masked, axis=-1, keepdims=True)
        ex = jnp.where(used_t, jnp.exp(masked - top), 0.0)
        return ex / jnp.sum(ex, axis=-1, keepdims=True)

    gates_all = gates_of(logits_all, used_all.transpose(0, 2, 1))
    gates_mine = lax.dynamic_slice_in_dim(gates_all, e_index * 4, 4, 2)
    slots = jnp.einsum("jlct,jtd->ljcd", place, normed_all, preferred_element_type=f32).astype(bf16).reshape(4, 320, D)
    slot_up = jnp.einsum("jlct,jtd->ljcd", place, upstream_all, preferred_element_type=f32)
    slot_gate = jnp.einsum("jlct,jtl->ljc", place.astype(f32), gates_mine, precision=highest)[..., None]
    slot_grad = (slot_up * slot_gate).astype(bf16).reshape(4, 320, D)
    in_matrix = moe_all[:, :, :64].transpose(1, 0, 2, 3).reshape(4, 1024, 1024)
    out_matrix = moe_all[:, :, 64:].transpose(1, 0, 2, 3).reshape(4, 512, 1024)
    both = jnp.einsum("erd,edf->erf", slots, in_matrix, preferred_element_type=f32)
    gate_part, up_part = both[..., :512], both[..., 512:]
    sig = jax.nn.sigmoid(gate_part)
    hidden = (gate_part * sig * up_part).astype(bf16)
    produced = jnp.einsum("erf,efd->erd", hidden, out_matrix, preferred_element_type=f32).astype(bf16)
    produced_j = produced.reshape(4, 8, CAP, D)
    slot_dgate = jnp.sum(slot_up * produced_j.astype(f32), axis=-1)
    dgate_mine = jnp.einsum("jlct,ljc->jtl", place.astype(f32), slot_dgate, precision=highest)
    weighted = (produced_j.astype(f32) * slot_gate).astype(bf16)
    out_part = jnp.einsum("jlct,ljcd->jtd", place, weighted, preferred_element_type=f32).astype(bf16)
    hidden_grad = jnp.einsum("erd,efd->erf", slot_grad, out_matrix, preferred_element_type=f32)
    gate_deriv = hidden_grad * up_part * sig * (1.0 + gate_part * (1.0 - sig))
    up_deriv = hidden_grad * gate_part * sig
    both_grad = jnp.concatenate([gate_deriv, up_deriv], axis=-1).astype(bf16)
    slot_dx = jnp.einsum("erf,edf->erd", both_grad, in_matrix, preferred_element_type=f32).astype(bf16)
    dn2_part = jnp.einsum(
        "jlct,ljcd->jtd", place, slot_dx.reshape(4, 8, CAP, D), preferred_element_type=f32
    ).astype(bf16)
    dgate_send = lax.dynamic_update_slice(jnp.zeros((8, 128, 128), bf16), dgate_mine.astype(bf16), (0, 0, e_index * 4))
    back = swap(jnp.concatenate([dn2_part, dgate_send], axis=2), "expert")
    in_grad = jnp.einsum("erd,erf->edf", slots, both_grad, preferred_element_type=f32).astype(bf16)
    down_grad = jnp.einsum("erf,erd->efd", hidden, slot_grad, preferred_element_type=f32).astype(bf16)
    moe_grad = jnp.concatenate(
        [in_grad.reshape(4, 16, 64, 1024), down_grad.reshape(4, 16, 32, 1024)], axis=2
    ).transpose(1, 0, 2, 3)
    moe_own = lax.psum_scatter(moe_grad.reshape(16 * 384, 1024), GROUP, scatter_dimension=0, tiled=True)
    moe_own = moe_own.reshape(4, 96, 1024).astype(f32)
    in_own = moe_own[:, :64].reshape(4, 64, 2, 512)
    down_own = moe_own[:, 64:]
    outs = swap(out_part, "expert")
    output = (middle + jnp.sum(outs.astype(f32), axis=0)).astype(bf16)
    back_sum = jnp.sum(back.astype(f32), axis=0)
    dgates = back_sum[:, 1024:1056]
    used_own = lax.dynamic_index_in_dim(used_all, e_index, 0, keepdims=False).T
    logits = dot(second_low, router, ((1,), (0,)))
    gates = gates_of(logits, used_own)
    logit_grad = gates * (dgates - jnp.sum(gates * dgates, axis=-1, keepdims=True))
    router_grad = dot(logit_grad, second_low.astype(f32), ((0,), (0,)), precision=highest)
    dn2 = back_sum[:, :1024] + dot(logit_grad, router.astype(f32), ((1,), (1,)), precision=highest)
    second_gain_grad = jnp.sum(dn2 * second_unit, axis=0)
    scaled = dn2 * gain_rows[1]
    upstream = cotangent[0].astype(f32)
    middle_grad = upstream + second_inverse * (
        scaled - second_unit * jnp.mean(scaled * second_unit, axis=-1, keepdims=True)
    )
    branch = middle_grad.astype(bf16)
    dattn = dot(branch, out_full, ((1,), (1,))).astype(bf16)
    grad_send = jnp.concatenate(
        [dattn.reshape(128, 4, 256).transpose(1, 0, 2), branch.reshape(128, 4, 256).transpose(1, 0, 2)], axis=2
    )
    grad_got = swap(grad_send, "seq").reshape(512, 512)
    heads_grad = grad_got[:, :256].reshape(512, 2, 2, 64)
    branch_cols = grad_got[:, 256:]
    scores = get_scores()
    probs = jnp.exp(scores - log_totals)
    prob_grad = jnp.einsum("qkgd,mkd->kgqm", heads_grad, values, preferred_element_type=f32)
    centre = jnp.sum(probs * prob_grad, axis=-1, keepdims=True)
    score_grad = (probs * (prob_grad - centre)).astype(bf16)
    dq = (jnp.einsum("kgqm,mkd->qkgd", score_grad, keys_g, preferred_element_type=f32) * 0.125).reshape(512, 256)
    dk = (jnp.einsum("kgqm,qkgd->mkd", score_grad, queries_g, preferred_element_type=f32) * 0.125).reshape(1536, 128)
    dv = jnp.einsum("kgqm,qkgd->mkd", probs.astype(bf16), heads_grad, preferred_element_type=f32).reshape(1536, 128)
    dq = dq.astype(bf16).astype(f32)
    dkv = jnp.concatenate([dk, dv], axis=1)
    dkv_low = dkv.astype(bf16)
    up, down = halo_back(dkv_low)
    q_dot = jnp.sum(dq * queries.astype(f32), axis=1).reshape(1, 4, 128)
    k_dot = jnp.sum(dk * keys.astype(f32), axis=1).reshape(3, 4, 128)
    q_place = lax.dynamic_update_slice(jnp.zeros((4, 4, 128), f32), q_dot, (d_index, 0, 0))
    k_place = lax.dynamic_update_slice(jnp.zeros((6, 4, 128), f32), k_dot, (d_index, 0, 0))[1:5]
    dots = jnp.concatenate([q_place, k_place], axis=1)
    dots = swap(jnp.broadcast_to(dots[:, None], (4, 4, 8, 128)).reshape(16, 8, 128), GROUP)
    dots = jnp.sum(dots, axis=0)
    q_mean = dots[:4].reshape(512, 1) / 1024
    k_mean = dots[4:].reshape(512, 1) / 512
    dkv_own = dkv[HALF : HALF + 512] + up.astype(f32) + down.astype(f32)
    wq = turn(dq, own_cos, -own_sin)
    wk = turn(dkv_own[:, :128].astype(bf16).astype(f32), own_cos, -own_sin)
    own_k_inverse = k_inverse[HALF : HALF + 512]
    k_unit = k_raw * own_k_inverse
    q_gain_grad = jnp.sum(wq * q_unit, axis=0)
    k_gain_grad = jnp.sum(wk * k_unit, axis=0)
    dq_raw = q_inverse * (wq * q_gain - q_unit * q_mean)
    dk_raw = own_k_inverse * (wk * k_gain - k_unit * k_mean)
    dqkv = jnp.concatenate([dq_raw, dk_raw, dkv_own[:, 128:]], axis=1).astype(bf16)
    dn1_part = dot(dqkv, w_cols, ((1,), (1,))).astype(bf16)
    dn1 = jnp.sum(swap(dn1_part.reshape(4, 128, 1024), "seq").astype(f32), axis=0)
    own_span = residual
    own_inverse = lax.rsqrt(jnp.mean(own_span * own_span, axis=-1, keepdims=True) + epsilon)
    own_unit = own_span * own_inverse
    scaled1 = dn1 * gain_rows[0]
    input_grad = middle_grad + own_inverse * (
        scaled1 - own_unit * jnp.mean(scaled1 * own_unit, axis=-1, keepdims=True)
    )
    qkv_part = dot(first_low, dqkv, ((0,), (0,)))
    attn_all = attn_span.transpose(1, 0, 2).reshape(512, 1024)
    o_part = dot(attn_all, branch_cols, ((0,), (0,)))
    q_row = lax.dynamic_update_slice(jnp.zeros((1024,), f32), q_gain_grad, (s_index * 256,))
    k_row = lax.dynamic_update_slice(jnp.zeros((512,), f32), k_gain_grad, (s_index * 128,))
    k_row = jnp.pad(k_row.reshape(16, 32), ((0, 0), (0, 32))).reshape(1024)
    small = jnp.concatenate(
        [router_grad, second_gain_grad[None], q_row[None], k_row[None], jnp.zeros((29, 1024), f32)], axis=0
    ).astype(bf16)
    small = small.reshape(8, 8, 16, 64).transpose(2, 0, 1, 3).reshape(128, 8, 64)
    final_send = jnp.concatenate(
        [qkv_part.astype(bf16).reshape(128, 8, 512), o_part.astype(bf16).reshape(128, 8, 256), small], axis=2
    )
    final_got = swap(final_send, ALL).astype(f32)
    by_seq = jnp.sum(final_got.reshape(4, 4, 8, 8, 832), axis=(0, 2))
    small_sum = jnp.sum(by_seq[:, :, 768:], axis=0)
    own = jnp.concatenate(
        [
            by_seq[:, :, :256].transpose(1, 0, 2).reshape(8, 1024),
            by_seq[:, :, 256:384].transpose(1, 0, 2).reshape(8, 512),
            by_seq[:, :, 384:512].transpose(1, 0, 2).reshape(8, 512),
            by_seq[:, :, 512:768].transpose(1, 0, 2).reshape(8, 1024),
            small_sum,
        ],
        axis=1,
    ).astype(bf16)
    rows = spread(own, "expert", 8).astype(f32)
    qkv_own = rows[:, :, :2048].reshape(64, 2048)
    o_own = rows[:, :, 2048:3072].reshape(64, 1024)
    small_own = rows[:, :, 3072:].reshape(64, 64)
    first_gain_own = jnp.sum(qkv_own * w_qkv.astype(f32), axis=1) / norm_gains[0].astype(f32)
    gains_own = jnp.stack([first_gain_own, small_own[32], small_own[33]])
    key_own = small_own[34, :32]
    router_own = small_own[:32].T
    return (output[None], input_grad[None], qkv_own, o_own, gains_own, key_own, router_own, in_own, down_own)


def halo_back(dkv_low):
    size = lax.axis_size("dp")
    up = [(i, i + 1) for i in range(size - 1)]
    down = [(i + 1, i) for i in range(size - 1)]
    return lax.ppermute(dkv_low[1024:], "dp", up), lax.ppermute(dkv_low[:512], "dp", down)


def solution(mesh):
    both = P("expert", GROUP, None)
    rows = P(GROUP, None)
    return jax.shard_map(
        shards,
        mesh=mesh,
        in_specs=(
            both,
            both,
            P("expert", None),
            both,
            P("expert", GROUP),
            rows,
            rows,
            P(None, GROUP),
            P(GROUP),
            rows,
            P("expert", GROUP, None, None),
            P("expert", GROUP, None),
        ),
        out_specs=(
            both,
            both,
            rows,
            rows,
            P(None, GROUP),
            P(GROUP),
            rows,
            P("expert", GROUP, None, None),
            P("expert", GROUP, None),
        ),
        check_vma=False,
    )
```

```python
import jax
import jax.numpy as jnp
from jax import lax
from jax.experimental import pallas as pl
from jax.experimental.pallas import tpu as pltpu
from jax.sharding import PartitionSpec as P

HEADS = 16
KV_HEADS = 8
HEAD_DIM = 64
TOPK = 8
HALF = 512
CAP = 40
SLOTS = 48
VMEM_BYTES = 60 * 1024 * 1024

GROUP = ("dp", "seq")
ALL = ("dp", "seq", "expert")
epsilon = 1e-05
highest = lax.Precision.HIGHEST
bf16 = jnp.bfloat16
f32 = jnp.float32


def dot(a, b, dims, **kw):
    return lax.dot_general(a, b, ((dims[0], dims[1]), ((), ())), preferred_element_type=f32, **kw)


def expert_step(where_ref, *refs):
    n2_refs, cot_refs = refs[0:8], refs[8:16]
    router_ref, w_ref = refs[16:18]
    dn_refs, out_refs = refs[18:26], refs[26:34]
    xin_ref, dgu_ref, hid_ref, dy_ref = refs[34:38]
    place, xs, gs, gate, ys, dxs, dgs = refs[38:45]
    step = pl.program_id(0)

    @pl.when(step == 0)
    def _():
        first = 4 * where_ref[0]
        ids = lax.broadcasted_iota(jnp.int32, (32, 128), 0) + first
        ids = jnp.where(ids >= 32, ids - 32, ids).astype(f32)
        slot = lax.broadcasted_iota(jnp.int32, (SLOTS, 128), 0).astype(f32)
        for j in range(8):
            n2 = n2_refs[j][...]
            meta = cot_refs[j][:, 1024:].astype(f32)
            turned = meta.T
            logits = dot(router_ref[...], n2, ((1,), (1,)))
            used = turned[0:1] == ids
            for k in range(1, TOPK):
                used = used | (turned[k : k + 1] == ids)
            masked = jnp.where(used, logits, -1e30)
            grown = jnp.where(used, jnp.exp(masked - jnp.max(masked, axis=0, keepdims=True)), 0.0)
            gates = grown / jnp.sum(grown, axis=0, keepdims=True)
            earlier = jnp.where(meta[:, 8:9] < turned[8:9], 1.0, 0.0).astype(bf16)
            before = dot(jnp.where(used, 1.0, 0.0).astype(bf16), earlier, ((1,), (0,)))
            spot = jnp.where(used & (before < CAP), before, 1000.0)
            parts = []
            for l in range(4):
                hit = jnp.where(slot == spot[l : l + 1], 1.0, 0.0)
                share = jnp.sum(hit * gates[l : l + 1], axis=1, keepdims=True)
                gate[l, SLOTS * j : SLOTS * (j + 1), :] = jnp.broadcast_to(share, (SLOTS, 128))
                parts.append(hit)
            chosen = jnp.concatenate(parts, axis=0).astype(bf16)
            place[j] = chosen
            rows = dot(chosen, n2, ((1,), (0,))).astype(bf16)
            ups = dot(chosen, cot_refs[j][:, :1024], ((1,), (0,))).astype(bf16)
            for l in range(4):
                xs[l, SLOTS * j : SLOTS * (j + 1), :] = rows[SLOTS * l : SLOTS * (l + 1)]
                gs[l, SLOTS * j : SLOTS * (j + 1), :] = ups[SLOTS * l : SLOTS * (l + 1)]

    w_in = w_ref[:, 0, :64, :].reshape(1024, 1024)
    w_out = w_ref[:, 0, 64:, :].reshape(512, 1024)
    x = xs[step]
    both = dot(x, w_in, ((1,), (0,)))
    gate_part, up_part = both[:, :512], both[:, 512:]
    sig = jax.nn.sigmoid(gate_part)
    silu = gate_part * sig
    hidden = (silu * up_part).astype(bf16)
    y = dot(hidden, w_out, ((1,), (0,))).astype(bf16).astype(f32)
    g = gs[step].astype(f32)
    share = gate[step][:, 0:1]
    dy = (g * share).astype(bf16)
    ys[step] = (y * share).astype(bf16)
    lane = lax.broadcasted_iota(jnp.int32, (8 * SLOTS, 128), 1)
    dgate = jnp.sum(g * y, axis=1, keepdims=True)
    dgs[step] = jnp.where(lane == 4 * where_ref[0] + step, dgate, 0.0).astype(bf16)
    dh = dot(dy, w_out, ((1,), (1,)))
    dgu = jnp.concatenate(
        [dh * up_part * (sig * (1.0 + gate_part * (1.0 - sig))), dh * silu], axis=1
    ).astype(bf16)
    dxs[step] = dot(dgu, w_in, ((1,), (1,))).astype(bf16)
    xin_ref[0] = x
    dgu_ref[0] = dgu
    hid_ref[0] = hidden
    dy_ref[0] = dy

    @pl.when(step == 3)
    def _():
        for j in range(8):
            chosen = place[j]
            span = slice(SLOTS * j, SLOTS * (j + 1))
            for source, target, lo, hi in ((dxs, dn_refs[j], 0, 1024), (dgs, dn_refs[j], 1024, 1152), (ys, out_refs[j], 0, 1024)):
                stacked = jnp.concatenate([source[l, span, :] for l in range(4)], axis=0)
                target[:, lo:hi] = dot(chosen, stacked, ((0,), (0,))).astype(bf16)


def experts(e_index, n2s, cots, router_t, weights):
    whole = lambda rows, cols: pl.BlockSpec((rows, cols), lambda i, *_: (0, 0))
    each = lambda cols: pl.BlockSpec((1, 8 * SLOTS, cols), lambda i, *_: (i, 0, 0))
    shape = lambda *s: jax.ShapeDtypeStruct(s, bf16)
    return pl.pallas_call(
        expert_step,
        grid_spec=pltpu.PrefetchScalarGridSpec(
            num_scalar_prefetch=1,
            grid=(4,),
            in_specs=[whole(128, 1024)] * 8
            + [whole(128, 1152)] * 8
            + [whole(32, 1024), pl.BlockSpec((16, 1, 96, 1024), lambda i, *_: (0, i, 0, 0))],
            out_specs=[whole(128, 1152)] * 8 + [whole(128, 1024)] * 8 + [each(1024), each(1024), each(512), each(1024)],
            scratch_shapes=[
                pltpu.VMEM((8, 4 * SLOTS, 128), bf16),
                pltpu.VMEM((4, 8 * SLOTS, 1024), bf16),
                pltpu.VMEM((4, 8 * SLOTS, 1024), bf16),
                pltpu.VMEM((4, 8 * SLOTS, 128), f32),
                pltpu.VMEM((4, 8 * SLOTS, 1024), bf16),
                pltpu.VMEM((4, 8 * SLOTS, 1024), bf16),
                pltpu.VMEM((4, 8 * SLOTS, 128), bf16),
            ],
        ),
        out_shape=[shape(128, 1152)] * 8
        + [shape(128, 1024)] * 8
        + [shape(4, 8 * SLOTS, 1024), shape(4, 8 * SLOTS, 1024), shape(4, 8 * SLOTS, 512), shape(4, 8 * SLOTS, 1024)],
        compiler_params=pltpu.CompilerParams(vmem_limit_bytes=VMEM_BYTES),
        cost_estimate=pl.CostEstimate(flops=12 * 10**9, bytes_accessed=40 * 10**6, transcendentals=10**6),
        name="experts",
    )(e_index, *n2s, *cots, router_t, weights)


def expert_grad_step(x_ref, dgu_ref, hid_ref, dy_ref, out_ref):
    grad_in = dot(x_ref[0], dgu_ref[0], ((0,), (0,))).astype(bf16)
    out_ref[:, 0, :64, :] = grad_in.reshape(16, 64, 1024)
    grad_out = dot(hid_ref[0], dy_ref[0], ((0,), (0,))).astype(bf16)
    out_ref[:, 0, 64:, :] = grad_out.reshape(16, 32, 1024)


def expert_grads(x, dgu, hid, dy):
    each = lambda cols: pl.BlockSpec((1, 8 * SLOTS, cols), lambda i: (i, 0, 0))
    return pl.pallas_call(
        expert_grad_step,
        grid=(4,),
        in_specs=[each(1024), each(1024), each(512), each(1024)],
        out_specs=pl.BlockSpec((16, 1, 96, 1024), lambda i: (0, i, 0, 0)),
        out_shape=jax.ShapeDtypeStruct((16, 4, 96, 1024), bf16),
        compiler_params=pltpu.CompilerParams(vmem_limit_bytes=VMEM_BYTES),
        cost_estimate=pl.CostEstimate(flops=5 * 10**9, bytes_accessed=24 * 10**6, transcendentals=0),
        name="expert_grads",
    )(x, dgu, hid, dy)


def call(kernel, name, out_shape, *args, flops=10**8, scratch=(), moved=10**7):
    specs = [pl.BlockSpec(memory_space=pltpu.SMEM)] + [pl.BlockSpec(memory_space=pltpu.VMEM)] * (len(args) - 1)
    return pl.pallas_call(
        kernel,
        in_specs=specs,
        out_specs=jax.tree.map(lambda _: pl.BlockSpec(memory_space=pltpu.VMEM), out_shape),
        out_shape=out_shape,
        scratch_shapes=list(scratch),
        compiler_params=pltpu.CompilerParams(vmem_limit_bytes=VMEM_BYTES),
        cost_estimate=pl.CostEstimate(flops=flops, bytes_accessed=moved, transcendentals=0),
        name=name,
    )(*args)


def sds(*shape, dtype=bf16):
    return jax.ShapeDtypeStruct(shape, dtype)


def block(index):
    return pl.ds(pl.multiple_of(index * 128, 128), 128)


def column(row):
    return jnp.broadcast_to(row, (128, 128)).T


def partner(x):
    lane = lax.broadcasted_iota(jnp.int32, x.shape, 1)
    return jnp.where(lane % 64 < 32, pltpu.roll(x, 96, 1), pltpu.roll(x, 32, 1))


def row_sums(x):
    ones = jnp.ones((8, x.shape[1]), f32)
    return dot(ones, x, ((1,), (1,)), precision=highest)[0:1]


def project_kernel(at, t0, t1, t2, t3, w_ref, n1_ref, raw_ref, kv_ref, parts_ref, small_ref, rows):
    s = at[1]
    w = w_ref[:, :, :512].reshape(1024, 512)
    extras = w_ref[:, :, 512:].reshape(1024, 128).astype(f32).T
    small_ref[...] = extras[:48]
    gain = extras[32:33]
    for ds, t in enumerate((t0, t1, t2, t3)):
        x = t[...].astype(f32)
        low = (x * lax.rsqrt(jnp.mean(x * x, axis=1, keepdims=True) + epsilon) * gain).astype(bf16)
        raw = dot(low, w, ((1,), (0,)))
        place = lax.rem(s - ds + 4, 4)
        n1_ref[block(place), :] = low
        raw_ref[block(place), :] = raw
        kv_ref[block(place), :] = raw[:, 256:].astype(bf16)
        rows[pl.ds(place, 1), :] = row_sums(raw[:, :256] * raw[:, :256])
        rows[pl.ds(place + 4, 1), :] = row_sums(raw[:, 256:384] * raw[:, 256:384])
    parts_ref[...] = jnp.broadcast_to(rows[...][None], (16, 8, 128))
    start = pl.multiple_of(s * 256, 256)
    chunk = small_ref[35:36, pl.ds(start, 256)]
    at_row = lax.broadcasted_iota(jnp.int32, (256, 128), 0)
    at_col = lax.broadcasted_iota(jnp.int32, (256, 128), 1)
    pick = jnp.where(at_row == 64 * (at_col // 32) + at_col % 32, 1.0, 0.0)
    small_ref[40:41, 0:256] = small_ref[34:35, pl.ds(start, 256)]
    small_ref[40:41, 256:384] = dot(jnp.broadcast_to(chunk, (8, 256)), pick, ((1,), (0,)), precision=highest)[0:1]


def project(at, pieces, w_got):
    return call(
        project_kernel,
        "project",
        [
            sds(512, 1024),
            sds(512, 512, dtype=f32),
            sds(512, 256),
            sds(16, 8, 128, dtype=f32),
            sds(48, 1024, dtype=f32),
        ],
        at,
        *pieces,
        w_got,
        flops=2 * 10**9,
        scratch=[pltpu.VMEM((8, 128), f32)],
    )


def document_of(places, at):
    found = jnp.zeros(places.shape, f32)
    for i in range(4):
        found = found + jnp.where(places >= at[3 + i], 1.0, 0.0)
    return jnp.where((places >= 0) & (places < 2048), found, -1.0)


def seen_bias(at, b):
    first = at[0] * 512 + 128 * b
    key = lax.broadcasted_iota(jnp.int32, (1152, 128), 0)
    query = lax.broadcasted_iota(jnp.int32, (1152, 128), 1)
    key_doc = document_of(first - HALF + key, at)
    query_doc = document_of(first + lax.broadcasted_iota(jnp.int32, (1, 128), 1), at)
    apart = key - query
    seen = (apart >= 0) & (apart < 2 * HALF) & (key_doc == query_doc)
    return jnp.where(seen, 0.0, -1e30)


def stacked_heads(tile, kh):
    lane = lax.broadcasted_iota(jnp.int32, (128, 128), 1)
    mine = (lane < 64) if kh == 0 else (lane >= 64)
    other = pltpu.roll(tile, 64, 1)
    first, second = (tile, other) if kh == 0 else (other, tile)
    return jnp.concatenate([jnp.where(mine, first, 0.0), jnp.where(mine, second, 0.0)], axis=0).astype(bf16)


def attend_kernel(at, raw, kv0, kv1, kv2, parts, small, cos, sin, attn, qb, kb, vb, lse, uq, uk, qinv, kinv, vt):
    d = at[0]
    for i in range(12):
        there = jnp.clip(d - 1 + i // 4, 0, 3)
        row = parts[4 * there][4 + i % 4 : 5 + i % 4]
        for s in range(1, 4):
            row = row + parts[4 * there + s][4 + i % 4 : 5 + i % 4]
        inverse = column(lax.rsqrt(row * (1.0 / 512) + epsilon))
        span = slice(128 * i, 128 * (i + 1))
        part = slice(128 * (i % 4), 128 * (i % 4 + 1))
        kv = (kv0, kv1, kv2)[i // 4]
        unit = kv[part, :128].astype(f32) * inverse
        key = unit * small[40:41, 256:384]
        uk[span, :] = unit
        kb[span, :] = (key * cos[span, :] + partner(key) * sin[span, :]).astype(bf16)
        value = kv[part, 128:]
        vb[span, :] = value
        vt[:, span] = value.T
        if i // 4 == 1:
            kinv[part, :] = inverse
            row = parts[4 * d][i % 4 : i % 4 + 1]
            for s in range(1, 4):
                row = row + parts[4 * d + s][i % 4 : i % 4 + 1]
            inverse = column(lax.rsqrt(row * (1.0 / 1024) + epsilon))
            qinv[part, :] = inverse
            for m in range(2):
                lanes = slice(128 * m, 128 * (m + 1))
                unit = raw[part, lanes] * inverse
                uq[part, lanes] = unit
                query = unit * small[40:41, lanes]
                qb[part, lanes] = (query * cos[span, :] + partner(query) * sin[span, :]).astype(bf16)
    for b in range(4):
        bias = seen_bias(at, b)
        bias = jnp.concatenate([bias, bias], axis=1)
        window = slice(128 * b, 128 * b + 1152)
        for kh in range(2):
            lanes = slice(128 * kh, 128 * (kh + 1))
            heads = stacked_heads(qb[128 * b : 128 * (b + 1), lanes].astype(f32), kh)
            scores = dot(kb[window, :], heads, ((1,), (1,))) * 0.125 + bias
            top = jnp.max(scores, axis=0, keepdims=True)
            weights = jnp.exp(scores - top)
            total = jnp.sum(weights, axis=0, keepdims=True)
            lse[2 * b + kh : 2 * b + kh + 1, :] = top + jnp.log(total)
            mixed = dot(vt[64 * kh : 64 * kh + 64, window], weights.astype(bf16), ((1,), (0,))) / total
            tile = jnp.concatenate([mixed[:, :128], mixed[:, 128:]], axis=0).T
            attn[b, :, lanes] = tile.astype(bf16)


def attend(at, raw, kvs, parts, small, cos, sin):
    return call(
        attend_kernel,
        "attend",
        [
            sds(4, 128, 256),
            sds(512, 256),
            sds(1536, 128),
            sds(1536, 128),
            sds(8, 256, dtype=f32),
            sds(512, 256, dtype=f32),
            sds(1536, 128, dtype=f32),
            sds(512, 128, dtype=f32),
            sds(512, 128, dtype=f32),
        ],
        at,
        raw,
        *kvs,
        parts,
        small,
        cos,
        sin,
        flops=10**10,
        scratch=[pltpu.VMEM((128, 1536), bf16)],
    )


def attend_back_kernel(
    at, got, qb, kb, vb, lse, uq, uk, cos, sin, wq, dkv_own, dkv_up, dkv_down, sums, kt, dk, dv, qgain, qrows
):
    for i in range(12):
        span = slice(128 * i, 128 * (i + 1))
        kt[:, span] = kb[span, :].T
    dk[...] = jnp.zeros_like(dk)
    dv[...] = jnp.zeros_like(dv)
    qgain[...] = jnp.zeros_like(qgain)
    for b in range(4):
        bias = seen_bias(at, b)
        bias = jnp.concatenate([bias, bias], axis=1)
        window = slice(128 * b, 128 * b + 1152)
        own = slice(128 * b, 128 * (b + 1))
        table = slice(HALF + 128 * b, HALF + 128 * (b + 1))
        total = jnp.zeros((128, 1), f32)
        for kh in range(2):
            lanes = slice(128 * kh, 128 * (kh + 1))
            query = qb[own, lanes].astype(f32)
            heads = stacked_heads(query, kh)
            grads = stacked_heads(got[b, :, lanes].astype(f32), kh)
            scores = dot(kb[window, :], heads, ((1,), (1,))) * 0.125 + bias
            probs = jnp.exp(scores - lse[2 * b + kh : 2 * b + kh + 1, :])
            prob_grad = dot(vb[window, :], grads, ((1,), (1,)))
            centre = jnp.sum(probs * prob_grad, axis=0, keepdims=True)
            score_grad = (probs * (prob_grad - centre)).astype(bf16)
            dv[window, :] += dot(probs.astype(bf16), grads, ((1,), (0,)))
            dk[window, :] += dot(score_grad, heads, ((1,), (0,))) * 0.125
            flat = dot(kt[64 * kh : 64 * kh + 64, window], score_grad, ((1,), (0,))) * 0.125
            dq = jnp.concatenate([flat[:, :128], flat[:, 128:]], axis=0).T.astype(bf16).astype(f32)
            total = total + jnp.sum(dq * query, axis=1, keepdims=True)
            turned = dq * cos[table, :] - partner(dq) * sin[table, :]
            wq[own, lanes] = turned
            qgain[0:1, lanes] += jnp.sum(turned * uq[own, lanes], axis=0, keepdims=True)
        qrows[b : b + 1, :] = jnp.broadcast_to(total, (128, 128)).T[0:1]
    kgain = jnp.zeros((1, 128), f32)
    krows = []
    for i in range(12):
        span = slice(128 * i, 128 * (i + 1))
        part = slice(128 * (i % 4), 128 * (i % 4 + 1))
        grad = dk[span, :]
        spot = jnp.sum(grad * kb[span, :].astype(f32), axis=1, keepdims=True)
        krows.append(jnp.broadcast_to(spot, (128, 128)).T[0:1])
        turned = grad * cos[span, :] - partner(grad) * sin[span, :]
        kgain = kgain + jnp.sum(turned * uk[span, :], axis=0, keepdims=True)
        target = (dkv_down, dkv_own, dkv_up)[i // 4]
        target[part, :128] = grad.astype(target.dtype)
        target[part, 128:] = dv[span, :].astype(target.dtype)
    lane = lax.broadcasted_iota(jnp.int32, (1, 128), 1)
    none = jnp.zeros((7, 128), f32)
    for there in range(4):
        here = jnp.where(at[0] == there, 1.0, 0.0)
        mine = jnp.where(at[1] == there, 1.0, 0.0)
        rows = [qrows[0:4, :] * here]
        for i in range(4):
            row = jnp.zeros((1, 128), f32)
            for part in range(3):
                row = row + krows[4 * part + i] * jnp.where(at[0] - 1 + part == there, 1.0, 0.0)
            rows.append(row)
        for s in range(4):
            q_tile = qgain[0:1, 128 * (s // 2) : 128 * (s // 2 + 1)]
            if s % 2:
                q_tile = pltpu.roll(q_tile, 64, 1)
            k_tile = pltpu.roll(kgain, (64 - 32 * s) % 128, 1)
            gains = jnp.where(lane < 64, q_tile, jnp.where(lane < 96, k_tile, 0.0)) * mine
            sums[4 * there + s] = jnp.concatenate(rows + [gains, none], axis=0)


def attend_back(at, got, qb, kb, vb, lse, uq, uk, cos, sin):
    return call(
        attend_back_kernel,
        "attend_back",
        [
            sds(512, 256, dtype=f32),
            sds(512, 256, dtype=f32),
            sds(512, 256),
            sds(512, 256),
            sds(16, 16, 128, dtype=f32),
        ],
        at,
        got,
        qb,
        kb,
        vb,
        lse,
        uq,
        uk,
        cos,
        sin,
        flops=2 * 10**10,
        scratch=[
            pltpu.VMEM((128, 1536), bf16),
            pltpu.VMEM((1536, 128), f32),
            pltpu.VMEM((1536, 128), f32),
            pltpu.VMEM((8, 256), f32),
            pltpu.VMEM((8, 128), f32),
        ],
    )


def split(x):
    high = x.astype(bf16)
    return high, (x - high.astype(f32)).astype(bf16)


def middle_kernel(at, tok, attn, o0, o1, o2, o3, small, middle_ref, low_ref, inverse_ref):
    d = at[0]
    total = tok[...].astype(f32)
    for k, part in enumerate((o0, o1, o2, o3)):
        total = total + dot(attn[lax.rem(d - k + 4, 4)], part[...], ((1,), (0,)))
    inverse = lax.rsqrt(jnp.mean(total * total, axis=1, keepdims=True) + epsilon)
    middle_ref[...] = total
    low_ref[...] = (total * inverse * small[33:34]).astype(bf16)
    inverse_ref[...] = jnp.broadcast_to(inverse, (128, 128))


def make_middle(at, tok, attn, parts, small):
    return call(
        middle_kernel,
        "middle",
        [sds(128, 1024, dtype=f32), sds(128, 1024), sds(128, 128, dtype=f32)],
        at,
        tok,
        attn,
        *parts,
        small,
        flops=10**9,
    )


def middle_back_kernel(
    at, p0a, p0b, p1, p2, p3, middle, inverse_ref, low, cot, small, o0, o1, o2, o3, grad_ref, send_ref, sums_ref
):
    d = at[0]
    total = p0a[...].astype(f32) + p0b[...].astype(f32) + p1[...].astype(f32) + p2[...].astype(f32) + p3[...].astype(f32)
    dgates = total[:, 1024:1056]
    router_t = small[0:32].astype(bf16)
    logits = dot(low[...], router_t, ((1,), (1,)))
    ids = lax.broadcasted_iota(jnp.int32, (128, 32), 1).astype(f32)
    named = cot[:, 1024:].astype(f32)
    used = named[:, 0:1] == ids
    for k in range(1, TOPK):
        used = used | (named[:, k : k + 1] == ids)
    masked = jnp.where(used, logits, -1e30)
    grown = jnp.where(used, jnp.exp(masked - jnp.max(masked, axis=1, keepdims=True)), 0.0)
    gates = grown / jnp.sum(grown, axis=1, keepdims=True)
    logit_grad = gates * (dgates - jnp.sum(gates * dgates, axis=1, keepdims=True))
    high, rest = split(logit_grad)
    dn2 = total[:, :1024] + dot(high, router_t, ((1,), (0,))) + dot(rest, router_t, ((1,), (0,)))
    inverse = inverse_ref[:, 0:1]
    unit = middle[...] * inverse
    scaled = dn2 * small[33:34]
    grad = cot[:, :1024].astype(f32) + inverse * (scaled - unit * jnp.mean(scaled * unit, axis=1, keepdims=True))
    grad_ref[...] = grad
    branch = grad.astype(bf16)
    for k, part in enumerate((o0, o1, o2, o3)):
        send_ref[lax.rem(d - k + 4, 4), :, 0:256] = dot(branch, part[...], ((1,), (1,))).astype(bf16)
    for s in range(4):
        send_ref[s, :, 256:512] = branch[:, 256 * s : 256 * (s + 1)]
    sums_ref[0:32, :] = dot(high, low[...], ((0,), (0,))) + dot(rest, low[...], ((0,), (0,)))
    sums_ref[32:33, :] = jnp.sum(dn2 * unit, axis=0, keepdims=True)
    sums_ref[33:40, :] = jnp.zeros((7, 1024), f32)


def middle_back(at, pieces, middle, inverse, low, cot, small, parts):
    return call(
        middle_back_kernel,
        "middle_back",
        [sds(128, 1024, dtype=f32), sds(4, 128, 512), sds(40, 1024, dtype=f32)],
        at,
        *pieces,
        middle,
        inverse,
        low,
        cot,
        small,
        *parts,
        flops=10**9,
    )


def out_grad_kernel(at, a0, a1, a2, a3, got, out_ref):
    cols = jnp.concatenate([got[i, :, 256:512] for i in range(4)], axis=0)
    for k, part in enumerate((a0, a1, a2, a3)):
        start = pl.multiple_of(lax.rem(at[1] - k + 4, 4) * 256, 256)
        rows = jnp.concatenate([part[i] for i in range(4)], axis=0)
        out_ref[pl.ds(start, 256), :] = dot(rows, cols, ((0,), (0,))).astype(bf16)


def out_grads(at, attns, got):
    return call(out_grad_kernel, "out_grads", sds(1024, 256), at, *attns, got, flops=10**9)


def finish_kernel(
    at, wq, own, up, down, sums, uq, uk, qinv, kinv, small, cos, sin, n1, w_ref, o_part,
    dn0, dn1, dn2, dn3, keep_ref, send_ref, sums_ref, dqkv, grads,
):
    got = sums[0]
    for i in range(1, 16):
        got = got + sums[i]
    sums_ref[...] = got
    for i in range(4):
        part = slice(128 * i, 128 * (i + 1))
        table = slice(HALF + 128 * i, HALF + 128 * (i + 1))
        q_mean = column(got[i : i + 1]) * (1.0 / 1024)
        for m in range(2):
            lanes = slice(128 * m, 128 * (m + 1))
            grad = wq[part, lanes] * small[40:41, lanes] - uq[part, lanes] * q_mean
            dqkv[part, lanes] = (qinv[part, :] * grad).astype(bf16)
        total = own[part, :] + up[part, :].astype(f32) + down[part, :].astype(f32)
        dk = total[:, :128].astype(bf16).astype(f32)
        turned = dk * cos[table, :] - partner(dk) * sin[table, :]
        k_mean = column(got[4 + i : 5 + i]) * (1.0 / 512)
        grad = turned * small[40:41, 256:384] - uk[table, :] * k_mean
        dqkv[part, 256:384] = (kinv[part, :] * grad).astype(bf16)
        dqkv[part, 384:512] = total[:, 128:].astype(bf16)
    w = w_ref[:, :, :512].reshape(1024, 512)
    for k, ref in enumerate((dn0, dn1, dn2, dn3)):
        ref[...] = dot(dqkv[block(lax.rem(at[1] + k, 4)), :], w, ((1,), (1,))).astype(bf16)
    grads[:, :512] = dot(n1[...], dqkv[...], ((0,), (0,))).astype(bf16)
    grads[:, 512:] = o_part[...]
    even = lax.rem(at[2], 2) == 0

    @pl.when(even)
    def _():
        keep_ref[...] = grads[:, :384].reshape(16, 64, 384)
        send_ref[...] = grads[:, 384:].reshape(16, 64, 384)

    @pl.when(jnp.logical_not(even))
    def _():
        keep_ref[...] = grads[:, 384:].reshape(16, 64, 384)
        send_ref[...] = grads[:, :384].reshape(16, 64, 384)


def finish(at, wq, own, up, down, sums, uq, uk, qinv, kinv, small, cos, sin, n1, w_got, o_part):
    return call(
        finish_kernel,
        "finish",
        [sds(128, 1024)] * 4 + [sds(16, 64, 384)] * 2 + [sds(sums.shape[1], 128, dtype=f32)],
        at, wq, own, up, down, sums, uq, uk, qinv, kinv, small, cos, sin, n1, w_got, o_part,
        flops=3 * 10**9,
        scratch=[pltpu.VMEM((512, 512), bf16), pltpu.VMEM((1024, 768), bf16)],
    )


def input_kernel(at, p0, p1, p2, p3, tok, grad_ref, small, out_ref):
    dn1 = p0[...].astype(f32) + p1[...].astype(f32) + p2[...].astype(f32) + p3[...].astype(f32)
    x = tok[...].astype(f32)
    inverse = lax.rsqrt(jnp.mean(x * x, axis=1, keepdims=True) + epsilon)
    unit = x * inverse
    scaled = dn1 * small[32:33]
    out_ref[...] = grad_ref[...] + inverse * (scaled - unit * jnp.mean(scaled * unit, axis=1, keepdims=True))


def input_back(at, pieces, tok, grad, small):
    return call(input_kernel, "input_back", sds(128, 1024, dtype=f32), at, *pieces, tok, grad, small)


def swap(array, axis):
    return lax.all_to_all(array, axis, split_axis=0, concat_axis=0, tiled=True)


def spread(array, axis, ways):
    return swap(jnp.broadcast_to(array[None], (ways,) + array.shape), axis)


def along_seq(array, k):
    return lax.ppermute(array, "seq", [(i, (i + k) % 4) for i in range(4)])


def along_dp(array, k):
    return lax.ppermute(array, "dp", [(i, (i + k) % 4) for i in range(4)])


def along_x(array, k):
    return lax.ppermute(array, "expert", [(i, (i + 2 * k) % 8) for i in range(8)])


def other_core(array):
    return lax.ppermute(array, "expert", [(i, i ^ 1) for i in range(8)])


def gather_blocks(array):
    mine = [array] + [along_x(array, k) for k in range(1, 4)]
    return mine + [other_core(a) for a in mine]


def return_blocks(pieces):
    joined = [other_core(p) for p in pieces[4:]]
    sums = [pieces[0]]
    for k in range(1, 4):
        total = (pieces[k].astype(f32) + joined[k].astype(f32)).astype(bf16)
        sums.append(along_x(total, -k))
    return [sums[0], joined[0]] + sums[1:]


def shards(tokens, cotangent, doc_lengths, routes, route_rank, w_qkv, w_o, norm_gains, key_gain, w_router, w_in, w_out):
    d_index = lax.axis_index("dp")
    s_index = lax.axis_index("seq")
    e_index = lax.axis_index("expert")
    lengths = doc_lengths[0]
    tok = tokens[0]
    ends = jnp.cumsum(lengths)
    at = jnp.concatenate([jnp.stack([d_index, s_index, e_index]), ends]).astype(jnp.int32)
    w_send = jnp.concatenate(
        [
            w_qkv[:, :1024].reshape(64, 4, 256),
            w_qkv[:, 1024:1536].reshape(64, 4, 128),
            w_qkv[:, 1536:].reshape(64, 4, 128),
        ],
        axis=2,
    ).transpose(1, 0, 2)
    extra = jnp.concatenate(
        [w_router, norm_gains.T, jnp.pad(key_gain[:, None], ((0, 32), (0, 0))), jnp.zeros((64, 92), bf16)], axis=1
    )
    w_send = jnp.concatenate([w_send, jnp.broadcast_to(extra[None], (4, 64, 128))], axis=2)
    w_send = jnp.broadcast_to(w_send[None], (4, 4, 64, 640)).reshape(16, 64, 640)
    w_got = swap(w_send, GROUP)
    tok_pieces = [tok] + [along_seq(tok, k) for k in range(1, 4)]
    moe_shard = jnp.concatenate([w_in.reshape(4, 64, 1024), w_out], axis=1)
    moe_all = lax.all_gather(moe_shard, GROUP, axis=0, tiled=False)
    o_rows = jnp.zeros((4, 64, 1024), bf16)
    for k in range(4):
        piece = w_o if k == 0 else along_seq(w_o, k)
        o_rows = lax.dynamic_update_slice(o_rows, piece[None], ((s_index - k) % 4, 0, 0))
    o_rows = o_rows.reshape(256, 1024)
    o_parts = [o_rows] + [along_dp(o_rows, k) for k in range(1, 4)]
    cot = jnp.concatenate(
        [cotangent[0], routes[0].astype(bf16), route_rank[0].astype(bf16)[:, None], jnp.zeros((128, 119), bf16)], axis=1
    )
    cots = gather_blocks(cot)

    places = d_index * 512 - HALF + jnp.arange(1536, dtype=jnp.int32)
    starts = jnp.concatenate([jnp.zeros((1,), jnp.int32), ends])
    begins = jnp.max(jnp.where(places[:, None] >= starts[None, :], starts[None, :], 0), axis=1)
    lane = jnp.arange(128, dtype=jnp.int32)
    frequency = 10000.0 ** (-(lane % 32).astype(f32) / 32)
    angles = (places - begins).astype(f32)[:, None] * frequency[None, :]
    cos = jnp.cos(angles)
    sin = jnp.sin(angles) * jnp.where(lane % 64 < 32, -1.0, 1.0)[None, :]

    n1, raw, kv, parts, small = project(at, tok_pieces, w_got)
    up = [(i, i + 1) for i in range(3)]
    down = [(i + 1, i) for i in range(3)]
    kv_before = lax.ppermute(kv, "dp", up)
    kv_after = lax.ppermute(kv, "dp", down)
    parts = swap(parts, GROUP)
    attn, qb, kb, vb, lse, uq, uk, qinv, kinv = attend(at, raw, [kv_before, kv, kv_after], parts, small, cos, sin)
    attn_got = swap(attn, "seq")
    attns = [attn] + [along_seq(attn, k) for k in range(1, 4)]
    middle, n2, inverse = make_middle(at, tok, attn_got, o_parts, small)
    n2s = gather_blocks(n2)
    router_t = jnp.roll(small[:32], -4 * e_index, axis=0).astype(bf16)
    made = experts(e_index[None].astype(jnp.int32), n2s, cots, router_t, moe_all)
    dn_pieces = return_blocks(made[0:8])
    moe_grad = expert_grads(*made[16:20])
    moe_own = lax.psum_scatter(moe_grad.reshape(16 * 384, 1024), GROUP, scatter_dimension=0, tiled=True)
    moe_own = moe_own.reshape(4, 96, 1024).astype(f32)
    in_own = moe_own[:, :64].reshape(4, 64, 2, 512)
    down_own = moe_own[:, 64:]
    middle_grad, grad_send, extra_sums = middle_back(at, dn_pieces, middle, inverse, n2, cot, small, o_parts)
    grad_got = swap(grad_send, "seq")
    out_pieces = return_blocks(made[8:16])
    output = middle
    for piece in out_pieces:
        output = output + piece.astype(f32)
    output = output.astype(bf16)
    o_part = out_grads(at, attns, grad_got)
    wq, dkv_own, dkv_up, dkv_down, sums = attend_back(at, grad_got, qb, kb, vb, lse, uq, uk, cos, sin)
    from_before = lax.ppermute(dkv_up, "dp", up)
    from_after = lax.ppermute(dkv_down, "dp", down)
    routers = extra_sums[:32].reshape(2, 16, 16, 64).transpose(2, 1, 0, 3).reshape(16, 16, 128)
    second = jnp.pad(extra_sums[32].reshape(16, 1, 64), ((0, 0), (0, 0), (0, 64)))
    sums = jnp.concatenate([sums[:, :9], second, jnp.zeros((16, 6, 128), f32), routers], axis=1)
    sums = swap(sums, GROUP)
    done = finish(
        at, wq, dkv_own, from_before, from_after, sums, uq, uk, qinv, kinv, small, cos, sin, n1, w_got, o_part
    )
    dn1_pieces = [done[0]] + [along_seq(done[k], k) for k in range(1, 4)]
    keep, send, summed = done[4:]
    halves = (keep.astype(f32) + other_core(send).astype(f32)).astype(bf16)
    halves = swap(halves, GROUP).reshape(4, 4, 64, 384)
    halves = jnp.sum(halves.astype(f32), axis=0).transpose(1, 0, 2).reshape(64, 1536)
    own = jnp.concatenate([halves, jnp.pad(summed, ((0, 32), (0, 0)))], axis=1).astype(bf16)
    total = own.astype(f32)
    for k in range(1, 4):
        total = total + along_x(own, k).astype(f32)
    total = total.astype(bf16)
    there = other_core(total)
    input_grad = input_back(at, dn1_pieces, tok, middle_grad, small)
    even = e_index % 2 == 0
    total, there = total.astype(f32), there.astype(f32)
    summed = (total + there)[:, 1536:]
    first = jnp.where(even, total[:, :1536], there[:, :1536]).reshape(64, 4, 384)
    later = jnp.where(even, there[:, :1536], total[:, :1536]).reshape(64, 4, 384)
    qkv_own = jnp.concatenate(
        [first[:, :, :256].reshape(64, 1024), first[:, :, 256:].reshape(64, 512), later[:, :, :128].reshape(64, 512)],
        axis=1,
    )
    o_own = later[:, :, 128:].reshape(64, 1024)
    first_gain = jnp.sum(qkv_own * w_qkv.astype(f32), axis=1) / norm_gains[0].astype(f32)
    gains_own = jnp.stack([first_gain, summed[9, :64], summed[8, :64]])
    key_own = summed[8, 64:96]
    router_own = jnp.concatenate([summed[16:32, :64], summed[16:32, 64:]], axis=0).T
    return (output[None], input_grad[None], qkv_own, o_own, gains_own, key_own, router_own, in_own, down_own)


def solution(mesh):
    both = P("expert", GROUP, None)
    rows = P(GROUP, None)
    return jax.shard_map(
        shards,
        mesh=mesh,
        in_specs=(
            both,
            both,
            P("expert", None),
            both,
            P("expert", GROUP),
            rows,
            rows,
            P(None, GROUP),
            P(GROUP),
            rows,
            P("expert", GROUP, None, None),
            P("expert", GROUP, None),
        ),
        out_specs=(
            both,
            both,
            rows,
            rows,
            P(None, GROUP),
            P(GROUP),
            rows,
            P("expert", GROUP, None, None),
            P("expert", GROUP, None),
        ),
        check_vma=False,
    )
```

```python
import jax
import jax.numpy as jnp
from jax import lax
from jax.experimental import pallas as pl
from jax.experimental.pallas import tpu as pltpu
from jax.sharding import PartitionSpec as P

HEADS = 16
KV_HEADS = 8
HEAD_DIM = 64
TOPK = 8
HALF = 512
CAP = 40
SLOTS = 48
VMEM_BYTES = 64 * 1024 * 1024

GROUP = ("dp", "seq")
ALL = ("dp", "seq", "expert")
epsilon = 1e-05
highest = lax.Precision.HIGHEST
bf16 = jnp.bfloat16
f32 = jnp.float32


def dot(a, b, dims, **kw):
    return lax.dot_general(a, b, ((dims[0], dims[1]), ((), ())), preferred_element_type=f32, **kw)


def call(kernel, name, out_shape, *args, flops=10**8, scratch=(), moved=10**6, middle=()):
    whole = lambda a: pl.BlockSpec(a.shape, lambda _: (0,) * len(a.shape))
    specs = [pl.BlockSpec(memory_space=pltpu.SMEM)] + [whole(a) for a in args[1:]]
    for i in middle:
        specs[i] = pl.BlockSpec((512, 128), lambda _: (1, 0))
    return pl.pallas_call(
        kernel,
        grid=(1,),
        in_specs=specs,
        out_specs=jax.tree.map(whole, out_shape),
        out_shape=out_shape,
        scratch_shapes=list(scratch),
        compiler_params=pltpu.CompilerParams(vmem_limit_bytes=VMEM_BYTES),
        cost_estimate=pl.CostEstimate(flops=flops, bytes_accessed=moved, transcendentals=0),
        name=name,
    )(*args)


def sds(*shape, dtype=bf16):
    return jax.ShapeDtypeStruct(shape, dtype)


def block(index):
    return pl.ds(pl.multiple_of(index * 128, 128), 128)


def column(row):
    return jnp.broadcast_to(row, (128, 128)).T


def partner(x):
    lane = lax.broadcasted_iota(jnp.int32, x.shape, 1)
    return jnp.where(lane % 64 < 32, pltpu.roll(x, 96, 1), pltpu.roll(x, 32, 1))


def row_sums(x):
    ones = jnp.ones((8, x.shape[1]), f32)
    return dot(ones, x, ((1,), (1,)), precision=highest)[0:1]


def project_kernel(at, t0, t1, t2, t3, mine, theirs, n1_ref, raw_ref, kv_ref, parts_ref, small_ref, w_ref, rows):
    s = at[1]
    even = lax.rem(at[2], 2) == 0
    here, there = mine[:, :, :256].reshape(1024, 256), theirs[:, :, :256].reshape(1024, 256)
    w_ref[:, :256] = jnp.where(even, here, there)
    w_ref[:, 256:] = jnp.where(even, there, here)
    w = w_ref[...]
    lane = lax.broadcasted_iota(jnp.int32, (48, 128), 1)
    for i in range(8):
        low, high = mine[2 * i, :48, 256:384].astype(f32), mine[2 * i + 1, :48, 256:384].astype(f32)
        small_ref[:, 128 * i : 128 * (i + 1)] = jnp.where(lane < 64, low, pltpu.roll(high, 64, 1))
    gain = small_ref[32:33, :]
    for ds, t in enumerate((t0, t1, t2, t3)):
        x = t[...].astype(f32)
        low = (x * lax.rsqrt(jnp.mean(x * x, axis=1, keepdims=True) + epsilon) * gain).astype(bf16)
        raw = dot(low, w, ((1,), (0,)))
        place = lax.rem(s - ds + 4, 4)
        n1_ref[block(place), :] = low
        raw_ref[block(place), :] = raw
        kv_ref[block(place), :] = raw[:, 256:].astype(bf16)
        rows[pl.ds(place, 1), :] = row_sums(raw[:, :256] * raw[:, :256])
        rows[pl.ds(place + 4, 1), :] = row_sums(raw[:, 256:384] * raw[:, 256:384])
    parts_ref[...] = jnp.broadcast_to(rows[...][None], (16, 8, 128))
    start = pl.multiple_of(s * 256, 256)
    chunk = small_ref[35:36, pl.ds(start, 256)]
    at_row = lax.broadcasted_iota(jnp.int32, (256, 128), 0)
    at_col = lax.broadcasted_iota(jnp.int32, (256, 128), 1)
    pick = jnp.where(at_row == 64 * (at_col // 32) + at_col % 32, 1.0, 0.0)
    small_ref[40:41, 0:256] = small_ref[34:35, pl.ds(start, 256)]
    small_ref[40:41, 256:384] = dot(jnp.broadcast_to(chunk, (8, 256)), pick, ((1,), (0,)), precision=highest)[0:1]


def project(at, pieces, mine, theirs):
    return call(
        project_kernel,
        "project",
        [
            sds(512, 1024),
            sds(512, 512, dtype=f32),
            sds(512, 256),
            sds(16, 8, 128, dtype=f32),
            sds(48, 1024, dtype=f32),
            sds(1024, 512),
        ],
        at,
        *pieces,
        mine,
        theirs,
        flops=8 * 10**9,
        scratch=[pltpu.VMEM((8, 128), f32)],
    )


def document_of(places, at):
    found = jnp.zeros(places.shape, f32)
    for i in range(4):
        found = found + jnp.where(places >= at[3 + i], 1.0, 0.0)
    return jnp.where((places >= 0) & (places < 2048), found, -1.0)


def seen_bias(at, b):
    first = at[0] * 512 + 128 * b
    key = lax.broadcasted_iota(jnp.int32, (1152, 128), 0)
    query = lax.broadcasted_iota(jnp.int32, (1152, 128), 1)
    key_doc = document_of(first - HALF + key, at)
    query_doc = document_of(first + lax.broadcasted_iota(jnp.int32, (1, 128), 1), at)
    apart = key - query
    seen = (apart >= 0) & (apart < 2 * HALF) & (key_doc == query_doc)
    return jnp.where(seen, 0.0, -1e30)


def stacked_heads(tile, kh):
    lane = lax.broadcasted_iota(jnp.int32, (128, 128), 1)
    mine = (lane < 64) if kh == 0 else (lane >= 64)
    other = pltpu.roll(tile, 64, 1)
    first, second = (tile, other) if kh == 0 else (other, tile)
    return jnp.concatenate([jnp.where(mine, first, 0.0), jnp.where(mine, second, 0.0)], axis=0).astype(bf16)


def attend_kernel(at, raw, kv0, kv1, kv2, parts, small, cos, sin, attn, qb, kb, vb, lse, uq, uk, qinv, kinv, vt):
    d = at[0]
    for i in range(12):
        there = jnp.clip(d - 1 + i // 4, 0, 3)
        row = parts[4 * there][4 + i % 4 : 5 + i % 4]
        for s in range(1, 4):
            row = row + parts[4 * there + s][4 + i % 4 : 5 + i % 4]
        inverse = column(lax.rsqrt(row * (1.0 / 512) + epsilon))
        span = slice(128 * i, 128 * (i + 1))
        part = slice(128 * (i % 4), 128 * (i % 4 + 1))
        kv = (kv0, kv1, kv2)[i // 4]
        unit = kv[part, :128].astype(f32) * inverse
        key = unit * small[40:41, 256:384]
        uk[span, :] = unit
        kb[span, :] = (key * cos[span, :] + partner(key) * sin[span, :]).astype(bf16)
        value = kv[part, 128:]
        vb[span, :] = value
        vt[:, span] = value.T
        if i // 4 == 1:
            kinv[part, :] = inverse
            row = parts[4 * d][i % 4 : i % 4 + 1]
            for s in range(1, 4):
                row = row + parts[4 * d + s][i % 4 : i % 4 + 1]
            inverse = column(lax.rsqrt(row * (1.0 / 1024) + epsilon))
            qinv[part, :] = inverse
            for m in range(2):
                lanes = slice(128 * m, 128 * (m + 1))
                unit = raw[part, lanes] * inverse
                uq[part, lanes] = unit
                query = unit * small[40:41, lanes]
                qb[part, lanes] = (query * cos[span, :] + partner(query) * sin[span, :]).astype(bf16)
    for b in range(4):
        bias = seen_bias(at, b)
        bias = jnp.concatenate([bias, bias], axis=1)
        window = slice(128 * b, 128 * b + 1152)
        for kh in range(2):
            lanes = slice(128 * kh, 128 * (kh + 1))
            heads = stacked_heads(qb[128 * b : 128 * (b + 1), lanes].astype(f32), kh)
            scores = dot(kb[window, :], heads, ((1,), (1,))) * 0.125 + bias
            top = jnp.max(scores, axis=0, keepdims=True)
            weights = jnp.exp(scores - top)
            total = jnp.sum(weights, axis=0, keepdims=True)
            lse[2 * b + kh : 2 * b + kh + 1, :] = top + jnp.log(total)
            mixed = dot(vt[64 * kh : 64 * kh + 64, window], weights.astype(bf16), ((1,), (0,))) / total
            tile = jnp.concatenate([mixed[:, :128], mixed[:, 128:]], axis=0).T
            attn[b, :, lanes] = tile.astype(bf16)


def attend(at, raw, kvs, parts, small, cos, sin):
    return call(
        attend_kernel,
        "attend",
        [
            sds(4, 128, 256),
            sds(512, 256),
            sds(1536, 128),
            sds(1536, 128),
            sds(8, 256, dtype=f32),
            sds(512, 256, dtype=f32),
            sds(1536, 128, dtype=f32),
            sds(512, 128, dtype=f32),
            sds(512, 128, dtype=f32),
        ],
        at,
        raw,
        *kvs,
        parts,
        small,
        cos,
        sin,
        flops=15 * 10**9,
        scratch=[pltpu.VMEM((128, 1536), bf16)],
    )


def attend_back_kernel(
    at, got, qb, kb, vb, lse, uq, uk, cos, sin, base, wq, dkv_own, dkv_up, dkv_down, sums, kt, dk, dv, qgain, qrows
):
    for i in range(12):
        span = slice(128 * i, 128 * (i + 1))
        kt[:, span] = kb[span, :].T
    dk[...] = jnp.zeros_like(dk)
    dv[...] = jnp.zeros_like(dv)
    qgain[...] = jnp.zeros_like(qgain)
    for b in range(4):
        bias = seen_bias(at, b)
        bias = jnp.concatenate([bias, bias], axis=1)
        window = slice(128 * b, 128 * b + 1152)
        own = slice(128 * b, 128 * (b + 1))
        table = slice(HALF + 128 * b, HALF + 128 * (b + 1))
        total = jnp.zeros((128, 1), f32)
        for kh in range(2):
            lanes = slice(128 * kh, 128 * (kh + 1))
            query = qb[own, lanes].astype(f32)
            heads = stacked_heads(query, kh)
            grads = stacked_heads(got[b, :, lanes].astype(f32), kh)
            scores = dot(kb[window, :], heads, ((1,), (1,))) * 0.125 + bias
            probs = jnp.exp(scores - lse[2 * b + kh : 2 * b + kh + 1, :])
            prob_grad = dot(vb[window, :], grads, ((1,), (1,)))
            centre = jnp.sum(probs * prob_grad, axis=0, keepdims=True)
            score_grad = (probs * (prob_grad - centre)).astype(bf16)
            dv[window, :] += dot(probs.astype(bf16), grads, ((1,), (0,)))
            dk[window, :] += dot(score_grad, heads, ((1,), (0,))) * 0.125
            flat = dot(kt[64 * kh : 64 * kh + 64, window], score_grad, ((1,), (0,))) * 0.125
            dq = jnp.concatenate([flat[:, :128], flat[:, 128:]], axis=0).T.astype(bf16).astype(f32)
            total = total + jnp.sum(dq * query, axis=1, keepdims=True)
            turned = dq * cos[table, :] - partner(dq) * sin[table, :]
            wq[own, lanes] = turned
            qgain[0:1, lanes] += jnp.sum(turned * uq[own, lanes], axis=0, keepdims=True)
        qrows[b : b + 1, :] = jnp.broadcast_to(total, (128, 128)).T[0:1]
    kgain = jnp.zeros((1, 128), f32)
    krows = []
    for i in range(12):
        span = slice(128 * i, 128 * (i + 1))
        part = slice(128 * (i % 4), 128 * (i % 4 + 1))
        grad = dk[span, :]
        spot = jnp.sum(grad * kb[span, :].astype(f32), axis=1, keepdims=True)
        krows.append(jnp.broadcast_to(spot, (128, 128)).T[0:1])
        turned = grad * cos[span, :] - partner(grad) * sin[span, :]
        kgain = kgain + jnp.sum(turned * uk[span, :], axis=0, keepdims=True)
        target = (dkv_down, dkv_own, dkv_up)[i // 4]
        target[part, :128] = grad.astype(target.dtype)
        target[part, 128:] = dv[span, :].astype(target.dtype)
    lane = lax.broadcasted_iota(jnp.int32, (1, 128), 1)
    none = jnp.zeros((6, 128), f32)
    for there in range(4):
        here = jnp.where(at[0] == there, 1.0, 0.0)
        mine = jnp.where(at[1] == there, 1.0, 0.0)
        rows = [qrows[0:4, :] * here]
        for i in range(4):
            row = jnp.zeros((1, 128), f32)
            for part in range(3):
                row = row + krows[4 * part + i] * jnp.where(at[0] - 1 + part == there, 1.0, 0.0)
            rows.append(row)
        for s in range(4):
            q_tile = qgain[0:1, 128 * (s // 2) : 128 * (s // 2 + 1)]
            if s % 2:
                q_tile = pltpu.roll(q_tile, 64, 1)
            k_tile = pltpu.roll(kgain, (64 - 32 * s) % 128, 1)
            gains = jnp.where(lane < 64, q_tile, jnp.where(lane < 96, k_tile, 0.0)) * mine
            more = base[4 * there + s]
            sums[4 * there + s] = jnp.concatenate(rows + [gains, more[0:1], none, more[8:24]], axis=0).astype(bf16)


def attend_back(at, got, qb, kb, vb, lse, uq, uk, cos, sin, base):
    return call(
        attend_back_kernel,
        "attend_back",
        [
            sds(512, 256, dtype=f32),
            sds(512, 256, dtype=f32),
            sds(512, 256),
            sds(512, 256),
            sds(16, 32, 128),
        ],
        at,
        got,
        qb,
        kb,
        vb,
        lse,
        uq,
        uk,
        cos,
        sin,
        base,
        flops=30 * 10**9,
        scratch=[
            pltpu.VMEM((128, 1536), bf16),
            pltpu.VMEM((1536, 128), f32),
            pltpu.VMEM((1536, 128), f32),
            pltpu.VMEM((8, 256), f32),
            pltpu.VMEM((8, 128), f32),
        ],
    )


def route_kernel(at, c0, c1, c2, c3, others, place_ref, used_ref, gs_ref):
    ids = lax.broadcasted_iota(jnp.int32, (32, 128), 0) + 4 * at[2]
    ids = jnp.where(ids >= 32, ids - 32, ids).astype(f32)
    slot = lax.broadcasted_iota(jnp.int32, (SLOTS, 128), 0).astype(f32)
    for j, ref in enumerate((c0, c1, c2, c3) + tuple(others.at[i] for i in range(4))):
        meta = ref[:, 1024:].astype(f32)
        turned = meta.T
        used = turned[0:1] == ids
        for k in range(1, TOPK):
            used = used | (turned[k : k + 1] == ids)
        used_ref[j] = jnp.where(used, 1.0, 0.0)
        earlier = jnp.where(meta[:, 8:9] < turned[8:9], 1.0, 0.0).astype(bf16)
        before = dot(jnp.where(used, 1.0, 0.0).astype(bf16), earlier, ((1,), (0,)))
        spot = jnp.where(used & (before < CAP), before, 1000.0)
        chosen = jnp.concatenate([jnp.where(slot == spot[l : l + 1], 1.0, 0.0) for l in range(4)], axis=0).astype(bf16)
        place_ref[j] = chosen
        ups = dot(chosen, ref[:, :1024], ((1,), (0,))).astype(bf16)
        for l in range(4):
            gs_ref[l, SLOTS * j : SLOTS * (j + 1), :] = ups[SLOTS * l : SLOTS * (l + 1)]


def route(at, cots):
    return call(
        route_kernel,
        "route",
        [sds(8, 4 * SLOTS, 128), sds(8, 32, 128, dtype=f32), sds(4, 8 * SLOTS, 1024)],
        at,
        *cots,
        flops=6 * 10**9,
    )


def expert_step(where_ref, *refs):
    n2_refs = refs[0:8]
    place, used_ref, gs, router_ref, w_ref = refs[8:13]
    dn_refs = tuple(ref.at[i] for ref in refs[13:15] for i in range(4))
    out_refs = tuple(ref.at[i] for ref in refs[15:17] for i in range(4))
    grads_ref = refs[17]
    xs, gate, ys, dxs, dgs = refs[18:23]
    step = pl.program_id(0)

    @pl.when(step == 0)
    def _():
        for j in range(8):
            n2 = n2_refs[j][...]
            used = used_ref[j] > 0.5
            logits = dot(router_ref[...], n2, ((1,), (1,)))
            masked = jnp.where(used, logits, -1e30)
            grown = jnp.where(used, jnp.exp(masked - jnp.max(masked, axis=0, keepdims=True)), 0.0)
            gates = grown / jnp.sum(grown, axis=0, keepdims=True)
            chosen = place[j]
            rows = dot(chosen, n2, ((1,), (0,))).astype(bf16)
            for l in range(4):
                span = slice(SLOTS * j, SLOTS * (j + 1))
                hit = chosen[SLOTS * l : SLOTS * (l + 1)].astype(f32)
                share = jnp.sum(hit * gates[l : l + 1], axis=1, keepdims=True)
                gate[l, span, :] = jnp.broadcast_to(share, (SLOTS, 128))
                xs[l, span, :] = rows[SLOTS * l : SLOTS * (l + 1)]

    w_in = w_ref[:, 0, :64, :].reshape(1024, 1024)
    w_out = w_ref[:, 0, 64:, :].reshape(512, 1024)
    x = xs[step]
    both = dot(x, w_in, ((1,), (0,)))
    gate_part, up_part = both[:, :512], both[:, 512:]
    sig = jax.nn.sigmoid(gate_part)
    silu = gate_part * sig
    hidden = (silu * up_part).astype(bf16)
    g = gs[0].astype(f32)
    share = gate[step][:, 0:1]
    dy = (g * share).astype(bf16)
    dh = dot(dy, w_out, ((1,), (1,)))
    dgu = jnp.concatenate(
        [dh * up_part * (sig * (1.0 + gate_part * (1.0 - sig))), dh * silu], axis=1
    ).astype(bf16)
    dxs[step] = dot(dgu, w_in, ((1,), (1,))).astype(bf16)
    y = dot(hidden, w_out, ((1,), (0,))).astype(bf16).astype(f32)
    ys[step] = (y * share).astype(bf16)
    lane = lax.broadcasted_iota(jnp.int32, (8 * SLOTS, 128), 1)
    dgate = jnp.sum(g * y, axis=1, keepdims=True)
    dgs[step] = jnp.where(lane == 4 * where_ref[0] + step, dgate, 0.0).astype(bf16)
    grads_ref[:, 0, :64, :] = dot(x, dgu, ((0,), (0,))).astype(bf16).reshape(16, 64, 1024)
    grads_ref[:, 0, 64:, :] = dot(hidden, dy, ((0,), (0,))).astype(bf16).reshape(16, 32, 1024)

    @pl.when(step == 3)
    def _():
        for j in range(8):
            chosen = place[j]
            span = slice(SLOTS * j, SLOTS * (j + 1))
            for source, target, lo, hi in ((dxs, dn_refs[j], 0, 1024), (dgs, dn_refs[j], 1024, 1152), (ys, out_refs[j], 0, 1024)):
                stacked = jnp.concatenate([source[l, span, :] for l in range(4)], axis=0)
                target[:, lo:hi] = dot(chosen, stacked, ((0,), (0,))).astype(bf16)


def experts(e_index, n2s, place, used, gs, router_t, weights):
    whole = lambda *s: pl.BlockSpec(s, lambda i, *_: (0,) * len(s))
    each = lambda cols: pl.BlockSpec((1, 8 * SLOTS, cols), lambda i, *_: (i, 0, 0))
    owned = pl.BlockSpec((16, 1, 96, 1024), lambda i, *_: (0, i, 0, 0))
    shape = lambda *s: jax.ShapeDtypeStruct(s, bf16)
    return pl.pallas_call(
        expert_step,
        grid_spec=pltpu.PrefetchScalarGridSpec(
            num_scalar_prefetch=1,
            grid=(4,),
            in_specs=[whole(128, 1024)] * 8
            + [
                whole(8, 4 * SLOTS, 128),
                whole(8, 32, 128),
                each(1024),
                whole(32, 1024),
                owned,
            ],
            out_specs=[whole(4, 128, 1152)] * 2 + [whole(4, 128, 1024)] * 2 + [owned],
            scratch_shapes=[
                pltpu.VMEM((4, 8 * SLOTS, 1024), bf16),
                pltpu.VMEM((4, 8 * SLOTS, 128), f32),
                pltpu.VMEM((4, 8 * SLOTS, 1024), bf16),
                pltpu.VMEM((4, 8 * SLOTS, 1024), bf16),
                pltpu.VMEM((4, 8 * SLOTS, 128), bf16),
            ],
        ),
        out_shape=[shape(4, 128, 1152)] * 2
        + [shape(4, 128, 1024)] * 2
        + [shape(16, 4, 96, 1024)],
        compiler_params=pltpu.CompilerParams(vmem_limit_bytes=VMEM_BYTES),
        cost_estimate=pl.CostEstimate(flops=28 * 10**9, bytes_accessed=40 * 10**6, transcendentals=10**6),
        name="experts",
    )(e_index, *n2s, place, used, gs, router_t, weights)


def split(x):
    high = x.astype(bf16)
    return high, (x - high.astype(f32)).astype(bf16)


def slice_of(at, i):
    chip, core = at[2] // 2, lax.rem(at[2], 2)
    return 2 * lax.rem(chip - i % 4 + 4, 4) + (core if i < 4 else 1 - core)


def o_piece(refs, i):
    mine, x1, x2, x3, theirs, others = refs
    if i % 4 == 0:
        return (mine if i == 0 else theirs)[:, :, 384:].reshape(1024, 128)
    return (x1, x2, x3)[i - 1][...] if i < 4 else others[i - 5]


def middle_kernel(at, tok, attn, *refs):
    parts, (small, middle_ref, low_ref, inverse_ref) = refs[:6], refs[6:]
    rows = jnp.concatenate([attn[i] for i in range(4)], axis=1)
    for i in range(8):
        lanes = block(slice_of(at, i))
        middle_ref[:, lanes] = tok[:, lanes].astype(f32) + dot(rows, o_piece(parts, i), ((1,), (0,)))
    total = middle_ref[...]
    inverse = lax.rsqrt(jnp.mean(total * total, axis=1, keepdims=True) + epsilon)
    low_ref[...] = (total * inverse * small[33:34]).astype(bf16)
    inverse_ref[...] = jnp.broadcast_to(inverse, (128, 128))


def make_middle(at, tok, attn, parts, small):
    return call(
        middle_kernel,
        "middle",
        [sds(128, 1024, dtype=f32), sds(128, 1024), sds(128, 128, dtype=f32)],
        at,
        tok,
        attn,
        *parts,
        small,
        flops=6 * 10**9,
    )


def middle_back_kernel(
    at, p0a, p0b, p1, p2, p3, middle, inverse_ref, low, cot, small, o0, o1, o2, o3, o4, o5, grad_ref, send_ref, sums_ref, branch_ref
):
    total = p0a[0].astype(f32) + p0b[0].astype(f32) + p1[...].astype(f32) + p2[...].astype(f32) + p3[...].astype(f32)
    dgates = total[:, 1024:1056]
    router_t = small[0:32].astype(bf16)
    logits = dot(low[...], router_t, ((1,), (1,)))
    ids = lax.broadcasted_iota(jnp.int32, (128, 32), 1).astype(f32)
    named = cot[:, 1024:].astype(f32)
    used = named[:, 0:1] == ids
    for k in range(1, TOPK):
        used = used | (named[:, k : k + 1] == ids)
    masked = jnp.where(used, logits, -1e30)
    grown = jnp.where(used, jnp.exp(masked - jnp.max(masked, axis=1, keepdims=True)), 0.0)
    gates = grown / jnp.sum(grown, axis=1, keepdims=True)
    logit_grad = gates * (dgates - jnp.sum(gates * dgates, axis=1, keepdims=True))
    high, rest = split(logit_grad)
    dn2 = total[:, :1024] + dot(high, router_t, ((1,), (0,))) + dot(rest, router_t, ((1,), (0,)))
    inverse = inverse_ref[:, 0:1]
    unit = middle[...] * inverse
    scaled = dn2 * small[33:34]
    grad = cot[:, :1024].astype(f32) + inverse * (scaled - unit * jnp.mean(scaled * unit, axis=1, keepdims=True))
    grad_ref[...] = grad
    branch = grad.astype(bf16)
    branch_ref[...] = branch
    back = jnp.zeros((128, 1024), f32)
    for i in range(8):
        piece = o_piece((o0, o1, o2, o3, o4, o5), i)
        back = back + dot(branch_ref[:, block(slice_of(at, i))], piece, ((1,), (1,)))
    for s in range(4):
        send_ref[s, :, 0:256] = back[:, 256 * s : 256 * (s + 1)].astype(bf16)
        send_ref[s, :, 256:512] = branch[:, 256 * s : 256 * (s + 1)]
    routers = dot(high, low[...], ((0,), (0,))) + dot(rest, low[...], ((0,), (0,)))
    second = jnp.sum(dn2 * unit, axis=0, keepdims=True)
    lane = lax.broadcasted_iota(jnp.int32, (16, 128), 1)
    for i in range(16):
        lanes = slice(128 * (i // 2), 128 * (i // 2 + 1))
        upper, lower, row = routers[0:16, lanes], routers[16:32, lanes], second[:, lanes]
        if i % 2 == 0:
            tile = jnp.where(lane < 64, upper, pltpu.roll(lower, 64, 1))
        else:
            tile = jnp.where(lane < 64, pltpu.roll(upper, 64, 1), lower)
            row = pltpu.roll(row, 64, 1)
        sums_ref[i] = jnp.concatenate([row, jnp.zeros((7, 128), f32), tile], axis=0)


def middle_back(at, pieces, middle, inverse, low, cot, small, parts):
    return call(
        middle_back_kernel,
        "middle_back",
        [sds(128, 1024, dtype=f32), sds(4, 128, 512), sds(16, 24, 128, dtype=f32)],
        at,
        *pieces,
        middle,
        inverse,
        low,
        cot,
        small,
        *parts,
        flops=12 * 10**9,
        scratch=[pltpu.VMEM((128, 1024), bf16)],
    )


def out_grad_kernel(at, a0, a1, a2, a3, got, out_ref):
    cols = jnp.concatenate([got[i, :, 256:512] for i in range(4)], axis=0)
    for k, part in enumerate((a0, a1, a2, a3)):
        start = pl.multiple_of(lax.rem(at[1] - k + 4, 4) * 256, 256)
        rows = jnp.concatenate([part[i] for i in range(4)], axis=0)
        out_ref[pl.ds(start, 256), :] = dot(rows, cols, ((0,), (0,))).astype(bf16)


def out_grads(at, attns, got):
    return call(out_grad_kernel, "out_grads", sds(1024, 256), at, *attns, got, flops=3 * 10**9)


def finish_kernel(
    at, wq, own, up, down, sums, uq, uk, qinv, kinv, small, cos, sin, n1, w_ref, o_part,
    dn0, dn1, dn2, dn3, keep_ref, send_ref, sums_ref, dqkv, grads,
):
    got = sums[0].astype(f32)
    for i in range(1, 16):
        got = got + sums[i].astype(f32)
    sums_ref[...] = got
    for i in range(4):
        part = slice(128 * i, 128 * (i + 1))
        q_mean = column(got[i : i + 1]) * (1.0 / 1024)
        for m in range(2):
            lanes = slice(128 * m, 128 * (m + 1))
            grad = wq[part, lanes] * small[40:41, lanes] - uq[part, lanes] * q_mean
            dqkv[part, lanes] = (qinv[part, :] * grad).astype(bf16)
        total = own[part, :] + up[part, :].astype(f32) + down[part, :].astype(f32)
        dk = total[:, :128].astype(bf16).astype(f32)
        turned = dk * cos[part, :] - partner(dk) * sin[part, :]
        k_mean = column(got[4 + i : 5 + i]) * (1.0 / 512)
        grad = turned * small[40:41, 256:384] - uk[part, :] * k_mean
        dqkv[part, 256:384] = (kinv[part, :] * grad).astype(bf16)
        dqkv[part, 384:512] = total[:, 128:].astype(bf16)
    w = w_ref[...]
    for k, ref in enumerate((dn0, dn1, dn2, dn3)):
        ref[...] = dot(dqkv[block(lax.rem(at[1] + k, 4)), :], w, ((1,), (1,))).astype(bf16)
    grads[:, :, :512] = dot(n1[...], dqkv[...], ((1,), (0,))).astype(bf16).reshape(16, 64, 512)
    grads[:, :, 512:] = o_part[...].reshape(16, 64, 256)
    even = lax.rem(at[2], 2) == 0
    for k in range(4):
        rows = pl.ds(pl.multiple_of(16 * lax.rem(at[2] // 2 + k, 4), 16), 16)
        left, right = grads[:, rows, :384], grads[:, rows, 384:]
        keep_ref[k] = jnp.where(even, left, right)
        send_ref[k] = jnp.where(even, right, left)


def finish(at, wq, own, up, down, sums, uq, uk, qinv, kinv, small, cos, sin, n1, w_got, o_part):
    return call(
        finish_kernel,
        "finish",
        [sds(128, 1024)] * 4 + [sds(4, 16, 16, 384)] * 2 + [sds(sums.shape[1], 128, dtype=f32)],
        at, wq, own, up, down, sums, uq, uk, qinv, kinv, small, cos, sin, n1, w_got, o_part,
        middle=(7, 11, 12),
        flops=20 * 10**9,
        scratch=[pltpu.VMEM((512, 512), bf16), pltpu.VMEM((16, 64, 768), bf16)],
    )


def input_kernel(at, p0, p1, p2, p3, tok, grad_ref, small, out_ref):
    dn1 = p0[...].astype(f32) + p1[...].astype(f32) + p2[...].astype(f32) + p3[...].astype(f32)
    x = tok[...].astype(f32)
    inverse = lax.rsqrt(jnp.mean(x * x, axis=1, keepdims=True) + epsilon)
    unit = x * inverse
    scaled = dn1 * small[32:33]
    out_ref[...] = grad_ref[...] + inverse * (scaled - unit * jnp.mean(scaled * unit, axis=1, keepdims=True))


def input_back(at, pieces, tok, grad, small):
    return call(input_kernel, "input_back", sds(128, 1024, dtype=f32), at, *pieces, tok, grad, small)


def pack_kernel(at, w_ref, o_ref, router_ref, gain_ref, key_ref, out_ref):
    even = lax.rem(at[2], 2) == 0
    piece = o_ref[:, block(at[2])]
    key = jnp.concatenate([key_ref[...].astype(f32), jnp.zeros((1, 32), f32)], axis=1)
    extra = jnp.concatenate(
        [router_ref[...].astype(f32), gain_ref[...].astype(f32), key, jnp.zeros((28, 64), f32)], axis=0
    )
    extra = jnp.concatenate([extra, jnp.zeros((64, 64), f32)], axis=1).astype(bf16)
    for s in range(4):
        queries = w_ref[:, 256 * s : 256 * (s + 1)]
        keys = w_ref[:, 1024 + 128 * s : 1024 + 128 * (s + 1)]
        values = w_ref[:, 1536 + 128 * s : 1536 + 128 * (s + 1)]
        half = jnp.where(even, queries, jnp.concatenate([keys, values], axis=1))
        for d in range(4):
            out_ref[4 * d + s, :, 0:256] = half
            out_ref[4 * d + s, :, 256:384] = extra
            out_ref[4 * d + s, :, 384:512] = piece


def pack(at, *args):
    return call(pack_kernel, "pack", sds(16, 64, 512), at, *args, flops=10**9)


def turn_kernel(at, x_ref, out_ref):
    out_ref[...] = x_ref[...].T


def turned(at, x):
    return call(turn_kernel, "turned", sds(x.shape[1], x.shape[0]), at, x, flops=10**9)


def last_kernel(at, *refs):
    pieces, (w_ref, gain_ref, qkv_ref, o_ref, gains_ref, key_ref, router_ref) = refs[:8], refs[8:]
    even = lax.rem(at[2], 2) == 0
    sums = jnp.zeros((16, 256), f32)
    for k in range(4):
        rows = pl.ds(pl.multiple_of(16 * lax.rem(at[2] // 2 - k + 4, 4), 16), 16)
        mine, theirs = pieces[k][...].astype(f32), pieces[4 + k][...].astype(f32)
        sums = sums + mine[:, 1536:] + theirs[:, 1536:]
        first, later = jnp.where(even, mine, theirs), jnp.where(even, theirs, mine)
        for s in range(4):
            lanes = 384 * s
            qkv_ref[rows, 256 * s : 256 * (s + 1)] = first[:, lanes : lanes + 256]
            qkv_ref[rows, 1024 + 128 * s : 1024 + 128 * (s + 1)] = first[:, lanes + 256 : lanes + 384]
            qkv_ref[rows, 1536 + 128 * s : 1536 + 128 * (s + 1)] = later[:, lanes : lanes + 128]
            o_ref[rows, 256 * s : 256 * (s + 1)] = later[:, lanes + 128 : lanes + 384]
    first_gain = row_sums(qkv_ref[...] * w_ref[...].astype(f32)) / gain_ref[0:1, :].astype(f32)
    gains_ref[0:1, :] = first_gain
    gains_ref[1:2, :] = sums[9:10, 128:192]
    gains_ref[2:3, :] = sums[8:9, 128:192]
    key_ref[...] = sums[8:9, 192:224]
    router_ref[...] = jnp.concatenate([sums[:, :64], sums[:, 64:128]], axis=0)


def last(at, pieces, w_qkv, norm_gains):
    return call(
        last_kernel,
        "last",
        [
            sds(64, 2048, dtype=f32),
            sds(64, 1024, dtype=f32),
            sds(3, 64, dtype=f32),
            sds(1, 32, dtype=f32),
            sds(32, 64, dtype=f32),
        ],
        at, *pieces, w_qkv, norm_gains,
    )


def chip_kernel(at, r0, r1, r2, r3, out_ref):
    total = r0[...].astype(f32) + r1[...].astype(f32) + r2[...].astype(f32) + r3[...].astype(f32)
    out_ref[...] = total.astype(bf16)


def chip_sum(at, pieces):
    return call(chip_kernel, "chip_sum", sds(*pieces[0].shape), at, *pieces, flops=10**9)


def rows_kernel(at, got, sums, out_ref):
    for s in range(4):
        total = got[s].astype(f32)
        for d in range(1, 4):
            total = total + got[4 * d + s].astype(f32)
        out_ref[:, 384 * s : 384 * (s + 1)] = total.astype(bf16)
    out_ref[:, 1536:1664] = sums[16:32, :].astype(bf16)
    out_ref[:, 1664:1792] = sums[0:16, :].astype(bf16)


def sum_rows(at, got, sums):
    return call(rows_kernel, "sum_rows", sds(16, 1792), at, got, sums, flops=10**9)


def join_kernel(at, mine, theirs, *outs):
    skipped = 4 - len(outs)
    for k, ref in enumerate(outs):
        ref[...] = (mine[k + skipped].astype(f32) + theirs[k + skipped].astype(f32)).astype(bf16)


def join(at, mine, theirs, count=3):
    return call(join_kernel, "join", [sds(*mine.shape[1:])] * count, at, mine, theirs, flops=2 * 10**9)


def swap(array, axis):
    return lax.all_to_all(array, axis, split_axis=0, concat_axis=0, tiled=True)


def spread(array, axis, ways):
    return swap(jnp.broadcast_to(array[None], (ways,) + array.shape), axis)


def along_seq(array, k):
    return lax.ppermute(array, "seq", [(i, (i + k) % 4) for i in range(4)])


def along_dp(array, k):
    return lax.ppermute(array, "dp", [(i, (i + k) % 4) for i in range(4)])


def along_x(array, k):
    return lax.ppermute(array, "expert", [(i, (i + 2 * k) % 8) for i in range(8)])


def other_core(array):
    return lax.ppermute(array, "expert", [(i, i ^ 1) for i in range(8)])


def gather_x(array):
    return [array] + [along_x(array, k) for k in range(1, 4)]


def return_x(mine, joined, sums):
    return [mine, joined] + [along_x(sums[k - 1], -k) for k in range(1, 4)]


def after(values, *others):
    return lax.optimization_barrier((values, others))[0]


def shards(tokens, cotangent, doc_lengths, routes, route_rank, w_qkv, w_o, norm_gains, key_gain, w_router, w_in, w_out):
    d_index = lax.axis_index("dp")
    s_index = lax.axis_index("seq")
    e_index = lax.axis_index("expert")
    lengths = doc_lengths[0]
    tok = tokens[0]
    place = jnp.stack([d_index, s_index, e_index]).astype(jnp.int32)
    ends = [lengths[0]]
    for i in range(1, 4):
        ends.append(ends[-1] + lengths[i])
    at = jnp.concatenate([place, jnp.stack(ends)])
    w_send = pack(place, w_qkv, w_o, w_router.T, norm_gains, key_gain[None])
    w_mine = swap(w_send, GROUP)
    tok_pieces = [tok] + [along_seq(tok, k) for k in range(1, 4)]
    w_in, w_out = after((w_in, w_out), w_send)
    moe_shard = jnp.concatenate([w_in.reshape(4, 64, 1024), w_out], axis=1)
    cot = jnp.concatenate(
        [cotangent[0], routes[0].astype(bf16), route_rank[0].astype(bf16)[:, None], jnp.zeros((128, 119), bf16)], axis=1
    )
    cots = gather_x(cot)
    places = d_index * 512 - HALF + jnp.arange(1536, dtype=jnp.int32)
    starts = [jnp.zeros((), jnp.int32)] + ends
    begins = jnp.zeros((1536,), jnp.int32)
    for start in starts:
        begins = jnp.maximum(begins, jnp.where(places >= start, start, 0))
    lane = jnp.arange(128, dtype=jnp.int32)
    frequency = 10000.0 ** (-(lane % 32).astype(f32) / 32)
    angles = (places - begins).astype(f32)[:, None] * frequency[None, :]
    cos = jnp.cos(angles)
    sin = jnp.sin(angles) * jnp.where(lane % 64 < 32, -1.0, 1.0)[None, :]

    moe_shard = after(moe_shard, tok_pieces)
    moe_all = lax.all_gather(moe_shard, GROUP, axis=0, tiled=False)
    w_mine, cots = after((w_mine, cots), cos, sin, tok_pieces)
    w_theirs = other_core(w_mine)
    o_mine = w_mine[:, :, 384:].reshape(1024, 128)
    o_x = [along_x(o_mine, k) for k in range(1, 4)]
    cots = cots + [other_core(jnp.stack(cots))]
    n1, raw, kv, parts, small, w_cols = project(at, tok_pieces, w_mine, w_theirs)
    up = [(i, i + 1) for i in range(3)]
    down = [(i + 1, i) for i in range(3)]
    kv_before = lax.ppermute(kv, "dp", up)
    kv_after = lax.ppermute(kv, "dp", down)
    parts = swap(parts, GROUP)
    raw = after(raw, o_x)
    attn, qb, kb, vb, lse, uq, uk, qinv, kinv = attend(at, raw, [kv_before, kv, kv_after], parts, small, cos, sin)
    attn_got = swap(attn, "seq")
    o_parts = [w_mine] + o_x + [w_theirs, other_core(jnp.stack(o_x))]
    middle, n2, inverse = make_middle(at, tok, attn_got, o_parts, small)
    router_t = jnp.roll(small[:32], -4 * e_index, axis=0).astype(bf16)
    routed = route(place, after(cots, n2))
    n2s, _ = lax.optimization_barrier((gather_x(n2), (routed, router_t)))
    n2s = n2s + [other_core(n) for n in n2s]
    made = experts(e_index[None].astype(jnp.int32), n2s, *routed, router_t, moe_all)
    attns = [attn] + [along_seq(attn, k) for k in range(1, 4)]
    made = after(made, attns)
    joined = other_core(made[1])
    sums = join(place, made[0], joined)
    dn_pieces = return_x(made[0], joined, sums)
    moe_own = lax.psum_scatter(made[4].reshape(16 * 384, 1024), GROUP, scatter_dimension=0, tiled=True)
    moe_own = moe_own.reshape(4, 96, 1024).astype(f32)
    in_own = moe_own[:, :64].reshape(4, 64, 2, 512)
    down_own = moe_own[:, 64:]
    middle_grad, grad_send, base = middle_back(at, dn_pieces, middle, inverse, n2, cot, small, o_parts)
    grad_got = swap(grad_send, "seq")
    n1_turned = turned(at, after(n1, grad_send))
    out_joined = other_core(after(made[3], n1_turned))
    out_sums = join(place, made[2], out_joined)
    out_pieces = [along_x(out_sums[k - 1], -k) for k in range(1, 4)]
    grad_got = after(grad_got, out_sums)
    wq, dkv_own, dkv_up, dkv_down, sums = attend_back(at, grad_got, qb, kb, vb, lse, uq, uk, cos, sin, base)
    from_before = lax.ppermute(dkv_up, "dp", up)
    from_after = lax.ppermute(dkv_down, "dp", down)
    sums = swap(after(sums, out_pieces), GROUP)
    o_part = out_grads(at, attns, after(grad_got, wq))
    done = finish(
        at, wq, dkv_own, from_before, from_after, sums, uq, uk, qinv, kinv, small, cos, sin, n1_turned, w_cols, o_part
    )
    dn1_pieces = [done[0]] + [along_seq(done[k], k) for k in range(1, 4)]
    keep, send, summed = done[4:]
    halves = join(place, keep, other_core(send), 4)
    halves = chip_sum(place, [halves[0]] + [along_x(halves[k], k) for k in range(1, 4)])
    halves = swap(after(halves, in_own, down_own), GROUP)
    input_grad = input_back(at, dn1_pieces, tok, middle_grad, small)
    output = middle + made[2][0].astype(f32) + out_joined[0].astype(f32)
    for piece in out_pieces:
        output = output + piece.astype(f32)
    output = output.astype(bf16)
    mine = gather_x(sum_rows(place, after(halves, output), summed))
    theirs = [other_core(piece) for piece in mine]
    theirs = after(theirs, input_grad)
    qkv_own, o_own, gains_own, key_own, router_own = last(place, mine + theirs, w_qkv, norm_gains)
    return (output[None], input_grad[None], qkv_own, o_own, gains_own, key_own[0], router_own.T, in_own, down_own)


def solution(mesh):
    both = P("expert", GROUP, None)
    rows = P(GROUP, None)
    return jax.shard_map(
        shards,
        mesh=mesh,
        in_specs=(
            both,
            both,
            P("expert", None),
            both,
            P("expert", GROUP),
            rows,
            rows,
            P(None, GROUP),
            P(GROUP),
            rows,
            P("expert", GROUP, None, None),
            P("expert", GROUP, None),
        ),
        out_specs=(
            both,
            both,
            rows,
            rows,
            P(None, GROUP),
            P(GROUP),
            rows,
            P("expert", GROUP, None, None),
            P("expert", GROUP, None),
        ),
        check_vma=False,
    )
```

```python
import jax
import jax.numpy as jnp
from jax import lax
from jax.experimental import pallas as pl
from jax.experimental.pallas import tpu as pltpu
from jax.sharding import PartitionSpec as P

HEADS = 16
KV_HEADS = 8
HEAD_DIM = 64
TOPK = 8
HALF = 512
CAP = 40
SLOTS = 48
VMEM_BYTES = 64 * 1024 * 1024

GROUP = ("dp", "seq")
ALL = ("dp", "seq", "expert")
epsilon = 1e-05
highest = lax.Precision.HIGHEST
bf16 = jnp.bfloat16
f32 = jnp.float32


def dot(a, b, dims, **kw):
    return lax.dot_general(a, b, ((dims[0], dims[1]), ((), ())), preferred_element_type=f32, **kw)


def call(kernel, name, out_shape, *args, flops=10**8, scratch=(), moved=10**6, middle=()):
    whole = lambda a: pl.BlockSpec(a.shape, lambda _: (0,) * len(a.shape))
    specs = [pl.BlockSpec(memory_space=pltpu.SMEM)] + [whole(a) for a in args[1:]]
    for i in middle:
        specs[i] = pl.BlockSpec((512, 128), lambda _: (1, 0))
    return pl.pallas_call(
        kernel,
        grid=(1,),
        in_specs=specs,
        out_specs=jax.tree.map(whole, out_shape),
        out_shape=out_shape,
        scratch_shapes=list(scratch),
        compiler_params=pltpu.CompilerParams(vmem_limit_bytes=VMEM_BYTES),
        cost_estimate=pl.CostEstimate(flops=flops, bytes_accessed=moved, transcendentals=0),
        name=name,
    )(*args)


def sds(*shape, dtype=bf16):
    return jax.ShapeDtypeStruct(shape, dtype)


def block(index):
    return pl.ds(pl.multiple_of(index * 128, 128), 128)


def column(row):
    return jnp.broadcast_to(row, (128, 128)).T


def partner(x):
    lane = lax.broadcasted_iota(jnp.int32, x.shape, 1)
    return jnp.where(lane % 64 < 32, pltpu.roll(x, 96, 1), pltpu.roll(x, 32, 1))


def row_sums(x):
    ones = jnp.ones((8, x.shape[1]), f32)
    return dot(ones, x, ((1,), (1,)), precision=highest)[0:1]


def project_kernel(at, t0, t1, t2, t3, mine, theirs, n1_ref, raw_ref, kv_ref, parts_ref, small_ref, w_ref, rows):
    s = at[1]
    even = lax.rem(at[2], 2) == 0
    here, there = mine[:, :, :256].reshape(1024, 256), theirs[:, :, :256].reshape(1024, 256)
    w_ref[:, :256] = jnp.where(even, here, there)
    w_ref[:, 256:] = jnp.where(even, there, here)
    w = w_ref[...]
    lane = lax.broadcasted_iota(jnp.int32, (48, 128), 1)
    for i in range(8):
        low, high = mine[2 * i, :48, 256:384].astype(f32), mine[2 * i + 1, :48, 256:384].astype(f32)
        small_ref[:, 128 * i : 128 * (i + 1)] = jnp.where(lane < 64, low, pltpu.roll(high, 64, 1))
    gain = small_ref[32:33, :]
    for ds, t in enumerate((t0, t1, t2, t3)):
        x = t[...].astype(f32)
        low = (x * lax.rsqrt(jnp.mean(x * x, axis=1, keepdims=True) + epsilon) * gain).astype(bf16)
        raw = dot(low, w, ((1,), (0,)))
        place = lax.rem(s - ds + 4, 4)
        n1_ref[block(place), :] = low
        raw_ref[block(place), :] = raw
        kv_ref[block(place), :] = raw[:, 256:].astype(bf16)
        rows[pl.ds(place, 1), :] = row_sums(raw[:, :256] * raw[:, :256])
        rows[pl.ds(place + 4, 1), :] = row_sums(raw[:, 256:384] * raw[:, 256:384])
    parts_ref[...] = jnp.broadcast_to(rows[...][None], (16, 8, 128))
    start = pl.multiple_of(s * 256, 256)
    chunk = small_ref[35:36, pl.ds(start, 256)]
    at_row = lax.broadcasted_iota(jnp.int32, (256, 128), 0)
    at_col = lax.broadcasted_iota(jnp.int32, (256, 128), 1)
    pick = jnp.where(at_row == 64 * (at_col // 32) + at_col % 32, 1.0, 0.0)
    small_ref[40:41, 0:256] = small_ref[34:35, pl.ds(start, 256)]
    small_ref[40:41, 256:384] = dot(jnp.broadcast_to(chunk, (8, 256)), pick, ((1,), (0,)), precision=highest)[0:1]


def project(at, pieces, mine, theirs):
    return call(
        project_kernel,
        "project",
        [
            sds(512, 1024),
            sds(512, 512, dtype=f32),
            sds(512, 256),
            sds(16, 8, 128, dtype=f32),
            sds(48, 1024, dtype=f32),
            sds(1024, 512),
        ],
        at,
        *pieces,
        mine,
        theirs,
        flops=8 * 10**9,
        scratch=[pltpu.VMEM((8, 128), f32)],
    )


def document_of(places, at):
    found = jnp.zeros(places.shape, f32)
    for i in range(4):
        found = found + jnp.where(places >= at[3 + i], 1.0, 0.0)
    return jnp.where((places >= 0) & (places < 2048), found, -1.0)


def seen_bias(at, b):
    first = at[0] * 512 + 128 * b
    key = lax.broadcasted_iota(jnp.int32, (1152, 128), 0)
    query = lax.broadcasted_iota(jnp.int32, (1152, 128), 1)
    key_doc = document_of(first - HALF + key, at)
    query_doc = document_of(first + lax.broadcasted_iota(jnp.int32, (1, 128), 1), at)
    apart = key - query
    seen = (apart >= 0) & (apart < 2 * HALF) & (key_doc == query_doc)
    return jnp.where(seen, 0.0, -1e30)


def stacked_heads(tile, kh):
    lane = lax.broadcasted_iota(jnp.int32, (128, 128), 1)
    mine = (lane < 64) if kh == 0 else (lane >= 64)
    other = pltpu.roll(tile, 64, 1)
    first, second = (tile, other) if kh == 0 else (other, tile)
    return jnp.concatenate([jnp.where(mine, first, 0.0), jnp.where(mine, second, 0.0)], axis=0).astype(bf16)


def attend_kernel(at, raw, kv0, kv1, kv2, parts, small, cos, sin, p0, p1, p2, p3, attn, qb, kb, vb, lse, uq, uk, qinv, kinv, vt):
    d = at[0]
    for i in range(12):
        there = jnp.clip(d - 1 + i // 4, 0, 3)
        row = parts[4 * there][4 + i % 4 : 5 + i % 4]
        for s in range(1, 4):
            row = row + parts[4 * there + s][4 + i % 4 : 5 + i % 4]
        inverse = column(lax.rsqrt(row * (1.0 / 512) + epsilon))
        span = slice(128 * i, 128 * (i + 1))
        part = slice(128 * (i % 4), 128 * (i % 4 + 1))
        kv = (kv0, kv1, kv2)[i // 4]
        unit = kv[part, :128].astype(f32) * inverse
        key = unit * small[40:41, 256:384]
        uk[span, :] = unit
        kb[span, :] = (key * cos[span, :] + partner(key) * sin[span, :]).astype(bf16)
        value = kv[part, 128:]
        vb[span, :] = value
        vt[:, span] = value.T
        if i // 4 == 1:
            kinv[part, :] = inverse
            row = parts[4 * d][i % 4 : i % 4 + 1]
            for s in range(1, 4):
                row = row + parts[4 * d + s][i % 4 : i % 4 + 1]
            inverse = column(lax.rsqrt(row * (1.0 / 1024) + epsilon))
            qinv[part, :] = inverse
            for m in range(2):
                lanes = slice(128 * m, 128 * (m + 1))
                unit = raw[part, lanes] * inverse
                uq[part, lanes] = unit
                query = unit * small[40:41, lanes]
                qb[part, lanes] = (query * cos[span, :] + partner(query) * sin[span, :]).astype(bf16)
    for b in range(4):
        bias = seen_bias(at, b)
        bias = jnp.concatenate([bias, bias], axis=1)
        window = slice(128 * b, 128 * b + 1152)
        for kh in range(2):
            lanes = slice(128 * kh, 128 * (kh + 1))
            heads = stacked_heads(qb[128 * b : 128 * (b + 1), lanes].astype(f32), kh)
            scores = dot(kb[window, :], heads, ((1,), (1,))) * 0.125 + bias
            top = jnp.max(scores, axis=0, keepdims=True)
            weights = jnp.exp(scores - top)
            total = jnp.sum(weights, axis=0, keepdims=True)
            lse[2 * b + kh : 2 * b + kh + 1, :] = top + jnp.log(total)
            mixed = dot(vt[64 * kh : 64 * kh + 64, window], weights.astype(bf16), ((1,), (0,))) / total
            tile = jnp.concatenate([mixed[:, :128], mixed[:, 128:]], axis=0).T
            attn[b, :, lanes] = tile.astype(bf16)
    for k, ref in enumerate((p0, p1, p2, p3)):
        ref[...] = attn[lax.rem(at[1] + k, 4)]


def attend(at, raw, kvs, parts, small, cos, sin):
    return call(
        attend_kernel,
        "attend",
        [sds(128, 256)] * 4
        + [
            sds(4, 128, 256),
            sds(512, 256),
            sds(1536, 128),
            sds(1536, 128),
            sds(8, 256, dtype=f32),
            sds(512, 256, dtype=f32),
            sds(1536, 128, dtype=f32),
            sds(512, 128, dtype=f32),
            sds(512, 128, dtype=f32),
        ],
        at,
        raw,
        *kvs,
        parts,
        small,
        cos,
        sin,
        flops=15 * 10**9,
        scratch=[pltpu.VMEM((128, 1536), bf16)],
    )


def attend_back_kernel(
    at, g0, g1, g2, g3, qb, kb, vb, lse, uq, uk, cos, sin, base, wq, dkv_own, dkv_up, dkv_down, sums, kt, dk, dv, qgain, qrows, got
):
    for k, ref in enumerate((g0, g1, g2, g3)):
        got[lax.rem(at[1] - k + 4, 4)] = ref[...]
    for i in range(12):
        span = slice(128 * i, 128 * (i + 1))
        kt[:, span] = kb[span, :].T
    dk[...] = jnp.zeros_like(dk)
    dv[...] = jnp.zeros_like(dv)
    qgain[...] = jnp.zeros_like(qgain)
    for b in range(4):
        bias = seen_bias(at, b)
        bias = jnp.concatenate([bias, bias], axis=1)
        window = slice(128 * b, 128 * b + 1152)
        own = slice(128 * b, 128 * (b + 1))
        table = slice(HALF + 128 * b, HALF + 128 * (b + 1))
        total = jnp.zeros((128, 1), f32)
        for kh in range(2):
            lanes = slice(128 * kh, 128 * (kh + 1))
            query = qb[own, lanes].astype(f32)
            heads = stacked_heads(query, kh)
            grads = stacked_heads(got[b, :, lanes].astype(f32), kh)
            scores = dot(kb[window, :], heads, ((1,), (1,))) * 0.125 + bias
            probs = jnp.exp(scores - lse[2 * b + kh : 2 * b + kh + 1, :])
            prob_grad = dot(vb[window, :], grads, ((1,), (1,)))
            centre = jnp.sum(probs * prob_grad, axis=0, keepdims=True)
            score_grad = (probs * (prob_grad - centre)).astype(bf16)
            dv[window, :] += dot(probs.astype(bf16), grads, ((1,), (0,)))
            dk[window, :] += dot(score_grad, heads, ((1,), (0,))) * 0.125
            flat = dot(kt[64 * kh : 64 * kh + 64, window], score_grad, ((1,), (0,))) * 0.125
            dq = jnp.concatenate([flat[:, :128], flat[:, 128:]], axis=0).T.astype(bf16).astype(f32)
            total = total + jnp.sum(dq * query, axis=1, keepdims=True)
            turned = dq * cos[table, :] - partner(dq) * sin[table, :]
            wq[own, lanes] = turned
            qgain[0:1, lanes] += jnp.sum(turned * uq[own, lanes], axis=0, keepdims=True)
        qrows[b : b + 1, :] = jnp.broadcast_to(total, (128, 128)).T[0:1]
    kgain = jnp.zeros((1, 128), f32)
    krows = []
    for i in range(12):
        span = slice(128 * i, 128 * (i + 1))
        part = slice(128 * (i % 4), 128 * (i % 4 + 1))
        grad = dk[span, :]
        spot = jnp.sum(grad * kb[span, :].astype(f32), axis=1, keepdims=True)
        krows.append(jnp.broadcast_to(spot, (128, 128)).T[0:1])
        turned = grad * cos[span, :] - partner(grad) * sin[span, :]
        kgain = kgain + jnp.sum(turned * uk[span, :], axis=0, keepdims=True)
        target = (dkv_down, dkv_own, dkv_up)[i // 4]
        target[part, :128] = grad.astype(target.dtype)
        target[part, 128:] = dv[span, :].astype(target.dtype)
    lane = lax.broadcasted_iota(jnp.int32, (1, 128), 1)
    none = jnp.zeros((6, 128), f32)
    for there in range(4):
        here = jnp.where(at[0] == there, 1.0, 0.0)
        mine = jnp.where(at[1] == there, 1.0, 0.0)
        rows = [qrows[0:4, :] * here]
        for i in range(4):
            row = jnp.zeros((1, 128), f32)
            for part in range(3):
                row = row + krows[4 * part + i] * jnp.where(at[0] - 1 + part == there, 1.0, 0.0)
            rows.append(row)
        for s in range(4):
            q_tile = qgain[0:1, 128 * (s // 2) : 128 * (s // 2 + 1)]
            if s % 2:
                q_tile = pltpu.roll(q_tile, 64, 1)
            k_tile = pltpu.roll(kgain, (64 - 32 * s) % 128, 1)
            gains = jnp.where(lane < 64, q_tile, jnp.where(lane < 96, k_tile, 0.0)) * mine
            more = base[4 * there + s]
            sums[4 * there + s] = jnp.concatenate(rows + [gains, more[0:1], none, more[8:24]], axis=0).astype(bf16)


def attend_back(at, gots, qb, kb, vb, lse, uq, uk, cos, sin, base):
    return call(
        attend_back_kernel,
        "attend_back",
        [
            sds(512, 256, dtype=f32),
            sds(512, 256, dtype=f32),
            sds(512, 256),
            sds(512, 256),
            sds(16, 32, 128),
        ],
        at,
        *gots,
        qb,
        kb,
        vb,
        lse,
        uq,
        uk,
        cos,
        sin,
        base,
        flops=30 * 10**9,
        scratch=[
            pltpu.VMEM((128, 1536), bf16),
            pltpu.VMEM((1536, 128), f32),
            pltpu.VMEM((1536, 128), f32),
            pltpu.VMEM((8, 256), f32),
            pltpu.VMEM((8, 128), f32),
            pltpu.VMEM((4, 128, 512), bf16),
        ],
    )


def route_kernel(at, *refs):
    place_ref, used_ref, gs_ref = refs[8:]
    ids = lax.broadcasted_iota(jnp.int32, (32, 128), 0) + 4 * at[2]
    ids = jnp.where(ids >= 32, ids - 32, ids).astype(f32)
    slot = lax.broadcasted_iota(jnp.int32, (SLOTS, 128), 0).astype(f32)
    for j, ref in enumerate(refs[:8]):
        meta = ref[:, 1024:].astype(f32)
        turned = meta.T
        used = turned[0:1] == ids
        for k in range(1, TOPK):
            used = used | (turned[k : k + 1] == ids)
        used_ref[j] = jnp.where(used, 1.0, 0.0)
        earlier = jnp.where(meta[:, 8:9] < turned[8:9], 1.0, 0.0).astype(bf16)
        before = dot(jnp.where(used, 1.0, 0.0).astype(bf16), earlier, ((1,), (0,)))
        spot = jnp.where(used & (before < CAP), before, 1000.0)
        chosen = jnp.concatenate([jnp.where(slot == spot[l : l + 1], 1.0, 0.0) for l in range(4)], axis=0).astype(bf16)
        place_ref[j] = chosen
        ups = dot(chosen, ref[:, :1024], ((1,), (0,))).astype(bf16)
        for l in range(4):
            gs_ref[l, SLOTS * j : SLOTS * (j + 1), :] = ups[SLOTS * l : SLOTS * (l + 1)]


def route(at, cots):
    return call(
        route_kernel,
        "route",
        [sds(8, 4 * SLOTS, 128), sds(8, 32, 128, dtype=f32), sds(4, 8 * SLOTS, 1024)],
        at,
        *cots,
        flops=0,
        moved=0,
    )


def expert_step(where_ref, *refs):
    n2_refs = refs[0:8]
    place, used_ref, gs, small, w_ref = refs[8:13]
    dn_refs = tuple(ref.at[i] for ref in refs[13:15] for i in range(4))
    out_refs = tuple(ref.at[i] for ref in refs[15:17] for i in range(4))
    grads_ref = refs[17]
    xs, gate, ys, dxs, dgs = refs[18:23]
    step = pl.program_id(0)

    @pl.when(step == 0)
    def _():
        router_t = small[0:32, :].astype(bf16)
        back = lax.rem(32 - 4 * where_ref[0], 32)
        for j in range(8):
            n2 = n2_refs[j][...]
            used = used_ref[j] > 0.5
            logits = pltpu.roll(dot(router_t, n2, ((1,), (1,))), back, 0)
            masked = jnp.where(used, logits, -1e30)
            grown = jnp.where(used, jnp.exp(masked - jnp.max(masked, axis=0, keepdims=True)), 0.0)
            gates = grown / jnp.sum(grown, axis=0, keepdims=True)
            chosen = place[j]
            rows = dot(chosen, n2, ((1,), (0,))).astype(bf16)
            for l in range(4):
                span = slice(SLOTS * j, SLOTS * (j + 1))
                hit = chosen[SLOTS * l : SLOTS * (l + 1)].astype(f32)
                share = jnp.sum(hit * gates[l : l + 1], axis=1, keepdims=True)
                gate[l, span, :] = jnp.broadcast_to(share, (SLOTS, 128))
                xs[l, span, :] = rows[SLOTS * l : SLOTS * (l + 1)]

    w_in = w_ref[:, 0, :64, :].reshape(1024, 1024)
    w_out = w_ref[:, 0, 64:, :].reshape(512, 1024)
    x = xs[step]
    both = dot(x, w_in, ((1,), (0,)))
    gate_part, up_part = both[:, :512], both[:, 512:]
    sig = jax.nn.sigmoid(gate_part)
    silu = gate_part * sig
    hidden = (silu * up_part).astype(bf16)
    g = gs[0].astype(f32)
    share = gate[step][:, 0:1]
    dy = (g * share).astype(bf16)
    dh = dot(dy, w_out, ((1,), (1,)))
    dgu = jnp.concatenate(
        [dh * up_part * (sig * (1.0 + gate_part * (1.0 - sig))), dh * silu], axis=1
    ).astype(bf16)
    dxs[step] = dot(dgu, w_in, ((1,), (1,))).astype(bf16)
    y = dot(hidden, w_out, ((1,), (0,))).astype(bf16).astype(f32)
    ys[step] = (y * share).astype(bf16)
    lane = lax.broadcasted_iota(jnp.int32, (8 * SLOTS, 128), 1)
    dgate = jnp.sum(g * y, axis=1, keepdims=True)
    dgs[step] = jnp.where(lane == 4 * where_ref[0] + step, dgate, 0.0).astype(bf16)
    grads_ref[:, 0, :64, :] = dot(x, dgu, ((0,), (0,))).astype(bf16).reshape(16, 64, 1024)
    grads_ref[:, 0, 64:, :] = dot(hidden, dy, ((0,), (0,))).astype(bf16).reshape(16, 32, 1024)

    @pl.when(step == 3)
    def _():
        for j in range(8):
            chosen = place[j]
            span = slice(SLOTS * j, SLOTS * (j + 1))
            for source, target, lo, hi in ((dxs, dn_refs[j], 0, 1024), (dgs, dn_refs[j], 1024, 1152), (ys, out_refs[j], 0, 1024)):
                stacked = jnp.concatenate([source[l, span, :] for l in range(4)], axis=0)
                target[:, lo:hi] = dot(chosen, stacked, ((0,), (0,))).astype(bf16)


def experts(e_index, n2s, place, used, gs, small, weights):
    whole = lambda *s: pl.BlockSpec(s, lambda i, *_: (0,) * len(s))
    each = lambda cols: pl.BlockSpec((1, 8 * SLOTS, cols), lambda i, *_: (i, 0, 0))
    owned = pl.BlockSpec((16, 1, 96, 1024), lambda i, *_: (0, i, 0, 0))
    shape = lambda *s: jax.ShapeDtypeStruct(s, bf16)
    return pl.pallas_call(
        expert_step,
        grid_spec=pltpu.PrefetchScalarGridSpec(
            num_scalar_prefetch=1,
            grid=(4,),
            in_specs=[whole(128, 1024)] * 8
            + [
                whole(8, 4 * SLOTS, 128),
                whole(8, 32, 128),
                each(1024),
                whole(48, 1024),
                owned,
            ],
            out_specs=[whole(4, 128, 1152)] * 2 + [whole(4, 128, 1024)] * 2 + [owned],
            scratch_shapes=[
                pltpu.VMEM((4, 8 * SLOTS, 1024), bf16),
                pltpu.VMEM((4, 8 * SLOTS, 128), f32),
                pltpu.VMEM((4, 8 * SLOTS, 1024), bf16),
                pltpu.VMEM((4, 8 * SLOTS, 1024), bf16),
                pltpu.VMEM((4, 8 * SLOTS, 128), bf16),
            ],
        ),
        out_shape=[shape(4, 128, 1152)] * 2
        + [shape(4, 128, 1024)] * 2
        + [shape(16, 4, 96, 1024)],
        compiler_params=pltpu.CompilerParams(vmem_limit_bytes=VMEM_BYTES),
        cost_estimate=pl.CostEstimate(flops=28 * 10**9, bytes_accessed=40 * 10**6, transcendentals=10**6),
        name="experts",
    )(e_index, *n2s, place, used, gs, small, weights)


def split(x):
    high = x.astype(bf16)
    return high, (x - high.astype(f32)).astype(bf16)


def o_pieces(at, refs):
    core = lax.rem(at[2], 2)
    for k, ref in enumerate(refs):
        chip = lax.rem(at[2] // 2 - k + 4, 4)
        yield block(2 * chip + core), ref[:, :128]
        yield block(2 * chip + 1 - core), ref[:, 128:]


def quarter(index):
    return pl.ds(pl.multiple_of(256 * index, 256), 256)


def middle_kernel(at, tok, a0, a1, a2, a3, o0, o1, o2, o3, small, middle_ref, low_ref, inverse_ref, rows_ref):
    for k, ref in enumerate((a0, a1, a2, a3)):
        rows_ref[:, quarter(lax.rem(at[1] - k + 4, 4))] = ref[...]
    rows = rows_ref[...]
    for lanes, piece in o_pieces(at, (o0, o1, o2, o3)):
        middle_ref[:, lanes] = tok[:, lanes].astype(f32) + dot(rows, piece, ((1,), (0,)))
    total = middle_ref[...]
    inverse = lax.rsqrt(jnp.mean(total * total, axis=1, keepdims=True) + epsilon)
    low_ref[...] = (total * inverse * small[33:34]).astype(bf16)
    inverse_ref[...] = jnp.broadcast_to(inverse, (128, 128))


def make_middle(at, tok, attns, parts, small):
    return call(
        middle_kernel,
        "middle",
        [sds(128, 1024, dtype=f32), sds(128, 1024), sds(128, 128, dtype=f32)],
        at,
        tok,
        *attns,
        *parts,
        small,
        flops=6 * 10**9,
        scratch=[pltpu.VMEM((128, 1024), bf16)],
    )


def middle_back_kernel(
    at, p0a, p0b, p1, p2, p3, middle, inverse_ref, low, cot, small, o0, o1, o2, o3, grad_ref, s0, s1, s2, s3, sums_ref, branch_ref, back_ref
):
    total = p0a[0].astype(f32) + p0b[0].astype(f32) + p1[...].astype(f32) + p2[...].astype(f32) + p3[...].astype(f32)
    dgates = total[:, 1024:1056]
    router_t = small[0:32].astype(bf16)
    logits = dot(low[...], router_t, ((1,), (1,)))
    ids = lax.broadcasted_iota(jnp.int32, (128, 32), 1).astype(f32)
    named = cot[:, 1024:].astype(f32)
    used = named[:, 0:1] == ids
    for k in range(1, TOPK):
        used = used | (named[:, k : k + 1] == ids)
    masked = jnp.where(used, logits, -1e30)
    grown = jnp.where(used, jnp.exp(masked - jnp.max(masked, axis=1, keepdims=True)), 0.0)
    gates = grown / jnp.sum(grown, axis=1, keepdims=True)
    logit_grad = gates * (dgates - jnp.sum(gates * dgates, axis=1, keepdims=True))
    high, rest = split(logit_grad)
    dn2 = total[:, :1024] + dot(high, router_t, ((1,), (0,))) + dot(rest, router_t, ((1,), (0,)))
    inverse = inverse_ref[:, 0:1]
    unit = middle[...] * inverse
    scaled = dn2 * small[33:34]
    grad = cot[:, :1024].astype(f32) + inverse * (scaled - unit * jnp.mean(scaled * unit, axis=1, keepdims=True))
    grad_ref[...] = grad
    branch = grad.astype(bf16)
    branch_ref[...] = branch
    back = jnp.zeros((128, 1024), f32)
    for lanes, piece in o_pieces(at, (o0, o1, o2, o3)):
        back = back + dot(branch_ref[:, lanes], piece, ((1,), (1,)))
    back_ref[...] = back.astype(bf16)
    for k, ref in enumerate((s0, s1, s2, s3)):
        lanes = quarter(lax.rem(at[1] + k, 4))
        ref[:, 0:256] = back_ref[:, lanes]
        ref[:, 256:512] = branch_ref[:, lanes]
    routers = dot(high, low[...], ((0,), (0,))) + dot(rest, low[...], ((0,), (0,)))
    second = jnp.sum(dn2 * unit, axis=0, keepdims=True)
    lane = lax.broadcasted_iota(jnp.int32, (16, 128), 1)
    for i in range(16):
        lanes = slice(128 * (i // 2), 128 * (i // 2 + 1))
        upper, lower, row = routers[0:16, lanes], routers[16:32, lanes], second[:, lanes]
        if i % 2 == 0:
            tile = jnp.where(lane < 64, upper, pltpu.roll(lower, 64, 1))
        else:
            tile = jnp.where(lane < 64, pltpu.roll(upper, 64, 1), lower)
            row = pltpu.roll(row, 64, 1)
        sums_ref[i] = jnp.concatenate([row, jnp.zeros((7, 128), f32), tile], axis=0)


def middle_back(at, pieces, middle, inverse, low, cot, small, parts):
    return call(
        middle_back_kernel,
        "middle_back",
        [sds(128, 1024, dtype=f32)] + [sds(128, 512)] * 4 + [sds(16, 24, 128, dtype=f32)],
        at,
        *pieces,
        middle,
        inverse,
        low,
        cot,
        small,
        *parts,
        flops=12 * 10**9,
        scratch=[pltpu.VMEM((128, 1024), bf16)] * 2,
    )


def out_grad_kernel(at, a0, a1, a2, a3, g0, g1, g2, g3, out_ref, cols):
    for k, ref in enumerate((g0, g1, g2, g3)):
        cols[block(lax.rem(at[1] - k + 4, 4)), :] = ref[:, 256:512]
    for k, part in enumerate((a0, a1, a2, a3)):
        rows = jnp.concatenate([part[i] for i in range(4)], axis=0)
        out_ref[quarter(lax.rem(at[1] - k + 4, 4)), :] = dot(rows, cols[...], ((0,), (0,))).astype(bf16)


def out_grads(at, attns, gots):
    scratch = [pltpu.VMEM((512, 256), bf16)]
    return call(out_grad_kernel, "out_grads", sds(1024, 256), at, *attns, *gots, flops=0, moved=0, scratch=scratch)


def finish_kernel(
    at, wq, own, up, down, sums, uq, uk, qinv, kinv, small, cos, sin, w_ref,
    dn0, dn1, dn2, dn3, keep_ref, send_ref, sums_ref, dqkv,
):
    got = sums[0].astype(f32)
    for i in range(1, 16):
        got = got + sums[i].astype(f32)
    sums_ref[...] = got
    for i in range(4):
        part = slice(128 * i, 128 * (i + 1))
        q_mean = column(got[i : i + 1]) * (1.0 / 1024)
        for m in range(2):
            lanes = slice(128 * m, 128 * (m + 1))
            grad = wq[part, lanes] * small[40:41, lanes] - uq[part, lanes] * q_mean
            dqkv[part, lanes] = (qinv[part, :] * grad).astype(bf16)
        total = own[part, :] + up[part, :].astype(f32) + down[part, :].astype(f32)
        dk = total[:, :128].astype(bf16).astype(f32)
        turned = dk * cos[part, :] - partner(dk) * sin[part, :]
        k_mean = column(got[4 + i : 5 + i]) * (1.0 / 512)
        grad = turned * small[40:41, 256:384] - uk[part, :] * k_mean
        dqkv[part, 256:384] = (kinv[part, :] * grad).astype(bf16)
        dqkv[part, 384:512] = total[:, 128:].astype(bf16)
    w = w_ref[...]
    for k, ref in enumerate((dn0, dn1, dn2, dn3)):
        ref[...] = dot(dqkv[block(lax.rem(at[1] + k, 4)), :], w, ((1,), (1,))).astype(bf16)
    even = lax.rem(at[2], 2) == 0
    left = dqkv[:, :384]
    right = jnp.concatenate([dqkv[:, 384:], jnp.zeros((512, 256), bf16)], axis=1)
    keep_ref[...] = jnp.where(even, left, right)
    send_ref[...] = jnp.where(even, right, left)


def finish(at, wq, own, up, down, sums, uq, uk, qinv, kinv, small, cos, sin, w_cols):
    return call(
        finish_kernel,
        "finish",
        [sds(128, 1024)] * 4 + [sds(512, 384)] * 2 + [sds(sums.shape[1], 128, dtype=f32)],
        at, wq, own, up, down, sums, uq, uk, qinv, kinv, small, cos, sin, w_cols,
        middle=(7, 11, 12),
        flops=10 * 10**9,
        scratch=[pltpu.VMEM((512, 512), bf16)],
    )


def weight_kernel(at, n1, n1_theirs, keep, got, o_part, o_theirs, r0, r1, r2, r3, grads):
    total = dot(n1[...], keep[...], ((1,), (0,))) + dot(n1_theirs[...], got[...], ((1,), (0,)))
    odd = lax.rem(at[2], 2).astype(f32)
    outs = (o_part[...].astype(f32) + o_theirs[...].astype(f32)) * odd
    grads[:, :, :128] = total[:, :128].astype(bf16).reshape(16, 64, 128)
    grads[:, :, 128:] = (total[:, 128:] + outs).astype(bf16).reshape(16, 64, 256)
    for k, ref in enumerate((r0, r1, r2, r3)):
        ref[...] = grads[:, pl.ds(pl.multiple_of(16 * lax.rem(at[2] // 2 + k, 4), 16), 16), :]


def weight_grads(at, *args):
    return call(
        weight_kernel,
        "weight_grads",
        [sds(16, 16, 384)] * 4,
        at,
        *args,
        flops=8 * 10**9,
        scratch=[pltpu.VMEM((16, 64, 384), bf16)],
    )


def input_kernel(at, p0, p1, p2, p3, tok, grad_ref, small, out_ref):
    dn1 = p0[...].astype(f32) + p1[...].astype(f32) + p2[...].astype(f32) + p3[...].astype(f32)
    x = tok[...].astype(f32)
    inverse = lax.rsqrt(jnp.mean(x * x, axis=1, keepdims=True) + epsilon)
    unit = x * inverse
    scaled = dn1 * small[32:33]
    out_ref[...] = grad_ref[...] + inverse * (scaled - unit * jnp.mean(scaled * unit, axis=1, keepdims=True))


def input_back(at, pieces, tok, grad, small):
    return call(input_kernel, "input_back", sds(128, 1024, dtype=f32), at, *pieces, tok, grad, small, flops=0, moved=0)


def pack_kernel(at, w_ref, o_ref, router_ref, gain_ref, key_ref, out_ref):
    even = lax.rem(at[2], 2) == 0
    piece = o_ref[:, block(at[2])]
    key = jnp.concatenate([key_ref[...].astype(f32), jnp.zeros((1, 32), f32)], axis=1)
    extra = jnp.concatenate(
        [router_ref[...].astype(f32), gain_ref[...].astype(f32), key, jnp.zeros((28, 64), f32)], axis=0
    )
    extra = jnp.concatenate([extra, jnp.zeros((64, 64), f32)], axis=1).astype(bf16)
    for s in range(4):
        queries = w_ref[:, 256 * s : 256 * (s + 1)]
        keys = w_ref[:, 1024 + 128 * s : 1024 + 128 * (s + 1)]
        values = w_ref[:, 1536 + 128 * s : 1536 + 128 * (s + 1)]
        half = jnp.where(even, queries, jnp.concatenate([keys, values], axis=1))
        for d in range(4):
            out_ref[4 * d + s, :, 0:256] = half
            out_ref[4 * d + s, :, 256:384] = extra
            out_ref[4 * d + s, :, 384:512] = piece


def pack(at, *args):
    return call(pack_kernel, "pack", sds(16, 64, 512), at, *args, flops=10**9)


def turn_kernel(at, x_ref, out_ref):
    out_ref[...] = x_ref[...].T


def turned(at, x):
    return call(turn_kernel, "turned", sds(x.shape[1], x.shape[0]), at, x, flops=0, moved=0)


def last_kernel(at, *refs):
    pieces, (w_ref, gain_ref, qkv_ref, o_ref, gains_ref, key_ref, router_ref) = refs[:4], refs[4:]
    even = lax.rem(at[2], 2) == 0
    sums = jnp.zeros((16, 256), f32)
    for k in range(4):
        rows = pl.ds(pl.multiple_of(16 * lax.rem(at[2] // 2 - k + 4, 4), 16), 16)
        mine, theirs = pieces[k][:, :1792].astype(f32), pieces[k][:, 1792:].astype(f32)
        sums = sums + mine[:, 1536:] + theirs[:, 1536:]
        first, later = jnp.where(even, mine, theirs), jnp.where(even, theirs, mine)
        for s in range(4):
            lanes = 384 * s
            qkv_ref[rows, 256 * s : 256 * (s + 1)] = first[:, lanes : lanes + 256]
            qkv_ref[rows, 1024 + 128 * s : 1024 + 128 * (s + 1)] = first[:, lanes + 256 : lanes + 384]
            qkv_ref[rows, 1536 + 128 * s : 1536 + 128 * (s + 1)] = later[:, lanes : lanes + 128]
            o_ref[rows, 256 * s : 256 * (s + 1)] = later[:, lanes + 128 : lanes + 384]
    first_gain = row_sums(qkv_ref[...] * w_ref[...].astype(f32)) / gain_ref[0:1, :].astype(f32)
    gains_ref[0:1, :] = first_gain
    gains_ref[1:2, :] = sums[9:10, 128:192]
    gains_ref[2:3, :] = sums[8:9, 128:192]
    key_ref[...] = sums[8:9, 192:224]
    router_ref[...] = jnp.concatenate([sums[:, :64], sums[:, 64:128]], axis=0)


def last(at, pieces, w_qkv, norm_gains):
    return call(
        last_kernel,
        "last",
        [
            sds(64, 2048, dtype=f32),
            sds(64, 1024, dtype=f32),
            sds(3, 64, dtype=f32),
            sds(1, 32, dtype=f32),
            sds(32, 64, dtype=f32),
        ],
        at, *pieces, w_qkv, norm_gains,
    )


def chip_kernel(at, r0, r1, r2, r3, out_ref):
    total = r0[...].astype(f32) + r1[...].astype(f32) + r2[...].astype(f32) + r3[...].astype(f32)
    out_ref[...] = total.astype(bf16)


def chip_sum(at, pieces):
    return call(chip_kernel, "chip_sum", sds(*pieces[0].shape), at, *pieces, flops=0, moved=0)


def rows_kernel(at, got, sums, out_ref):
    for s in range(4):
        total = got[s].astype(f32)
        for d in range(1, 4):
            total = total + got[4 * d + s].astype(f32)
        out_ref[:, 384 * s : 384 * (s + 1)] = total.astype(bf16)
    out_ref[:, 1536:1664] = sums[16:32, :].astype(bf16)
    out_ref[:, 1664:1792] = sums[0:16, :].astype(bf16)


def sum_rows(at, got, sums):
    return call(rows_kernel, "sum_rows", sds(16, 1792), at, got, sums, flops=0, moved=0)


def join_kernel(at, mine, theirs, *outs):
    skipped = 4 - len(outs)
    for k, ref in enumerate(outs):
        ref[...] = (mine[k + skipped].astype(f32) + theirs[k + skipped].astype(f32)).astype(bf16)


def join(at, mine, theirs, count=3):
    return call(join_kernel, "join", [sds(*mine.shape[1:])] * count, at, mine, theirs, flops=0, moved=0)


def swap(array, axis):
    return lax.all_to_all(array, axis, split_axis=0, concat_axis=0, tiled=True)


def spread(array, axis, ways):
    return swap(jnp.broadcast_to(array[None], (ways,) + array.shape), axis)


def along_seq(array, k):
    return lax.ppermute(array, "seq", [(i, (i + k) % 4) for i in range(4)])


def along_dp(array, k):
    return lax.ppermute(array, "dp", [(i, (i + k) % 4) for i in range(4)])


def along_x(array, k):
    return lax.ppermute(array, "expert", [(i, (i + 2 * k) % 8) for i in range(8)])


def other_core(array):
    return lax.ppermute(array, "expert", [(i, i ^ 1) for i in range(8)])


def gather_x(array):
    return [array] + [along_x(array, k) for k in range(1, 4)]


def return_x(mine, joined, sums):
    return [mine, joined] + [along_x(sums[k - 1], -k) for k in range(1, 4)]


def after(values, *others):
    return lax.optimization_barrier((values, others))[0]


def shards(tokens, cotangent, doc_lengths, routes, route_rank, w_qkv, w_o, norm_gains, key_gain, w_router, w_in, w_out):
    d_index = lax.axis_index("dp")
    s_index = lax.axis_index("seq")
    e_index = lax.axis_index("expert")
    lengths = doc_lengths[0]
    tok = tokens[0]
    place = jnp.stack([d_index, s_index, e_index]).astype(jnp.int32)
    ends = [lengths[0]]
    for i in range(1, 4):
        ends.append(ends[-1] + lengths[i])
    at = jnp.concatenate([place, jnp.stack(ends)])
    w_send = pack(at, w_qkv, w_o, w_router.T, norm_gains, key_gain[None])
    w_mine = swap(w_send, GROUP)
    tok_pieces = [tok] + [along_seq(tok, k) for k in range(1, 4)]
    w_in, w_out = after((w_in, w_out), w_send)
    moe_shard = jnp.concatenate([w_in.reshape(4, 64, 1024), w_out], axis=1)
    cot = jnp.concatenate(
        [cotangent[0], routes[0].astype(bf16), route_rank[0].astype(bf16)[:, None], jnp.zeros((128, 119), bf16)], axis=1
    )
    cots = gather_x(cot)
    places = d_index * 512 - HALF + jnp.arange(1536, dtype=jnp.int32)
    starts = [jnp.zeros((), jnp.int32)] + ends
    begins = jnp.zeros((1536,), jnp.int32)
    for start in starts:
        begins = jnp.maximum(begins, jnp.where(places >= start, start, 0))
    lane = jnp.arange(128, dtype=jnp.int32)
    frequency = 10000.0 ** (-(lane % 32).astype(f32) / 32)
    angles = (places - begins).astype(f32)[:, None] * frequency[None, :]
    cos = jnp.cos(angles)
    sin = jnp.sin(angles) * jnp.where(lane % 64 < 32, -1.0, 1.0)[None, :]

    moe_shard = after(moe_shard, tok_pieces)
    moe_all = lax.all_gather(moe_shard, GROUP, axis=0, tiled=False)
    w_mine, cots = after((w_mine, cots), cos, sin, tok_pieces)
    cots = cots + [other_core(c) for c in cots]
    w_theirs = after(other_core(w_mine), cots)
    n1, raw, kv, parts, small, w_cols = project(at, tok_pieces, w_mine, w_theirs)
    up = [(i, i + 1) for i in range(3)]
    down = [(i + 1, i) for i in range(3)]
    kv_before = lax.ppermute(kv, "dp", up)
    kv_after = lax.ppermute(kv, "dp", down)
    parts = swap(parts, GROUP)
    o_pair = jnp.concatenate([w_mine[:, :, 384:], w_theirs[:, :, 384:]], axis=2).reshape(1024, 256)
    o_parts = gather_x(after(o_pair, kv_before, kv_after))
    *attn_send, attn, qb, kb, vb, lse, uq, uk, qinv, kinv = attend(at, raw, [kv_before, kv, kv_after], parts, small, cos, sin)
    attn_got = [attn_send[0]] + [along_seq(attn_send[k], k) for k in range(1, 4)]
    middle, n2, inverse = make_middle(at, tok, attn_got, o_parts, small)
    routed = route(place, after(cots, n2))
    n2s = after(gather_x(n2), routed)
    n2s = n2s + [other_core(n) for n in n2s]
    made = experts(e_index[None].astype(jnp.int32), n2s, *routed, small, moe_all)
    attns = [attn] + [along_seq(attn, k) for k in range(1, 4)]
    made = after(made, attns)
    joined = other_core(made[1])
    sums = join(place, made[0], joined)
    n1_turned = turned(place, after(n1, sums))
    out_joined = other_core(after(made[3], sums))
    out_sums = join(place, made[2], out_joined)
    dn_pieces = after(return_x(made[0], joined, sums), n1_turned, out_sums)
    moe_own = lax.psum_scatter(made[4].reshape(16 * 384, 1024), GROUP, scatter_dimension=0, tiled=True)
    moe_own = moe_own.reshape(4, 96, 1024).astype(f32)
    in_own = moe_own[:, :64].reshape(4, 64, 2, 512)
    down_own = moe_own[:, 64:]
    middle_grad, *grad_send, base = middle_back(at, dn_pieces, middle, inverse, n2, cot, small, o_parts)
    grad_got = [grad_send[0]] + [along_seq(grad_send[k], k) for k in range(1, 4)]
    n1_theirs = other_core(after(n1_turned, grad_send))
    out_pieces = [along_x(out_sums[k - 1], -k) for k in range(1, 4)]
    wq, dkv_own, dkv_up, dkv_down, sums = attend_back(at, grad_got, qb, kb, vb, lse, uq, uk, cos, sin, base)
    from_before = lax.ppermute(dkv_up, "dp", up)
    from_after = lax.ppermute(dkv_down, "dp", down)
    sums = swap(after(sums, out_pieces), GROUP)
    o_part = out_grads(at, attns, after(grad_got, wq))
    output = middle + made[2][0].astype(f32) + out_joined[0].astype(f32)
    for piece in out_pieces:
        output = output + piece.astype(f32)
    output = output.astype(bf16)
    o_theirs = other_core(o_part)
    done = finish(
        at, wq, dkv_own, from_before, from_after, sums, uq, uk, qinv, kinv, small, cos, sin, w_cols
    )
    dn1_pieces = [done[0]] + [along_seq(done[k], k) for k in range(1, 4)]
    keep, send, summed = done[4:]
    parts = weight_grads(place, after(n1_turned, output), n1_theirs, keep, other_core(send), o_part, o_theirs)
    halves = chip_sum(place, [parts[0]] + [along_x(parts[k], k) for k in range(1, 4)])
    halves = swap(halves, GROUP)
    input_grad = input_back(at, dn1_pieces, tok, middle_grad, small)
    own = sum_rows(place, after(halves, in_own, down_own, input_grad), summed)
    pieces = gather_x(jnp.concatenate([own, other_core(own)], axis=1))
    qkv_own, o_own, gains_own, key_own, router_own = last(place, pieces, w_qkv, norm_gains)
    return (output[None], input_grad[None], qkv_own, o_own, gains_own, key_own[0], router_own.T, in_own, down_own)


def solution(mesh):
    both = P("expert", GROUP, None)
    rows = P(GROUP, None)
    return jax.shard_map(
        shards,
        mesh=mesh,
        in_specs=(
            both,
            both,
            P("expert", None),
            both,
            P("expert", GROUP),
            rows,
            rows,
            P(None, GROUP),
            P(GROUP),
            rows,
            P("expert", GROUP, None, None),
            P("expert", GROUP, None),
        ),
        out_specs=(
            both,
            both,
            rows,
            rows,
            P(None, GROUP),
            P(GROUP),
            rows,
            P("expert", GROUP, None, None),
            P("expert", GROUP, None),
        ),
        check_vma=False,
    )
```

```python
import jax
import jax.numpy as jnp
from jax import lax
from jax.experimental import pallas as pl
from jax.experimental.pallas import tpu as pltpu
from jax.sharding import PartitionSpec as P

HEADS = 16
KV_HEADS = 8
HEAD_DIM = 64
TOPK = 8
HALF = 512
CAP = 40
PAIR = 2 * CAP
ROWS = 8 * CAP
VMEM_BYTES = 64 * 1024 * 1024

GROUP = ("dp", "seq")
ALL = ("dp", "seq", "expert")
epsilon = 1e-05
highest = lax.Precision.HIGHEST
bf16 = jnp.bfloat16
f32 = jnp.float32


def dot(a, b, dims, **kw):
    return lax.dot_general(a, b, ((dims[0], dims[1]), ((), ())), preferred_element_type=f32, **kw)


def call(kernel, name, out_shape, *args, flops=10**8, scratch=(), moved=10**6, middle=()):
    whole = lambda a: pl.BlockSpec(a.shape, lambda _: (0,) * len(a.shape))
    specs = [pl.BlockSpec(memory_space=pltpu.SMEM)] + [whole(a) for a in args[1:]]
    for i in middle:
        specs[i] = pl.BlockSpec((512, 128), lambda _: (1, 0))
    return pl.pallas_call(
        kernel,
        grid=(1,),
        in_specs=specs,
        out_specs=jax.tree.map(whole, out_shape),
        out_shape=out_shape,
        scratch_shapes=list(scratch),
        compiler_params=pltpu.CompilerParams(vmem_limit_bytes=VMEM_BYTES),
        cost_estimate=pl.CostEstimate(flops=flops, bytes_accessed=moved, transcendentals=0),
        name=name,
    )(*args)


def sds(*shape, dtype=bf16):
    return jax.ShapeDtypeStruct(shape, dtype)


def block(index):
    return pl.ds(pl.multiple_of(index * 128, 128), 128)


def column(row):
    return jnp.broadcast_to(row, (128, 128)).T


def partner(x):
    lane = lax.broadcasted_iota(jnp.int32, x.shape, 1)
    return jnp.where(lane % 64 < 32, pltpu.roll(x, 96, 1), pltpu.roll(x, 32, 1))


def row_sums(x):
    ones = jnp.ones((8, x.shape[1]), f32)
    return dot(ones, x, ((1,), (1,)), precision=highest)[0:1]


def project_kernel(at, t0, t1, t2, t3, mine, theirs, n1_ref, raw_ref, kv_ref, parts_ref, small_ref, w_ref, o_ref, rows):
    s = at[1]
    even = lax.rem(at[2], 2) == 0
    here, there = mine[:, :, :256].reshape(1024, 256), theirs[:, :, :256].reshape(1024, 256)
    w_ref[:, :256] = jnp.where(even, here, there)
    w_ref[:, 256:] = jnp.where(even, there, here)
    o_ref[:, :128] = mine[:, :, 384:].reshape(1024, 128)
    o_ref[:, 128:] = theirs[:, :, 384:].reshape(1024, 128)
    w = w_ref[...]
    lane = lax.broadcasted_iota(jnp.int32, (48, 128), 1)
    for i in range(8):
        low, high = mine[2 * i, :48, 256:384].astype(f32), mine[2 * i + 1, :48, 256:384].astype(f32)
        small_ref[:, 128 * i : 128 * (i + 1)] = jnp.where(lane < 64, low, pltpu.roll(high, 64, 1))
    gain = small_ref[32:33, :]
    for ds, t in enumerate((t0, t1, t2, t3)):
        x = t[...].astype(f32)
        low = (x * lax.rsqrt(jnp.mean(x * x, axis=1, keepdims=True) + epsilon) * gain).astype(bf16)
        turned = low.astype(f32).T.astype(bf16)
        raw = dot(low, w, ((1,), (0,)))
        place = lax.rem(s - ds + 4, 4)
        n1_ref[:, block(place)] = turned
        raw_ref[block(place), :] = raw
        kv_ref[block(place), :] = raw[:, 256:].astype(bf16)
        rows[pl.ds(place, 1), :] = row_sums(raw[:, :256] * raw[:, :256])
        rows[pl.ds(place + 4, 1), :] = row_sums(raw[:, 256:384] * raw[:, 256:384])
    parts_ref[...] = jnp.broadcast_to(rows[...][None], (16, 8, 128))
    start = pl.multiple_of(s * 256, 256)
    chunk = small_ref[35:36, pl.ds(start, 256)]
    at_row = lax.broadcasted_iota(jnp.int32, (256, 128), 0)
    at_col = lax.broadcasted_iota(jnp.int32, (256, 128), 1)
    pick = jnp.where(at_row == 64 * (at_col // 32) + at_col % 32, 1.0, 0.0)
    small_ref[40:41, 0:256] = small_ref[34:35, pl.ds(start, 256)]
    small_ref[40:41, 256:384] = dot(jnp.broadcast_to(chunk, (8, 256)), pick, ((1,), (0,)), precision=highest)[0:1]


def project(at, pieces, mine, theirs):
    return call(
        project_kernel,
        "project",
        [
            sds(1024, 512),
            sds(512, 512, dtype=f32),
            sds(512, 256),
            sds(16, 8, 128, dtype=f32),
            sds(48, 1024, dtype=f32),
            sds(1024, 512),
            sds(1024, 256),
        ],
        at,
        *pieces,
        mine,
        theirs,
        flops=8 * 10**9,
        scratch=[pltpu.VMEM((8, 128), f32)],
    )


def document_of(places, at):
    found = jnp.zeros(places.shape, f32)
    for i in range(4):
        found = found + jnp.where(places >= at[3 + i], 1.0, 0.0)
    return jnp.where((places >= 0) & (places < 2048), found, -1.0)


def mark_documents(at, docs):
    docs[...] = document_of(at[0] * 512 - HALF + lax.broadcasted_iota(jnp.int32, (1536, 128), 0), at)
    apart = lax.broadcasted_iota(jnp.int32, (1152, 128), 0) - lax.broadcasted_iota(jnp.int32, (1152, 128), 1)
    return jnp.where((apart >= 0) & (apart < 2 * HALF), 0.0, -1e30)


def seen_bias(at, b, docs, near):
    first = at[0] * 512 + 128 * b
    query_doc = document_of(first + lax.broadcasted_iota(jnp.int32, (1, 128), 1), at)
    return jnp.where(docs[128 * b : 128 * b + 1152, :] == query_doc, near, -1e30)


def stacked_heads(tile, kh):
    lane = lax.broadcasted_iota(jnp.int32, (128, 128), 1)
    mine = (lane < 64) if kh == 0 else (lane >= 64)
    other = pltpu.roll(tile, 64, 1)
    first, second = (tile, other) if kh == 0 else (other, tile)
    return jnp.concatenate([jnp.where(mine, first, 0.0), jnp.where(mine, second, 0.0)], axis=0).astype(bf16)


def attend_kernel(at, raw, kv0, kv1, kv2, parts, small, cos, sin, p0, p1, p2, p3, attn, qb, kb, vb, lse, uq, uk, qinv, kinv, vt, docs):
    d = at[0]
    near = mark_documents(at, docs)
    for i in range(12):
        there = jnp.clip(d - 1 + i // 4, 0, 3)
        row = parts[4 * there][4 + i % 4 : 5 + i % 4]
        for s in range(1, 4):
            row = row + parts[4 * there + s][4 + i % 4 : 5 + i % 4]
        inverse = column(lax.rsqrt(row * (1.0 / 512) + epsilon))
        span = slice(128 * i, 128 * (i + 1))
        part = slice(128 * (i % 4), 128 * (i % 4 + 1))
        kv = (kv0, kv1, kv2)[i // 4]
        unit = kv[part, :128].astype(f32) * inverse
        key = unit * small[40:41, 256:384]
        uk[span, :] = unit
        kb[span, :] = (key * cos[span, :] + partner(key) * sin[span, :]).astype(bf16)
        value = kv[part, 128:]
        vb[span, :] = value
        vt[:, span] = value.T
        if i // 4 == 1:
            kinv[part, :] = inverse
            row = parts[4 * d][i % 4 : i % 4 + 1]
            for s in range(1, 4):
                row = row + parts[4 * d + s][i % 4 : i % 4 + 1]
            inverse = column(lax.rsqrt(row * (1.0 / 1024) + epsilon))
            qinv[part, :] = inverse
            for m in range(2):
                lanes = slice(128 * m, 128 * (m + 1))
                unit = raw[part, lanes] * inverse
                uq[part, lanes] = unit
                query = unit * small[40:41, lanes]
                qb[part, lanes] = (query * cos[span, :] + partner(query) * sin[span, :]).astype(bf16)
    for b in range(4):
        bias = seen_bias(at, b, docs, near)
        bias = jnp.concatenate([bias, bias], axis=1)
        window = slice(128 * b, 128 * b + 1152)
        for kh in range(2):
            lanes = slice(128 * kh, 128 * (kh + 1))
            heads = stacked_heads(qb[128 * b : 128 * (b + 1), lanes].astype(f32), kh)
            scores = dot(kb[window, :], heads, ((1,), (1,))) * 0.125 + bias
            top = jnp.max(scores, axis=0, keepdims=True)
            weights = jnp.exp(scores - top)
            total = jnp.sum(weights, axis=0, keepdims=True)
            lse[2 * b + kh : 2 * b + kh + 1, :] = top + jnp.log(total)
            mixed = dot(vt[64 * kh : 64 * kh + 64, window], weights.astype(bf16), ((1,), (0,))) / total
            tile = jnp.concatenate([mixed[:, :128], mixed[:, 128:]], axis=0).T
            attn[b, :, lanes] = tile.astype(bf16)
    for k, ref in enumerate((p0, p1, p2, p3)):
        ref[...] = attn[lax.rem(at[1] + k, 4)]


def attend(at, raw, kvs, parts, small, cos, sin):
    return call(
        attend_kernel,
        "attend",
        [sds(128, 256)] * 4
        + [
            sds(4, 128, 256),
            sds(512, 256),
            sds(1536, 128),
            sds(1536, 128),
            sds(8, 256, dtype=f32),
            sds(512, 256, dtype=f32),
            sds(1536, 128, dtype=f32),
            sds(512, 128, dtype=f32),
            sds(512, 128, dtype=f32),
        ],
        at,
        raw,
        *kvs,
        parts,
        small,
        cos,
        sin,
        flops=15 * 10**9,
        scratch=[pltpu.VMEM((128, 1536), bf16), pltpu.VMEM((1536, 128), f32)],
    )


def attend_back_kernel(
    at, g0, g1, g2, g3, qb, kb, vb, lse, uq, uk, cos, sin, base, wq, dkv_own, dkv_up, dkv_down, sums, kt, dk, dv, qgain, qrows, got, docs
):
    near = mark_documents(at, docs)
    for k, ref in enumerate((g0, g1, g2, g3)):
        got[lax.rem(at[1] - k + 4, 4)] = ref[...]
    for i in range(12):
        span = slice(128 * i, 128 * (i + 1))
        kt[:, span] = kb[span, :].T
    dk[...] = jnp.zeros_like(dk)
    dv[...] = jnp.zeros_like(dv)
    qgain[...] = jnp.zeros_like(qgain)
    for b in range(4):
        bias = seen_bias(at, b, docs, near)
        bias = jnp.concatenate([bias, bias], axis=1)
        window = slice(128 * b, 128 * b + 1152)
        own = slice(128 * b, 128 * (b + 1))
        table = slice(HALF + 128 * b, HALF + 128 * (b + 1))
        total = jnp.zeros((128, 1), f32)
        for kh in range(2):
            lanes = slice(128 * kh, 128 * (kh + 1))
            query = qb[own, lanes].astype(f32)
            heads = stacked_heads(query, kh)
            grads = stacked_heads(got[b, :, lanes].astype(f32), kh)
            scores = dot(kb[window, :], heads, ((1,), (1,))) * 0.125 + bias
            probs = jnp.exp(scores - lse[2 * b + kh : 2 * b + kh + 1, :])
            prob_grad = dot(vb[window, :], grads, ((1,), (1,)))
            centre = jnp.sum(probs * prob_grad, axis=0, keepdims=True)
            score_grad = (probs * (prob_grad - centre)).astype(bf16)
            dv[window, :] += dot(probs.astype(bf16), grads, ((1,), (0,)))
            dk[window, :] += dot(score_grad, heads, ((1,), (0,))) * 0.125
            flat = dot(kt[64 * kh : 64 * kh + 64, window], score_grad, ((1,), (0,))) * 0.125
            dq = jnp.concatenate([flat[:, :128], flat[:, 128:]], axis=0).T.astype(bf16).astype(f32)
            total = total + jnp.sum(dq * query, axis=1, keepdims=True)
            turned = dq * cos[table, :] - partner(dq) * sin[table, :]
            wq[own, lanes] = turned
            qgain[0:1, lanes] += jnp.sum(turned * uq[own, lanes], axis=0, keepdims=True)
        qrows[b : b + 1, :] = jnp.broadcast_to(total, (128, 128)).T[0:1]
    kgain = jnp.zeros((1, 128), f32)
    krows = []
    for i in range(12):
        span = slice(128 * i, 128 * (i + 1))
        part = slice(128 * (i % 4), 128 * (i % 4 + 1))
        grad = dk[span, :]
        spot = jnp.sum(grad * kb[span, :].astype(f32), axis=1, keepdims=True)
        krows.append(jnp.broadcast_to(spot, (128, 128)).T[0:1])
        turned = grad * cos[span, :] - partner(grad) * sin[span, :]
        kgain = kgain + jnp.sum(turned * uk[span, :], axis=0, keepdims=True)
        target = (dkv_down, dkv_own, dkv_up)[i // 4]
        target[part, :128] = grad.astype(target.dtype)
        target[part, 128:] = dv[span, :].astype(target.dtype)
    lane = lax.broadcasted_iota(jnp.int32, (1, 128), 1)
    none = jnp.zeros((6, 128), f32)
    for there in range(4):
        here = jnp.where(at[0] == there, 1.0, 0.0)
        mine = jnp.where(at[1] == there, 1.0, 0.0)
        rows = [qrows[0:4, :] * here]
        for i in range(4):
            row = jnp.zeros((1, 128), f32)
            for part in range(3):
                row = row + krows[4 * part + i] * jnp.where(at[0] - 1 + part == there, 1.0, 0.0)
            rows.append(row)
        for s in range(4):
            q_tile = qgain[0:1, 128 * (s // 2) : 128 * (s // 2 + 1)]
            if s % 2:
                q_tile = pltpu.roll(q_tile, 64, 1)
            k_tile = pltpu.roll(kgain, (64 - 32 * s) % 128, 1)
            gains = jnp.where(lane < 64, q_tile, jnp.where(lane < 96, k_tile, 0.0)) * mine
            more = base[4 * there + s]
            sums[4 * there + s] = jnp.concatenate(rows + [gains, more[0:1], none, more[8:24]], axis=0).astype(bf16)


def attend_back(at, gots, qb, kb, vb, lse, uq, uk, cos, sin, base):
    return call(
        attend_back_kernel,
        "attend_back",
        [
            sds(512, 256, dtype=f32),
            sds(512, 256, dtype=f32),
            sds(512, 256),
            sds(512, 256),
            sds(16, 32, 128),
        ],
        at,
        *gots,
        qb,
        kb,
        vb,
        lse,
        uq,
        uk,
        cos,
        sin,
        base,
        flops=30 * 10**9,
        scratch=[
            pltpu.VMEM((128, 1536), bf16),
            pltpu.VMEM((1536, 128), f32),
            pltpu.VMEM((1536, 128), f32),
            pltpu.VMEM((8, 256), f32),
            pltpu.VMEM((8, 128), f32),
            pltpu.VMEM((4, 128, 512), bf16),
            pltpu.VMEM((1536, 128), f32),
        ],
    )


def route_kernel(at, *refs):
    place_ref, used_ref, gs_ref = refs[8:]
    ids = lax.broadcasted_iota(jnp.int32, (32, 128), 0) + 4 * at[2]
    ids = jnp.where(ids >= 32, ids - 32, ids).astype(f32)
    slot = lax.broadcasted_iota(jnp.int32, (CAP, 128), 0).astype(f32)
    empty = jnp.zeros((CAP, 128), f32)
    hits = []
    for j, ref in enumerate(refs[:8]):
        meta = ref[:, 1024:].astype(f32)
        turned = meta.T
        used = turned[0:1] == ids
        for k in range(1, TOPK):
            used = used | (turned[k : k + 1] == ids)
        used_ref[j] = jnp.where(used, 1.0, 0.0)
        earlier = jnp.where(meta[:, 8:9] < turned[8:9], 1.0, 0.0).astype(bf16)
        before = dot(jnp.where(used, 1.0, 0.0).astype(bf16), earlier, ((1,), (0,)))
        spot = jnp.where(used & (before < CAP), before, 1000.0)
        hits.append([jnp.where(slot == spot[l : l + 1], 1.0, 0.0) for l in range(4)])
    for p in range(4):
        rows = []
        for l in range(4):
            rows.append(jnp.concatenate([hits[2 * p][l], empty], axis=1))
            rows.append(jnp.concatenate([empty, hits[2 * p + 1][l]], axis=1))
        chosen = jnp.concatenate(rows, axis=0).astype(bf16)
        place_ref[p] = chosen
        both = jnp.concatenate([refs[2 * p][:, :1024], refs[2 * p + 1][:, :1024]], axis=0)
        ups = dot(chosen, both, ((1,), (0,))).astype(bf16)
        for l in range(4):
            gs_ref[l, PAIR * p : PAIR * (p + 1), :] = ups[PAIR * l : PAIR * (l + 1)]


def route(at, cots):
    return call(
        route_kernel,
        "route",
        [sds(4, 4 * PAIR, 256), sds(8, 32, 128, dtype=f32), sds(4, ROWS, 1024)],
        at,
        *cots,
        flops=0,
        moved=0,
    )


def expert_step(where_ref, *refs):
    n2_refs = refs[0:8]
    place, used_ref, gs, small, w_ref = refs[8:13]
    dn_refs = tuple(ref.at[i] for ref in refs[13:15] for i in range(4))
    out_refs = tuple(ref.at[i] for ref in refs[15:17] for i in range(4))
    grads_ref = refs[17]
    xs, gate, ys, dxs, dgs = refs[18:23]
    step = pl.program_id(0)

    @pl.when(step == 0)
    def _():
        router_t = small[0:32, :].astype(bf16)
        back = lax.rem(32 - 4 * where_ref[0], 32)
        for p in range(4):
            both = jnp.concatenate([n2_refs[2 * p][...], n2_refs[2 * p + 1][...]], axis=0)
            used = jnp.concatenate([used_ref[2 * p], used_ref[2 * p + 1]], axis=1) > 0.5
            logits = pltpu.roll(dot(router_t, both, ((1,), (1,))), back, 0)
            masked = jnp.where(used, logits, -1e30)
            grown = jnp.where(used, jnp.exp(masked - jnp.max(masked, axis=0, keepdims=True)), 0.0)
            gates = grown / jnp.sum(grown, axis=0, keepdims=True)
            chosen = place[p]
            rows = dot(chosen, both, ((1,), (0,))).astype(bf16)
            hit = chosen.astype(f32)
            span = slice(PAIR * p, PAIR * (p + 1))
            for l in range(4):
                part = slice(PAIR * l, PAIR * (l + 1))
                share = jnp.sum(hit[part] * gates[l : l + 1], axis=1, keepdims=True)
                gate[l, span, :] = jnp.broadcast_to(share, (PAIR, 128))
                xs[l, span, :] = rows[part]

    w_in = w_ref[:, 0, :64, :].reshape(1024, 1024)
    w_out = w_ref[:, 0, 64:, :].reshape(512, 1024)
    x = xs[step]
    both = dot(x, w_in, ((1,), (0,)))
    gate_part, up_part = both[:, :512], both[:, 512:]
    sig = jax.nn.sigmoid(gate_part)
    silu = gate_part * sig
    hidden = (silu * up_part).astype(bf16)
    g = gs[0].astype(f32)
    share = gate[step][:, 0:1]
    dy = (g * share).astype(bf16)
    dh = dot(dy, w_out, ((1,), (1,)))
    dgu = jnp.concatenate(
        [dh * up_part * (sig * (1.0 + gate_part * (1.0 - sig))), dh * silu], axis=1
    ).astype(bf16)
    dxs[step] = dot(dgu, w_in, ((1,), (1,))).astype(bf16)
    y = dot(hidden, w_out, ((1,), (0,))).astype(bf16).astype(f32)
    ys[step] = (y * share).astype(bf16)
    lane = lax.broadcasted_iota(jnp.int32, (ROWS, 128), 1)
    dgate = jnp.sum(g * y, axis=1, keepdims=True)
    dgs[step] = jnp.where(lane == 4 * where_ref[0] + step, dgate, 0.0).astype(bf16)
    grads_ref[:, 0, :64, :] = dot(x, dgu, ((0,), (0,))).astype(bf16).reshape(16, 64, 1024)
    grads_ref[:, 0, 64:, :] = dot(hidden, dy, ((0,), (0,))).astype(bf16).reshape(16, 32, 1024)

    @pl.when(step == 3)
    def _():
        for p in range(4):
            chosen = place[p]
            span = slice(PAIR * p, PAIR * (p + 1))
            for source, targets, lo, hi in ((dxs, dn_refs, 0, 1024), (dgs, dn_refs, 1024, 1152), (ys, out_refs, 0, 1024)):
                stacked = jnp.concatenate([source[l, span, :] for l in range(4)], axis=0)
                total = dot(chosen, stacked, ((0,), (0,))).astype(bf16)
                targets[2 * p][:, lo:hi] = total[:128]
                targets[2 * p + 1][:, lo:hi] = total[128:]


def experts(e_index, n2s, place, used, gs, small, weights):
    whole = lambda *s: pl.BlockSpec(s, lambda i, *_: (0,) * len(s))
    each = lambda cols: pl.BlockSpec((1, ROWS, cols), lambda i, *_: (i, 0, 0))
    owned = pl.BlockSpec((16, 1, 96, 1024), lambda i, *_: (0, i, 0, 0))
    shape = lambda *s: jax.ShapeDtypeStruct(s, bf16)
    return pl.pallas_call(
        expert_step,
        grid_spec=pltpu.PrefetchScalarGridSpec(
            num_scalar_prefetch=1,
            grid=(4,),
            in_specs=[whole(128, 1024)] * 8
            + [
                whole(4, 4 * PAIR, 256),
                whole(8, 32, 128),
                each(1024),
                whole(48, 1024),
                owned,
            ],
            out_specs=[whole(4, 128, 1152)] * 2 + [whole(4, 128, 1024)] * 2 + [owned],
            scratch_shapes=[
                pltpu.VMEM((4, ROWS, 1024), bf16),
                pltpu.VMEM((4, ROWS, 128), f32),
                pltpu.VMEM((4, ROWS, 1024), bf16),
                pltpu.VMEM((4, ROWS, 1024), bf16),
                pltpu.VMEM((4, ROWS, 128), bf16),
            ],
        ),
        out_shape=[shape(4, 128, 1152)] * 2
        + [shape(4, 128, 1024)] * 2
        + [shape(16, 4, 96, 1024)],
        compiler_params=pltpu.CompilerParams(vmem_limit_bytes=VMEM_BYTES),
        cost_estimate=pl.CostEstimate(flops=28 * 10**9, bytes_accessed=40 * 10**6, transcendentals=10**6),
        name="experts",
    )(e_index, *n2s, place, used, gs, small, weights)


def split(x):
    high = x.astype(bf16)
    return high, (x - high.astype(f32)).astype(bf16)


def o_pieces(at, refs):
    core = lax.rem(at[2], 2)
    for k, ref in enumerate(refs):
        chip = lax.rem(at[2] // 2 - k + 4, 4)
        yield block(2 * chip + core), ref[:, :128]
        yield block(2 * chip + 1 - core), ref[:, 128:]


def quarter(index):
    return pl.ds(pl.multiple_of(256 * index, 256), 256)


def middle_kernel(at, tok, a0, a1, a2, a3, o0, o1, o2, o3, small, middle_ref, low_ref, inverse_ref, rows_ref):
    for k, ref in enumerate((a0, a1, a2, a3)):
        rows_ref[:, quarter(lax.rem(at[1] - k + 4, 4))] = ref[...]
    rows = rows_ref[...]
    for lanes, piece in o_pieces(at, (o0, o1, o2, o3)):
        middle_ref[:, lanes] = tok[:, lanes].astype(f32) + dot(rows, piece, ((1,), (0,)))
    total = middle_ref[...]
    inverse = lax.rsqrt(jnp.mean(total * total, axis=1, keepdims=True) + epsilon)
    low_ref[...] = (total * inverse * small[33:34]).astype(bf16)
    inverse_ref[...] = jnp.broadcast_to(inverse, (128, 128))


def make_middle(at, tok, attns, parts, small):
    return call(
        middle_kernel,
        "middle",
        [sds(128, 1024, dtype=f32), sds(128, 1024), sds(128, 128, dtype=f32)],
        at,
        tok,
        *attns,
        *parts,
        small,
        flops=6 * 10**9,
        scratch=[pltpu.VMEM((128, 1024), bf16)],
    )


def middle_back_kernel(
    at, p0a, p0b, p1, p2, p3, middle, inverse_ref, low, cot, small, o0, o1, o2, o3, grad_ref, s0, s1, s2, s3, sums_ref, branch_ref, back_ref
):
    total = p0a[0].astype(f32) + p0b[0].astype(f32) + p1[...].astype(f32) + p2[...].astype(f32) + p3[...].astype(f32)
    dgates = total[:, 1024:1056]
    router_t = small[0:32].astype(bf16)
    logits = dot(low[...], router_t, ((1,), (1,)))
    ids = lax.broadcasted_iota(jnp.int32, (128, 32), 1).astype(f32)
    named = cot[:, 1024:].astype(f32)
    used = named[:, 0:1] == ids
    for k in range(1, TOPK):
        used = used | (named[:, k : k + 1] == ids)
    masked = jnp.where(used, logits, -1e30)
    grown = jnp.where(used, jnp.exp(masked - jnp.max(masked, axis=1, keepdims=True)), 0.0)
    gates = grown / jnp.sum(grown, axis=1, keepdims=True)
    logit_grad = gates * (dgates - jnp.sum(gates * dgates, axis=1, keepdims=True))
    high, rest = split(logit_grad)
    dn2 = total[:, :1024] + dot(high, router_t, ((1,), (0,))) + dot(rest, router_t, ((1,), (0,)))
    inverse = inverse_ref[:, 0:1]
    unit = middle[...] * inverse
    scaled = dn2 * small[33:34]
    grad = cot[:, :1024].astype(f32) + inverse * (scaled - unit * jnp.mean(scaled * unit, axis=1, keepdims=True))
    grad_ref[...] = grad
    branch = grad.astype(bf16)
    branch_ref[...] = branch
    back = jnp.zeros((128, 1024), f32)
    for lanes, piece in o_pieces(at, (o0, o1, o2, o3)):
        back = back + dot(branch_ref[:, lanes], piece, ((1,), (1,)))
    back_ref[...] = back.astype(bf16)
    for k, ref in enumerate((s0, s1, s2, s3)):
        lanes = quarter(lax.rem(at[1] + k, 4))
        ref[:, 0:256] = back_ref[:, lanes]
        ref[:, 256:512] = branch_ref[:, lanes]
    routers = dot(high, low[...], ((0,), (0,))) + dot(rest, low[...], ((0,), (0,)))
    second = jnp.sum(dn2 * unit, axis=0, keepdims=True)
    lane = lax.broadcasted_iota(jnp.int32, (16, 128), 1)
    for i in range(16):
        lanes = slice(128 * (i // 2), 128 * (i // 2 + 1))
        upper, lower, row = routers[0:16, lanes], routers[16:32, lanes], second[:, lanes]
        if i % 2 == 0:
            tile = jnp.where(lane < 64, upper, pltpu.roll(lower, 64, 1))
        else:
            tile = jnp.where(lane < 64, pltpu.roll(upper, 64, 1), lower)
            row = pltpu.roll(row, 64, 1)
        sums_ref[i] = jnp.concatenate([row, jnp.zeros((7, 128), f32), tile], axis=0)


def middle_back(at, pieces, middle, inverse, low, cot, small, parts):
    return call(
        middle_back_kernel,
        "middle_back",
        [sds(128, 1024, dtype=f32)] + [sds(128, 512)] * 4 + [sds(16, 24, 128, dtype=f32)],
        at,
        *pieces,
        middle,
        inverse,
        low,
        cot,
        small,
        *parts,
        flops=12 * 10**9,
        scratch=[pltpu.VMEM((128, 1024), bf16)] * 2,
    )


def out_grad_kernel(at, a0, a1, a2, a3, g0, g1, g2, g3, out_ref, cols):
    for k, ref in enumerate((g0, g1, g2, g3)):
        cols[block(lax.rem(at[1] - k + 4, 4)), :] = ref[:, 256:512]
    for k, part in enumerate((a0, a1, a2, a3)):
        rows = jnp.concatenate([part[i] for i in range(4)], axis=0)
        out_ref[quarter(lax.rem(at[1] - k + 4, 4)), :] = dot(rows, cols[...], ((0,), (0,))).astype(bf16)


def out_grads(at, attns, gots):
    scratch = [pltpu.VMEM((512, 256), bf16)]
    return call(out_grad_kernel, "out_grads", sds(1024, 256), at, *attns, *gots, flops=0, moved=0, scratch=scratch)


def finish_kernel(
    at, wq, own, up, down, sums, uq, uk, qinv, kinv, small, cos, sin, w_ref,
    dn0, dn1, dn2, dn3, keep_ref, send_ref, sums_ref, dqkv,
):
    got = sums[0].astype(f32)
    for i in range(1, 16):
        got = got + sums[i].astype(f32)
    sums_ref[...] = got
    for i in range(4):
        part = slice(128 * i, 128 * (i + 1))
        q_mean = column(got[i : i + 1]) * (1.0 / 1024)
        for m in range(2):
            lanes = slice(128 * m, 128 * (m + 1))
            grad = wq[part, lanes] * small[40:41, lanes] - uq[part, lanes] * q_mean
            dqkv[part, lanes] = (qinv[part, :] * grad).astype(bf16)
        total = own[part, :] + up[part, :].astype(f32) + down[part, :].astype(f32)
        dk = total[:, :128].astype(bf16).astype(f32)
        turned = dk * cos[part, :] - partner(dk) * sin[part, :]
        k_mean = column(got[4 + i : 5 + i]) * (1.0 / 512)
        grad = turned * small[40:41, 256:384] - uk[part, :] * k_mean
        dqkv[part, 256:384] = (kinv[part, :] * grad).astype(bf16)
        dqkv[part, 384:512] = total[:, 128:].astype(bf16)
    w = w_ref[...]
    for k, ref in enumerate((dn0, dn1, dn2, dn3)):
        ref[...] = dot(dqkv[block(lax.rem(at[1] + k, 4)), :], w, ((1,), (1,))).astype(bf16)
    even = lax.rem(at[2], 2) == 0
    left = dqkv[:, :384]
    right = jnp.concatenate([dqkv[:, 384:], jnp.zeros((512, 256), bf16)], axis=1)
    keep_ref[...] = jnp.where(even, left, right)
    send_ref[...] = jnp.where(even, right, left)


def finish(at, wq, own, up, down, sums, uq, uk, qinv, kinv, small, cos, sin, w_cols):
    return call(
        finish_kernel,
        "finish",
        [sds(128, 1024)] * 4 + [sds(512, 384)] * 2 + [sds(sums.shape[1], 128, dtype=f32)],
        at, wq, own, up, down, sums, uq, uk, qinv, kinv, small, cos, sin, w_cols,
        middle=(7, 11, 12),
        flops=10 * 10**9,
        scratch=[pltpu.VMEM((512, 512), bf16)],
    )


def weight_kernel(at, n1, n1_theirs, keep, got, o_part, o_theirs, r0, r1, r2, r3, grads):
    total = dot(n1[...], keep[...], ((1,), (0,))) + dot(n1_theirs[...], got[...], ((1,), (0,)))
    odd = lax.rem(at[2], 2).astype(f32)
    outs = (o_part[...].astype(f32) + o_theirs[...].astype(f32)) * odd
    grads[:, :, :128] = total[:, :128].astype(bf16).reshape(16, 64, 128)
    grads[:, :, 128:] = (total[:, 128:] + outs).astype(bf16).reshape(16, 64, 256)
    for k, ref in enumerate((r0, r1, r2, r3)):
        ref[...] = grads[:, pl.ds(pl.multiple_of(16 * lax.rem(at[2] // 2 + k, 4), 16), 16), :]


def weight_grads(at, *args):
    return call(
        weight_kernel,
        "weight_grads",
        [sds(16, 16, 384)] * 4,
        at,
        *args,
        flops=8 * 10**9,
        scratch=[pltpu.VMEM((16, 64, 384), bf16)],
    )


def input_kernel(at, p0, p1, p2, p3, tok, grad_ref, small, out_ref):
    dn1 = p0[...].astype(f32) + p1[...].astype(f32) + p2[...].astype(f32) + p3[...].astype(f32)
    x = tok[...].astype(f32)
    inverse = lax.rsqrt(jnp.mean(x * x, axis=1, keepdims=True) + epsilon)
    unit = x * inverse
    scaled = dn1 * small[32:33]
    out_ref[...] = grad_ref[...] + inverse * (scaled - unit * jnp.mean(scaled * unit, axis=1, keepdims=True))


def input_back(at, pieces, tok, grad, small):
    return call(input_kernel, "input_back", sds(128, 1024, dtype=f32), at, *pieces, tok, grad, small, flops=0, moved=0)


def pack_kernel(at, w_ref, o_ref, router_ref, gain_ref, key_ref, in_ref, down_ref, out_ref, moe_ref):
    moe_ref[:, :64, :] = in_ref[...]
    moe_ref[:, 64:, :] = down_ref[...]
    even = lax.rem(at[2], 2) == 0
    piece = o_ref[:, block(at[2])]
    key = jnp.concatenate([key_ref[...].astype(f32), jnp.zeros((1, 32), f32)], axis=1)
    extra = jnp.concatenate(
        [router_ref[...].astype(f32), gain_ref[...].astype(f32), key, jnp.zeros((28, 64), f32)], axis=0
    )
    extra = jnp.concatenate([extra, jnp.zeros((64, 64), f32)], axis=1).astype(bf16)
    for s in range(4):
        queries = w_ref[:, 256 * s : 256 * (s + 1)]
        keys = w_ref[:, 1024 + 128 * s : 1024 + 128 * (s + 1)]
        values = w_ref[:, 1536 + 128 * s : 1536 + 128 * (s + 1)]
        half = jnp.where(even, queries, jnp.concatenate([keys, values], axis=1))
        for d in range(4):
            out_ref[4 * d + s, :, 0:256] = half
            out_ref[4 * d + s, :, 256:384] = extra
            out_ref[4 * d + s, :, 384:512] = piece


def pack(at, *args):
    return call(pack_kernel, "pack", [sds(16, 64, 512), sds(4, 96, 1024)], at, *args, flops=10**9)


def last_kernel(at, *refs):
    pieces, (w_ref, gain_ref, qkv_ref, o_ref, gains_ref, key_ref, router_ref) = refs[:4], refs[4:]
    even = lax.rem(at[2], 2) == 0
    sums = jnp.zeros((16, 256), f32)
    for k in range(4):
        rows = pl.ds(pl.multiple_of(16 * lax.rem(at[2] // 2 - k + 4, 4), 16), 16)
        mine, theirs = pieces[k][:, :1792].astype(f32), pieces[k][:, 1792:].astype(f32)
        sums = sums + mine[:, 1536:] + theirs[:, 1536:]
        first, later = jnp.where(even, mine, theirs), jnp.where(even, theirs, mine)
        for s in range(4):
            lanes = 384 * s
            qkv_ref[rows, 256 * s : 256 * (s + 1)] = first[:, lanes : lanes + 256]
            qkv_ref[rows, 1024 + 128 * s : 1024 + 128 * (s + 1)] = first[:, lanes + 256 : lanes + 384]
            qkv_ref[rows, 1536 + 128 * s : 1536 + 128 * (s + 1)] = later[:, lanes : lanes + 128]
            o_ref[rows, 256 * s : 256 * (s + 1)] = later[:, lanes + 128 : lanes + 384]
    first_gain = row_sums(qkv_ref[...] * w_ref[...].astype(f32)) / gain_ref[0:1, :].astype(f32)
    gains_ref[0:1, :] = first_gain
    gains_ref[1:2, :] = sums[9:10, 128:192]
    gains_ref[2:3, :] = sums[8:9, 128:192]
    key_ref[...] = sums[8:9, 192:224]
    router_ref[...] = jnp.concatenate([sums[:, :64], sums[:, 64:128]], axis=0)


def last(at, pieces, w_qkv, norm_gains):
    return call(
        last_kernel,
        "last",
        [
            sds(64, 2048, dtype=f32),
            sds(64, 1024, dtype=f32),
            sds(3, 64, dtype=f32),
            sds(1, 32, dtype=f32),
            sds(32, 64, dtype=f32),
        ],
        at, *pieces, w_qkv, norm_gains,
    )


def chip_kernel(at, r0, r1, r2, r3, out_ref):
    total = r0[...].astype(f32) + r1[...].astype(f32) + r2[...].astype(f32) + r3[...].astype(f32)
    out_ref[...] = total.astype(bf16)


def chip_sum(at, pieces):
    return call(chip_kernel, "chip_sum", sds(*pieces[0].shape), at, *pieces, flops=0, moved=0)


def rows_kernel(at, got, sums, out_ref):
    for s in range(4):
        total = got[s].astype(f32)
        for d in range(1, 4):
            total = total + got[4 * d + s].astype(f32)
        out_ref[:, 384 * s : 384 * (s + 1)] = total.astype(bf16)
    out_ref[:, 1536:1664] = sums[16:32, :].astype(bf16)
    out_ref[:, 1664:1792] = sums[0:16, :].astype(bf16)


def sum_rows(at, got, sums):
    return call(rows_kernel, "sum_rows", sds(16, 1792), at, got, sums, flops=0, moved=0)


def join_kernel(at, mine, theirs, *outs):
    skipped = 4 - len(outs)
    for k, ref in enumerate(outs):
        ref[...] = (mine[k + skipped].astype(f32) + theirs[k + skipped].astype(f32)).astype(bf16)


def join(at, mine, theirs, count=3):
    return call(join_kernel, "join", [sds(*mine.shape[1:])] * count, at, mine, theirs, flops=0, moved=0)


def swap(array, axis):
    return lax.all_to_all(array, axis, split_axis=0, concat_axis=0, tiled=True)


def spread(array, axis, ways):
    return swap(jnp.broadcast_to(array[None], (ways,) + array.shape), axis)


def along_seq(array, k):
    return lax.ppermute(array, "seq", [(i, (i + k) % 4) for i in range(4)])


def along_dp(array, k):
    return lax.ppermute(array, "dp", [(i, (i + k) % 4) for i in range(4)])


def along_x(array, k):
    return lax.ppermute(array, "expert", [(i, (i + 2 * k) % 8) for i in range(8)])


def other_core(array):
    return lax.ppermute(array, "expert", [(i, i ^ 1) for i in range(8)])


def gather_x(array):
    return [array] + [along_x(array, k) for k in range(1, 4)]


def return_x(mine, joined, sums):
    return [mine, joined] + [along_x(sums[k - 1], -k) for k in range(1, 4)]


def after(values, *others):
    return lax.optimization_barrier((values, others))[0]


def shards(tokens, cotangent, doc_lengths, routes, route_rank, w_qkv, w_o, norm_gains, key_gain, w_router, w_in, w_out):
    d_index = lax.axis_index("dp")
    s_index = lax.axis_index("seq")
    e_index = lax.axis_index("expert")
    lengths = doc_lengths[0]
    tok = tokens[0]
    place = jnp.stack([d_index, s_index, e_index]).astype(jnp.int32)
    ends = [lengths[0]]
    for i in range(1, 4):
        ends.append(ends[-1] + lengths[i])
    at = jnp.concatenate([place, jnp.stack(ends)])
    w_send, moe_shard = pack(
        place, w_qkv, w_o, w_router.T, norm_gains, key_gain[None], w_in.reshape(4, 64, 1024), w_out
    )
    w_mine = swap(w_send, GROUP)
    tok_pieces = [tok] + [along_seq(tok, k) for k in range(1, 4)]
    cot = jnp.concatenate(
        [cotangent[0], routes[0].astype(bf16), route_rank[0].astype(bf16)[:, None], jnp.zeros((128, 119), bf16)], axis=1
    )
    cots = gather_x(cot)
    places = d_index * 512 - HALF + jnp.arange(1536, dtype=jnp.int32)
    starts = [jnp.zeros((), jnp.int32)] + ends
    begins = jnp.zeros((1536,), jnp.int32)
    for start in starts:
        begins = jnp.maximum(begins, jnp.where(places >= start, start, 0))
    lane = jnp.arange(128, dtype=jnp.int32)
    frequency = 10000.0 ** (-(lane % 32).astype(f32) / 32)
    angles = (places - begins).astype(f32)[:, None] * frequency[None, :]
    cos = jnp.cos(angles)
    sin = jnp.sin(angles) * jnp.where(lane % 64 < 32, -1.0, 1.0)[None, :]

    moe_shard = after(moe_shard, tok_pieces[1], tok_pieces[3])
    moe_all = lax.all_gather(moe_shard, GROUP, axis=0, tiled=False)
    w_mine, cots = after((w_mine, cots), cos, sin, tok_pieces)
    cots = cots + [other_core(c) for c in cots]
    w_theirs = after(other_core(w_mine), cots)
    n1, raw, kv, parts, small, w_cols, o_pair = project(at, tok_pieces, w_mine, w_theirs)
    up = [(i, i + 1) for i in range(3)]
    down = [(i + 1, i) for i in range(3)]
    kv_before = lax.ppermute(kv, "dp", up)
    kv_after = lax.ppermute(kv, "dp", down)
    parts = swap(parts, GROUP)
    o_parts = gather_x(after(o_pair, kv_before, kv_after))
    *attn_send, attn, qb, kb, vb, lse, uq, uk, qinv, kinv = attend(at, raw, [kv_before, kv, kv_after], parts, small, cos, sin)
    attn_got = [attn_send[0]] + [along_seq(attn_send[k], k) for k in range(1, 4)]
    middle, n2, inverse = make_middle(at, tok, attn_got, o_parts, small)
    routed = route(at, after(cots, n2))
    n2s = after(gather_x(n2), routed)
    n2s = n2s + [other_core(n) for n in n2s]
    made = experts(e_index[None].astype(jnp.int32), n2s, *routed, small, moe_all)
    attns = [attn] + [along_seq(attn, k) for k in range(1, 4)]
    made = after(made, attns)
    joined = other_core(made[1])
    sums = join(at, made[0], joined)
    n1_theirs = other_core(after(n1, sums))
    out_joined = other_core(after(made[3], sums))
    out_sums = join(at, made[2], out_joined)
    dn_pieces = after(return_x(made[0], joined, sums), n1_theirs, out_sums)
    moe_own = lax.psum_scatter(made[4].reshape(16 * 384, 1024), GROUP, scatter_dimension=0, tiled=True)
    moe_own = moe_own.reshape(4, 96, 1024).astype(f32)
    in_own = moe_own[:, :64].reshape(4, 64, 2, 512)
    down_own = moe_own[:, 64:]
    middle_grad, *grad_send, base = middle_back(at, dn_pieces, middle, inverse, n2, cot, small, o_parts)
    grad_got = [grad_send[0]] + [along_seq(grad_send[k], k) for k in range(1, 4)]
    out_pieces = [along_x(out_sums[k - 1], -k) for k in range(1, 4)]
    wq, dkv_own, dkv_up, dkv_down, sums = attend_back(at, grad_got, qb, kb, vb, lse, uq, uk, cos, sin, base)
    from_before = lax.ppermute(dkv_up, "dp", up)
    from_after = lax.ppermute(dkv_down, "dp", down)
    sums = swap(after(sums, out_pieces), GROUP)
    o_part = out_grads(at, attns, after(grad_got, wq))
    output = middle + made[2][0].astype(f32) + out_joined[0].astype(f32)
    for piece in out_pieces:
        output = output + piece.astype(f32)
    output = output.astype(bf16)
    done = finish(
        at, wq, dkv_own, from_before, from_after, sums, uq, uk, qinv, kinv, small, cos, sin, w_cols
    )
    dn1_pieces = [done[0]] + [along_seq(done[k], k) for k in range(1, 4)]
    keep, send, summed = done[4:]
    o_theirs = other_core(after(o_part, send))
    parts = weight_grads(at, after(n1, output), n1_theirs, keep, other_core(send), o_part, o_theirs)
    halves = chip_sum(at, [parts[0]] + [along_x(parts[k], k) for k in range(1, 4)])
    halves = swap(halves, GROUP)
    input_grad = input_back(at, dn1_pieces, tok, middle_grad, small)
    own = sum_rows(at, after(halves, in_own, down_own, input_grad), summed)
    pieces = gather_x(jnp.concatenate([own, other_core(own)], axis=1))
    qkv_own, o_own, gains_own, key_own, router_own = last(at, pieces, w_qkv, norm_gains)
    return (output[None], input_grad[None], qkv_own, o_own, gains_own, key_own[0], router_own.T, in_own, down_own)


def solution(mesh):
    both = P("expert", GROUP, None)
    rows = P(GROUP, None)
    return jax.shard_map(
        shards,
        mesh=mesh,
        in_specs=(
            both,
            both,
            P("expert", None),
            both,
            P("expert", GROUP),
            rows,
            rows,
            P(None, GROUP),
            P(GROUP),
            rows,
            P("expert", GROUP, None, None),
            P("expert", GROUP, None),
        ),
        out_specs=(
            both,
            both,
            rows,
            rows,
            P(None, GROUP),
            P(GROUP),
            rows,
            P("expert", GROUP, None, None),
            P("expert", GROUP, None),
        ),
        check_vma=False,
    )
```

```python
import jax
import jax.numpy as jnp
from jax import lax
from jax.experimental import pallas as pl
from jax.experimental.pallas import tpu as pltpu
from jax.sharding import PartitionSpec as P

HEADS = 16
KV_HEADS = 8
HEAD_DIM = 64
TOPK = 8
HALF = 512
CAP = 40
PAIR = 2 * CAP
ROWS = 8 * CAP
VMEM_BYTES = 64 * 1024 * 1024

GROUP = ("dp", "seq")
ALL = ("dp", "seq", "expert")
epsilon = 1e-05
highest = lax.Precision.HIGHEST
bf16 = jnp.bfloat16
f32 = jnp.float32


def dot(a, b, dims, **kw):
    return lax.dot_general(a, b, ((dims[0], dims[1]), ((), ())), preferred_element_type=f32, **kw)


def call(kernel, name, out_shape, *args, flops=10**8, scratch=(), moved=10**6, middle=()):
    whole = lambda a: pl.BlockSpec(a.shape, lambda _: (0,) * len(a.shape))
    specs = [pl.BlockSpec(memory_space=pltpu.SMEM)] + [whole(a) for a in args[1:]]
    for i in middle:
        specs[i] = pl.BlockSpec((512, 128), lambda _: (1, 0))
    return pl.pallas_call(
        kernel,
        grid=(1,),
        in_specs=specs,
        out_specs=jax.tree.map(whole, out_shape),
        out_shape=out_shape,
        scratch_shapes=list(scratch),
        compiler_params=pltpu.CompilerParams(vmem_limit_bytes=VMEM_BYTES),
        cost_estimate=pl.CostEstimate(flops=flops, bytes_accessed=moved, transcendentals=0),
        name=name,
    )(*args)


def sds(*shape, dtype=bf16):
    return jax.ShapeDtypeStruct(shape, dtype)


def block(index):
    return pl.ds(pl.multiple_of(index * 128, 128), 128)


def column(row):
    return jnp.broadcast_to(row, (128, 128)).T


def partner(x):
    lane = lax.broadcasted_iota(jnp.int32, x.shape, 1)
    return jnp.where(lane % 64 < 32, pltpu.roll(x, 96, 1), pltpu.roll(x, 32, 1))


def row_sums(x):
    ones = jnp.ones((8, x.shape[1]), f32)
    return dot(ones, x, ((1,), (1,)), precision=highest)[0:1]


def project_kernel(at, t0, t1, t2, t3, mine, theirs, n1_ref, raw_ref, kv_ref, parts_ref, small_ref, w_ref, o_ref, rows):
    s = at[1]
    even = lax.rem(at[2], 2) == 0
    here, there = mine[:, :, :256].reshape(1024, 256), theirs[:, :, :256].reshape(1024, 256)
    w_ref[:, :256] = jnp.where(even, here, there)
    w_ref[:, 256:] = jnp.where(even, there, here)
    o_ref[:, :128] = mine[:, :, 384:].reshape(1024, 128)
    o_ref[:, 128:] = theirs[:, :, 384:].reshape(1024, 128)
    w = w_ref[...]
    lane = lax.broadcasted_iota(jnp.int32, (48, 128), 1)
    for i in range(8):
        low, high = mine[2 * i, :48, 256:384].astype(f32), mine[2 * i + 1, :48, 256:384].astype(f32)
        small_ref[:, 128 * i : 128 * (i + 1)] = jnp.where(lane < 64, low, pltpu.roll(high, 64, 1))
    gain = small_ref[32:33, :]
    for ds, t in enumerate((t0, t1, t2, t3)):
        x = t[...].astype(f32)
        low = (x * lax.rsqrt(jnp.mean(x * x, axis=1, keepdims=True) + epsilon) * gain).astype(bf16)
        turned = low.astype(f32).T.astype(bf16)
        raw = dot(low, w, ((1,), (0,)))
        place = lax.rem(s - ds + 4, 4)
        n1_ref[:, block(place)] = turned
        raw_ref[block(place), :] = raw
        kv_ref[block(place), :] = raw[:, 256:].astype(bf16)
        rows[pl.ds(place, 1), :] = row_sums(raw[:, :256] * raw[:, :256])
        rows[pl.ds(place + 4, 1), :] = row_sums(raw[:, 256:384] * raw[:, 256:384])
    parts_ref[...] = jnp.broadcast_to(rows[...][None], (16, 8, 128))
    start = pl.multiple_of(s * 256, 256)
    chunk = small_ref[35:36, pl.ds(start, 256)]
    at_row = lax.broadcasted_iota(jnp.int32, (256, 128), 0)
    at_col = lax.broadcasted_iota(jnp.int32, (256, 128), 1)
    pick = jnp.where(at_row == 64 * (at_col // 32) + at_col % 32, 1.0, 0.0)
    small_ref[40:41, 0:256] = small_ref[34:35, pl.ds(start, 256)]
    small_ref[40:41, 256:384] = dot(jnp.broadcast_to(chunk, (8, 256)), pick, ((1,), (0,)), precision=highest)[0:1]


def project(at, pieces, mine, theirs):
    return call(
        project_kernel,
        "project",
        [
            sds(1024, 512),
            sds(512, 512, dtype=f32),
            sds(512, 256),
            sds(16, 8, 128, dtype=f32),
            sds(48, 1024, dtype=f32),
            sds(1024, 512),
            sds(1024, 256),
        ],
        at,
        *pieces,
        mine,
        theirs,
        flops=8 * 10**9,
        scratch=[pltpu.VMEM((8, 128), f32)],
    )


def document_of(places, at):
    found = jnp.zeros(places.shape, f32)
    for i in range(4):
        found = found + jnp.where(places >= at[3 + i], 1.0, 0.0)
    return jnp.where((places >= 0) & (places < 2048), found, -1.0)


def mark_documents(at, docs):
    docs[...] = document_of(at[0] * 512 - HALF + lax.broadcasted_iota(jnp.int32, (1536, 128), 0), at)
    apart = lax.broadcasted_iota(jnp.int32, (1152, 128), 0) - lax.broadcasted_iota(jnp.int32, (1152, 128), 1)
    return jnp.where((apart >= 0) & (apart < 2 * HALF), 0.0, -1e30)


def seen_bias(at, b, docs, near):
    first = at[0] * 512 + 128 * b
    query_doc = document_of(first + lax.broadcasted_iota(jnp.int32, (1, 128), 1), at)
    return jnp.where(docs[128 * b : 128 * b + 1152, :] == query_doc, near, -1e30)


def stacked_heads(tile, kh):
    lane = lax.broadcasted_iota(jnp.int32, (128, 128), 1)
    mine = (lane < 64) if kh == 0 else (lane >= 64)
    other = pltpu.roll(tile, 64, 1)
    first, second = (tile, other) if kh == 0 else (other, tile)
    return jnp.concatenate([jnp.where(mine, first, 0.0), jnp.where(mine, second, 0.0)], axis=0).astype(bf16)


def attend_kernel(at, raw, kv0, kv1, kv2, parts, small, cos, sin, p0, p1, p2, p3, attn, qb, kb, vb, lse, uq, uk, qinv, kinv, vt, docs):
    d = at[0]
    near = mark_documents(at, docs)
    for i in range(12):
        there = jnp.clip(d - 1 + i // 4, 0, 3)
        row = parts[4 * there][4 + i % 4 : 5 + i % 4]
        for s in range(1, 4):
            row = row + parts[4 * there + s][4 + i % 4 : 5 + i % 4]
        inverse = column(lax.rsqrt(row * (1.0 / 512) + epsilon))
        span = slice(128 * i, 128 * (i + 1))
        part = slice(128 * (i % 4), 128 * (i % 4 + 1))
        kv = (kv0, kv1, kv2)[i // 4]
        unit = kv[part, :128].astype(f32) * inverse
        key = unit * small[40:41, 256:384]
        uk[span, :] = unit
        kb[span, :] = (key * cos[span, :] + partner(key) * sin[span, :]).astype(bf16)
        value = kv[part, 128:]
        vb[span, :] = value
        vt[:, span] = value.T
        if i // 4 == 1:
            kinv[part, :] = inverse
            row = parts[4 * d][i % 4 : i % 4 + 1]
            for s in range(1, 4):
                row = row + parts[4 * d + s][i % 4 : i % 4 + 1]
            inverse = column(lax.rsqrt(row * (1.0 / 1024) + epsilon))
            qinv[part, :] = inverse
            for m in range(2):
                lanes = slice(128 * m, 128 * (m + 1))
                unit = raw[part, lanes] * inverse
                uq[part, lanes] = unit
                query = unit * small[40:41, lanes]
                qb[part, lanes] = (query * cos[span, :] + partner(query) * sin[span, :]).astype(bf16)
    for b in range(4):
        bias = seen_bias(at, b, docs, near)
        bias = jnp.concatenate([bias, bias], axis=1)
        window = slice(128 * b, 128 * b + 1152)
        for kh in range(2):
            lanes = slice(128 * kh, 128 * (kh + 1))
            heads = stacked_heads(qb[128 * b : 128 * (b + 1), lanes].astype(f32), kh)
            scores = dot(kb[window, :], heads, ((1,), (1,))) * 0.125 + bias
            top = jnp.max(scores, axis=0, keepdims=True)
            weights = jnp.exp(scores - top)
            total = jnp.sum(weights, axis=0, keepdims=True)
            lse[2 * b + kh : 2 * b + kh + 1, :] = top + jnp.log(total)
            mixed = dot(vt[64 * kh : 64 * kh + 64, window], weights.astype(bf16), ((1,), (0,))) / total
            tile = jnp.concatenate([mixed[:, :128], mixed[:, 128:]], axis=0).T
            attn[b, :, lanes] = tile.astype(bf16)
    for k, ref in enumerate((p0, p1, p2, p3)):
        ref[...] = attn[lax.rem(at[1] + k, 4)]


def attend(at, raw, kvs, parts, small, cos, sin):
    return call(
        attend_kernel,
        "attend",
        [sds(128, 256)] * 4
        + [
            sds(4, 128, 256),
            sds(512, 256),
            sds(1536, 128),
            sds(1536, 128),
            sds(8, 256, dtype=f32),
            sds(512, 256, dtype=f32),
            sds(1536, 128, dtype=f32),
            sds(512, 128, dtype=f32),
            sds(512, 128, dtype=f32),
        ],
        at,
        raw,
        *kvs,
        parts,
        small,
        cos,
        sin,
        flops=15 * 10**9,
        scratch=[pltpu.VMEM((128, 1536), bf16), pltpu.VMEM((1536, 128), f32)],
    )


def attend_back_kernel(
    at, g0, g1, g2, g3, qb, kb, vb, lse, uq, uk, cos, sin, base, wq, dkv_own, dkv_up, dkv_down, sums, kt, dk, dv, qgain, qrows, got, docs
):
    near = mark_documents(at, docs)
    for k, ref in enumerate((g0, g1, g2, g3)):
        got[lax.rem(at[1] - k + 4, 4)] = ref[...]
    for i in range(12):
        span = slice(128 * i, 128 * (i + 1))
        kt[:, span] = kb[span, :].T
    dk[...] = jnp.zeros_like(dk)
    dv[...] = jnp.zeros_like(dv)
    qgain[...] = jnp.zeros_like(qgain)
    for b in range(4):
        bias = seen_bias(at, b, docs, near)
        bias = jnp.concatenate([bias, bias], axis=1)
        window = slice(128 * b, 128 * b + 1152)
        own = slice(128 * b, 128 * (b + 1))
        table = slice(HALF + 128 * b, HALF + 128 * (b + 1))
        total = jnp.zeros((128, 1), f32)
        for kh in range(2):
            lanes = slice(128 * kh, 128 * (kh + 1))
            query = qb[own, lanes].astype(f32)
            heads = stacked_heads(query, kh)
            grads = stacked_heads(got[b, :, lanes].astype(f32), kh)
            scores = dot(kb[window, :], heads, ((1,), (1,))) * 0.125 + bias
            probs = jnp.exp(scores - lse[2 * b + kh : 2 * b + kh + 1, :])
            prob_grad = dot(vb[window, :], grads, ((1,), (1,)))
            centre = jnp.sum(probs * prob_grad, axis=0, keepdims=True)
            score_grad = (probs * (prob_grad - centre)).astype(bf16)
            dv[window, :] += dot(probs.astype(bf16), grads, ((1,), (0,)))
            dk[window, :] += dot(score_grad, heads, ((1,), (0,))) * 0.125
            flat = dot(kt[64 * kh : 64 * kh + 64, window], score_grad, ((1,), (0,))) * 0.125
            dq = jnp.concatenate([flat[:, :128], flat[:, 128:]], axis=0).T.astype(bf16).astype(f32)
            total = total + jnp.sum(dq * query, axis=1, keepdims=True)
            turned = dq * cos[table, :] - partner(dq) * sin[table, :]
            wq[own, lanes] = turned
            qgain[0:1, lanes] += jnp.sum(turned * uq[own, lanes], axis=0, keepdims=True)
        qrows[b : b + 1, :] = jnp.broadcast_to(total, (128, 128)).T[0:1]
    kgain = jnp.zeros((1, 128), f32)
    krows = []
    for i in range(12):
        span = slice(128 * i, 128 * (i + 1))
        part = slice(128 * (i % 4), 128 * (i % 4 + 1))
        grad = dk[span, :]
        spot = jnp.sum(grad * kb[span, :].astype(f32), axis=1, keepdims=True)
        krows.append(jnp.broadcast_to(spot, (128, 128)).T[0:1])
        turned = grad * cos[span, :] - partner(grad) * sin[span, :]
        kgain = kgain + jnp.sum(turned * uk[span, :], axis=0, keepdims=True)
        target = (dkv_down, dkv_own, dkv_up)[i // 4]
        target[part, :128] = grad.astype(target.dtype)
        target[part, 128:] = dv[span, :].astype(target.dtype)
    lane = lax.broadcasted_iota(jnp.int32, (1, 128), 1)
    none = jnp.zeros((6, 128), f32)
    for there in range(4):
        here = jnp.where(at[0] == there, 1.0, 0.0)
        mine = jnp.where(at[1] == there, 1.0, 0.0)
        rows = [qrows[0:4, :] * here]
        for i in range(4):
            row = jnp.zeros((1, 128), f32)
            for part in range(3):
                row = row + krows[4 * part + i] * jnp.where(at[0] - 1 + part == there, 1.0, 0.0)
            rows.append(row)
        for s in range(4):
            q_tile = qgain[0:1, 128 * (s // 2) : 128 * (s // 2 + 1)]
            if s % 2:
                q_tile = pltpu.roll(q_tile, 64, 1)
            k_tile = pltpu.roll(kgain, (64 - 32 * s) % 128, 1)
            gains = jnp.where(lane < 64, q_tile, jnp.where(lane < 96, k_tile, 0.0)) * mine
            more = base[4 * there + s]
            sums[4 * there + s] = jnp.concatenate(rows + [gains, more[0:1], none, more[8:24]], axis=0).astype(bf16)


def attend_back(at, gots, qb, kb, vb, lse, uq, uk, cos, sin, base):
    return call(
        attend_back_kernel,
        "attend_back",
        [
            sds(512, 256, dtype=f32),
            sds(512, 256, dtype=f32),
            sds(512, 256),
            sds(512, 256),
            sds(16, 32, 128),
        ],
        at,
        *gots,
        qb,
        kb,
        vb,
        lse,
        uq,
        uk,
        cos,
        sin,
        base,
        flops=30 * 10**9,
        scratch=[
            pltpu.VMEM((128, 1536), bf16),
            pltpu.VMEM((1536, 128), f32),
            pltpu.VMEM((1536, 128), f32),
            pltpu.VMEM((8, 256), f32),
            pltpu.VMEM((8, 128), f32),
            pltpu.VMEM((4, 128, 512), bf16),
            pltpu.VMEM((1536, 128), f32),
        ],
    )


def route_kernel(at, *refs):
    place_ref, used_ref, gs_ref = refs[8:]
    ids = lax.broadcasted_iota(jnp.int32, (32, 128), 0) + 4 * at[2]
    ids = jnp.where(ids >= 32, ids - 32, ids).astype(f32)
    slot = lax.broadcasted_iota(jnp.int32, (CAP, 128), 0).astype(f32)
    empty = jnp.zeros((CAP, 128), f32)
    hits = []
    for j, ref in enumerate(refs[:8]):
        meta = ref[:, 1024:].astype(f32)
        turned = meta.T
        used = turned[0:1] == ids
        for k in range(1, TOPK):
            used = used | (turned[k : k + 1] == ids)
        used_ref[j] = jnp.where(used, 1.0, 0.0)
        earlier = jnp.where(meta[:, 8:9] < turned[8:9], 1.0, 0.0).astype(bf16)
        before = dot(jnp.where(used, 1.0, 0.0).astype(bf16), earlier, ((1,), (0,)))
        spot = jnp.where(used & (before < CAP), before, 1000.0)
        hits.append([jnp.where(slot == spot[l : l + 1], 1.0, 0.0) for l in range(4)])
    for p in range(4):
        rows = []
        for l in range(4):
            rows.append(jnp.concatenate([hits[2 * p][l], empty], axis=1))
            rows.append(jnp.concatenate([empty, hits[2 * p + 1][l]], axis=1))
        chosen = jnp.concatenate(rows, axis=0).astype(bf16)
        place_ref[p] = chosen
        both = jnp.concatenate([refs[2 * p][:, :1024], refs[2 * p + 1][:, :1024]], axis=0)
        ups = dot(chosen, both, ((1,), (0,))).astype(bf16)
        for l in range(4):
            gs_ref[l, PAIR * p : PAIR * (p + 1), :] = ups[PAIR * l : PAIR * (l + 1)]


def route(at, cots):
    return call(
        route_kernel,
        "route",
        [sds(4, 4 * PAIR, 256), sds(8, 32, 128, dtype=f32), sds(4, ROWS, 1024)],
        at,
        *cots,
        flops=0,
        moved=0,
    )


def expert_step(where_ref, *refs):
    n2_refs = refs[0:8]
    place, used_ref, gs, small, weights = refs[8:13]
    results, grads_ref = refs[13:17], refs[17]
    xs, gate, ys, dxs, dgs, held = refs[18:24]
    staged, load_sems, store_sems = refs[24:28], refs[28], refs[29]
    dn_refs = tuple(ref.at[i] for ref in staged[:2] for i in range(4))
    out_refs = tuple(ref.at[i] for ref in staged[2:] for i in range(4))
    step = pl.program_id(0)
    slot = lax.rem(step, 2)
    load = lambda l, s: pltpu.make_async_copy(weights.at[:, l], held.at[s], load_sems.at[s])
    stores = [pltpu.make_async_copy(staged[i], results[i], store_sems.at[i]) for i in range(4)]

    @pl.when(step == 0)
    def _():
        load(0, 0).start()
        load(1, 1).start()
        router_t = small[0:32, :].astype(bf16)
        back = lax.rem(32 - 4 * where_ref[0], 32)
        for p in range(4):
            both = jnp.concatenate([n2_refs[2 * p][...], n2_refs[2 * p + 1][...]], axis=0)
            used = jnp.concatenate([used_ref[2 * p], used_ref[2 * p + 1]], axis=1) > 0.5
            logits = pltpu.roll(dot(router_t, both, ((1,), (1,))), back, 0)
            masked = jnp.where(used, logits, -1e30)
            grown = jnp.where(used, jnp.exp(masked - jnp.max(masked, axis=0, keepdims=True)), 0.0)
            gates = grown / jnp.sum(grown, axis=0, keepdims=True)
            chosen = place[p]
            rows = dot(chosen, both, ((1,), (0,))).astype(bf16)
            hit = chosen.astype(f32)
            span = slice(PAIR * p, PAIR * (p + 1))
            for l in range(4):
                part = slice(PAIR * l, PAIR * (l + 1))
                share = jnp.sum(hit[part] * gates[l : l + 1], axis=1, keepdims=True)
                gate[l, span, :] = jnp.broadcast_to(share, (PAIR, 128))
                xs[l, span, :] = rows[part]

    load(step, slot).wait()
    w_in = held[slot, :, :64, :].reshape(1024, 1024)
    w_out = held[slot, :, 64:, :].reshape(512, 1024)
    x = xs[step]
    both = dot(x, w_in, ((1,), (0,)))
    gate_part, up_part = both[:, :512], both[:, 512:]
    sig = jax.nn.sigmoid(gate_part)
    silu = gate_part * sig
    hidden = (silu * up_part).astype(bf16)
    g = gs[0].astype(f32)
    share = gate[step][:, 0:1]
    dy = (g * share).astype(bf16)
    dh = dot(dy, w_out, ((1,), (1,)))
    dgu = jnp.concatenate(
        [dh * up_part * (sig * (1.0 + gate_part * (1.0 - sig))), dh * silu], axis=1
    ).astype(bf16)
    dxs[step] = dot(dgu, w_in, ((1,), (1,))).astype(bf16)
    y = dot(hidden, w_out, ((1,), (0,))).astype(bf16).astype(f32)
    ys[step] = (y * share).astype(bf16)
    lane = lax.broadcasted_iota(jnp.int32, (ROWS, 128), 1)
    dgate = jnp.sum(g * y, axis=1, keepdims=True)
    dgs[step] = jnp.where(lane == 4 * where_ref[0] + step, dgate, 0.0).astype(bf16)

    @pl.when(step == 3)
    def _():
        for p in range(4):
            chosen = place[p]
            span = slice(PAIR * p, PAIR * (p + 1))
            for source, targets, lo, hi in ((dxs, dn_refs, 0, 1024), (dgs, dn_refs, 1024, 1152), (ys, out_refs, 0, 1024)):
                stacked = jnp.concatenate([source[l, span, :] for l in range(4)], axis=0)
                total = dot(chosen, stacked, ((0,), (0,))).astype(bf16)
                targets[2 * p][:, lo:hi] = total[:128]
                targets[2 * p + 1][:, lo:hi] = total[128:]
        for store in stores:
            store.start()

    @pl.when(step < 2)
    def _():
        load(step + 2, slot).start()

    grads_ref[:, 0, :64, :] = dot(x, dgu, ((0,), (0,))).astype(bf16).reshape(16, 64, 1024)
    grads_ref[:, 0, 64:, :] = dot(hidden, dy, ((0,), (0,))).astype(bf16).reshape(16, 32, 1024)

    @pl.when(step == 3)
    def _():
        for store in stores:
            store.wait()


def experts(e_index, n2s, place, used, gs, small, weights):
    whole = lambda *s: pl.BlockSpec(s, lambda i, *_: (0,) * len(s))
    each = lambda cols: pl.BlockSpec((1, ROWS, cols), lambda i, *_: (i, 0, 0))
    owned = pl.BlockSpec((16, 1, 96, 1024), lambda i, *_: (0, i, 0, 0))
    shape = lambda *s: jax.ShapeDtypeStruct(s, bf16)
    return pl.pallas_call(
        expert_step,
        grid_spec=pltpu.PrefetchScalarGridSpec(
            num_scalar_prefetch=1,
            grid=(4,),
            in_specs=[whole(128, 1024)] * 8
            + [
                whole(4, 4 * PAIR, 256),
                whole(8, 32, 128),
                each(1024),
                whole(48, 1024),
                pl.BlockSpec(memory_space=pl.ANY),
            ],
            out_specs=[pl.BlockSpec(memory_space=pl.ANY)] * 4 + [owned],
            scratch_shapes=[
                pltpu.VMEM((4, ROWS, 1024), bf16),
                pltpu.VMEM((4, ROWS, 128), f32),
                pltpu.VMEM((4, ROWS, 1024), bf16),
                pltpu.VMEM((4, ROWS, 1024), bf16),
                pltpu.VMEM((4, ROWS, 128), bf16),
                pltpu.VMEM((2, 16, 96, 1024), bf16),
                pltpu.VMEM((4, 128, 1152), bf16),
                pltpu.VMEM((4, 128, 1152), bf16),
                pltpu.VMEM((4, 128, 1024), bf16),
                pltpu.VMEM((4, 128, 1024), bf16),
                pltpu.SemaphoreType.DMA((2,)),
                pltpu.SemaphoreType.DMA((4,)),
            ],
        ),
        out_shape=[shape(4, 128, 1152)] * 2
        + [shape(4, 128, 1024)] * 2
        + [shape(16, 4, 96, 1024)],
        compiler_params=pltpu.CompilerParams(vmem_limit_bytes=VMEM_BYTES),
        cost_estimate=pl.CostEstimate(flops=28 * 10**9, bytes_accessed=40 * 10**6, transcendentals=10**6),
        name="experts",
    )(e_index, *n2s, place, used, gs, small, weights)


def split(x):
    high = x.astype(bf16)
    return high, (x - high.astype(f32)).astype(bf16)


def o_pieces(at, refs):
    core = lax.rem(at[2], 2)
    for k, ref in enumerate(refs):
        chip = lax.rem(at[2] // 2 - k + 4, 4)
        yield block(2 * chip + core), ref[:, :128]
        yield block(2 * chip + 1 - core), ref[:, 128:]


def quarter(index):
    return pl.ds(pl.multiple_of(256 * index, 256), 256)


def middle_kernel(at, tok, a0, a1, a2, a3, o0, o1, o2, o3, small, middle_ref, low_ref, inverse_ref, rows_ref):
    for k, ref in enumerate((a0, a1, a2, a3)):
        rows_ref[:, quarter(lax.rem(at[1] - k + 4, 4))] = ref[...]
    rows = rows_ref[...]
    for lanes, piece in o_pieces(at, (o0, o1, o2, o3)):
        middle_ref[:, lanes] = tok[:, lanes].astype(f32) + dot(rows, piece, ((1,), (0,)))
    total = middle_ref[...]
    inverse = lax.rsqrt(jnp.mean(total * total, axis=1, keepdims=True) + epsilon)
    low_ref[...] = (total * inverse * small[33:34]).astype(bf16)
    inverse_ref[...] = jnp.broadcast_to(inverse, (128, 128))


def make_middle(at, tok, attns, parts, small):
    return call(
        middle_kernel,
        "middle",
        [sds(128, 1024, dtype=f32), sds(128, 1024), sds(128, 128, dtype=f32)],
        at,
        tok,
        *attns,
        *parts,
        small,
        flops=6 * 10**9,
        scratch=[pltpu.VMEM((128, 1024), bf16)],
    )


def middle_back_kernel(
    at, p0a, p0b, p1, p2, p3, middle, inverse_ref, low, cot, small, o0, o1, o2, o3, grad_ref, s0, s1, s2, s3, sums_ref, branch_ref, back_ref
):
    total = p0a[0].astype(f32) + p0b[0].astype(f32) + p1[...].astype(f32) + p2[...].astype(f32) + p3[...].astype(f32)
    dgates = total[:, 1024:1056]
    router_t = small[0:32].astype(bf16)
    logits = dot(low[...], router_t, ((1,), (1,)))
    ids = lax.broadcasted_iota(jnp.int32, (128, 32), 1).astype(f32)
    named = cot[:, 1024:].astype(f32)
    used = named[:, 0:1] == ids
    for k in range(1, TOPK):
        used = used | (named[:, k : k + 1] == ids)
    masked = jnp.where(used, logits, -1e30)
    grown = jnp.where(used, jnp.exp(masked - jnp.max(masked, axis=1, keepdims=True)), 0.0)
    gates = grown / jnp.sum(grown, axis=1, keepdims=True)
    logit_grad = gates * (dgates - jnp.sum(gates * dgates, axis=1, keepdims=True))
    high, rest = split(logit_grad)
    dn2 = total[:, :1024] + dot(high, router_t, ((1,), (0,))) + dot(rest, router_t, ((1,), (0,)))
    inverse = inverse_ref[:, 0:1]
    unit = middle[...] * inverse
    scaled = dn2 * small[33:34]
    grad = cot[:, :1024].astype(f32) + inverse * (scaled - unit * jnp.mean(scaled * unit, axis=1, keepdims=True))
    grad_ref[...] = grad
    branch = grad.astype(bf16)
    branch_ref[...] = branch
    back = jnp.zeros((128, 1024), f32)
    for lanes, piece in o_pieces(at, (o0, o1, o2, o3)):
        back = back + dot(branch_ref[:, lanes], piece, ((1,), (1,)))
    back_ref[...] = back.astype(bf16)
    for k, ref in enumerate((s0, s1, s2, s3)):
        lanes = quarter(lax.rem(at[1] + k, 4))
        ref[:, 0:256] = back_ref[:, lanes]
        ref[:, 256:512] = branch_ref[:, lanes]
    routers = dot(high, low[...], ((0,), (0,))) + dot(rest, low[...], ((0,), (0,)))
    second = jnp.sum(dn2 * unit, axis=0, keepdims=True)
    lane = lax.broadcasted_iota(jnp.int32, (16, 128), 1)
    for i in range(16):
        lanes = slice(128 * (i // 2), 128 * (i // 2 + 1))
        upper, lower, row = routers[0:16, lanes], routers[16:32, lanes], second[:, lanes]
        if i % 2 == 0:
            tile = jnp.where(lane < 64, upper, pltpu.roll(lower, 64, 1))
        else:
            tile = jnp.where(lane < 64, pltpu.roll(upper, 64, 1), lower)
            row = pltpu.roll(row, 64, 1)
        sums_ref[i] = jnp.concatenate([row, jnp.zeros((7, 128), f32), tile], axis=0)


def middle_back(at, pieces, middle, inverse, low, cot, small, parts):
    return call(
        middle_back_kernel,
        "middle_back",
        [sds(128, 1024, dtype=f32)] + [sds(128, 512)] * 4 + [sds(16, 24, 128, dtype=f32)],
        at,
        *pieces,
        middle,
        inverse,
        low,
        cot,
        small,
        *parts,
        flops=12 * 10**9,
        scratch=[pltpu.VMEM((128, 1024), bf16)] * 2,
    )


def out_grad_kernel(at, a0, a1, a2, a3, g0, g1, g2, g3, out_ref, cols):
    for k, ref in enumerate((g0, g1, g2, g3)):
        cols[block(lax.rem(at[1] - k + 4, 4)), :] = ref[:, 256:512]
    for k, part in enumerate((a0, a1, a2, a3)):
        rows = jnp.concatenate([part[i] for i in range(4)], axis=0)
        out_ref[quarter(lax.rem(at[1] - k + 4, 4)), :] = dot(rows, cols[...], ((0,), (0,))).astype(bf16)


def out_grads(at, attns, gots):
    scratch = [pltpu.VMEM((512, 256), bf16)]
    return call(out_grad_kernel, "out_grads", sds(1024, 256), at, *attns, *gots, flops=0, moved=0, scratch=scratch)


def finish_kernel(
    at, wq, own, up, down, sums, uq, uk, qinv, kinv, small, cos, sin, w_ref,
    dn0, dn1, dn2, dn3, keep_ref, send_ref, sums_ref, dqkv,
):
    got = sums[0].astype(f32)
    for i in range(1, 16):
        got = got + sums[i].astype(f32)
    sums_ref[...] = got
    for i in range(4):
        part = slice(128 * i, 128 * (i + 1))
        q_mean = column(got[i : i + 1]) * (1.0 / 1024)
        for m in range(2):
            lanes = slice(128 * m, 128 * (m + 1))
            grad = wq[part, lanes] * small[40:41, lanes] - uq[part, lanes] * q_mean
            dqkv[part, lanes] = (qinv[part, :] * grad).astype(bf16)
        total = own[part, :] + up[part, :].astype(f32) + down[part, :].astype(f32)
        dk = total[:, :128].astype(bf16).astype(f32)
        turned = dk * cos[part, :] - partner(dk) * sin[part, :]
        k_mean = column(got[4 + i : 5 + i]) * (1.0 / 512)
        grad = turned * small[40:41, 256:384] - uk[part, :] * k_mean
        dqkv[part, 256:384] = (kinv[part, :] * grad).astype(bf16)
        dqkv[part, 384:512] = total[:, 128:].astype(bf16)
    w = w_ref[...]
    for k, ref in enumerate((dn0, dn1, dn2, dn3)):
        ref[...] = dot(dqkv[block(lax.rem(at[1] + k, 4)), :], w, ((1,), (1,))).astype(bf16)
    even = lax.rem(at[2], 2) == 0
    left = dqkv[:, :384]
    right = jnp.concatenate([dqkv[:, 384:], jnp.zeros((512, 256), bf16)], axis=1)
    keep_ref[...] = jnp.where(even, left, right)
    send_ref[...] = jnp.where(even, right, left)


def finish(at, wq, own, up, down, sums, uq, uk, qinv, kinv, small, cos, sin, w_cols):
    return call(
        finish_kernel,
        "finish",
        [sds(128, 1024)] * 4 + [sds(512, 384)] * 2 + [sds(sums.shape[1], 128, dtype=f32)],
        at, wq, own, up, down, sums, uq, uk, qinv, kinv, small, cos, sin, w_cols,
        middle=(7, 11, 12),
        flops=10 * 10**9,
        scratch=[pltpu.VMEM((512, 512), bf16)],
    )


def weight_kernel(at, n1, n1_theirs, keep, got, o_part, o_theirs, r0, r1, r2, r3, grads):
    total = dot(n1[...], keep[...], ((1,), (0,))) + dot(n1_theirs[...], got[...], ((1,), (0,)))
    odd = lax.rem(at[2], 2).astype(f32)
    outs = (o_part[...].astype(f32) + o_theirs[...].astype(f32)) * odd
    grads[:, :, :128] = total[:, :128].astype(bf16).reshape(16, 64, 128)
    grads[:, :, 128:] = (total[:, 128:] + outs).astype(bf16).reshape(16, 64, 256)
    for k, ref in enumerate((r0, r1, r2, r3)):
        ref[...] = grads[:, pl.ds(pl.multiple_of(16 * lax.rem(at[2] // 2 + k, 4), 16), 16), :]


def weight_grads(at, *args):
    return call(
        weight_kernel,
        "weight_grads",
        [sds(16, 16, 384)] * 4,
        at,
        *args,
        flops=8 * 10**9,
        scratch=[pltpu.VMEM((16, 64, 384), bf16)],
    )


def input_kernel(at, p0, p1, p2, p3, tok, grad_ref, small, out_ref):
    dn1 = p0[...].astype(f32) + p1[...].astype(f32) + p2[...].astype(f32) + p3[...].astype(f32)
    x = tok[...].astype(f32)
    inverse = lax.rsqrt(jnp.mean(x * x, axis=1, keepdims=True) + epsilon)
    unit = x * inverse
    scaled = dn1 * small[32:33]
    out_ref[...] = grad_ref[...] + inverse * (scaled - unit * jnp.mean(scaled * unit, axis=1, keepdims=True))


def input_back(at, pieces, tok, grad, small):
    return call(input_kernel, "input_back", sds(128, 1024, dtype=f32), at, *pieces, tok, grad, small, flops=0, moved=0)


def pack_kernel(at, w_ref, o_ref, router_ref, gain_ref, key_ref, in_ref, down_ref, out_ref, moe_ref):
    moe_ref[:, :64, :] = in_ref[...]
    moe_ref[:, 64:, :] = down_ref[...]
    even = lax.rem(at[2], 2) == 0
    piece = o_ref[:, block(at[2])]
    key = jnp.concatenate([key_ref[...].astype(f32), jnp.zeros((1, 32), f32)], axis=1)
    extra = jnp.concatenate(
        [router_ref[...].astype(f32), gain_ref[...].astype(f32), key, jnp.zeros((28, 64), f32)], axis=0
    )
    extra = jnp.concatenate([extra, jnp.zeros((64, 64), f32)], axis=1).astype(bf16)
    for s in range(4):
        queries = w_ref[:, 256 * s : 256 * (s + 1)]
        keys = w_ref[:, 1024 + 128 * s : 1024 + 128 * (s + 1)]
        values = w_ref[:, 1536 + 128 * s : 1536 + 128 * (s + 1)]
        half = jnp.where(even, queries, jnp.concatenate([keys, values], axis=1))
        for d in range(4):
            out_ref[4 * d + s, :, 0:256] = half
            out_ref[4 * d + s, :, 256:384] = extra
            out_ref[4 * d + s, :, 384:512] = piece


def pack(at, *args):
    return call(pack_kernel, "pack", [sds(16, 64, 512), sds(4, 96, 1024)], at, *args, flops=10**9)


def last_kernel(at, *refs):
    pieces, (w_ref, gain_ref, qkv_ref, o_ref, gains_ref, key_ref, router_ref) = refs[:4], refs[4:]
    even = lax.rem(at[2], 2) == 0
    sums = jnp.zeros((16, 256), f32)
    for k in range(4):
        rows = pl.ds(pl.multiple_of(16 * lax.rem(at[2] // 2 - k + 4, 4), 16), 16)
        mine, theirs = pieces[k][:, :1792].astype(f32), pieces[k][:, 1792:].astype(f32)
        sums = sums + mine[:, 1536:] + theirs[:, 1536:]
        first, later = jnp.where(even, mine, theirs), jnp.where(even, theirs, mine)
        for s in range(4):
            lanes = 384 * s
            qkv_ref[rows, 256 * s : 256 * (s + 1)] = first[:, lanes : lanes + 256]
            qkv_ref[rows, 1024 + 128 * s : 1024 + 128 * (s + 1)] = first[:, lanes + 256 : lanes + 384]
            qkv_ref[rows, 1536 + 128 * s : 1536 + 128 * (s + 1)] = later[:, lanes : lanes + 128]
            o_ref[rows, 256 * s : 256 * (s + 1)] = later[:, lanes + 128 : lanes + 384]
    first_gain = row_sums(qkv_ref[...] * w_ref[...].astype(f32)) / gain_ref[0:1, :].astype(f32)
    gains_ref[0:1, :] = first_gain
    gains_ref[1:2, :] = sums[9:10, 128:192]
    gains_ref[2:3, :] = sums[8:9, 128:192]
    key_ref[...] = sums[8:9, 192:224]
    router_ref[...] = jnp.concatenate([sums[:, :64], sums[:, 64:128]], axis=0)


def last(at, pieces, w_qkv, norm_gains):
    return call(
        last_kernel,
        "last",
        [
            sds(64, 2048, dtype=f32),
            sds(64, 1024, dtype=f32),
            sds(3, 64, dtype=f32),
            sds(1, 32, dtype=f32),
            sds(32, 64, dtype=f32),
        ],
        at, *pieces, w_qkv, norm_gains,
    )


def chip_kernel(at, r0, r1, r2, r3, out_ref):
    total = r0[...].astype(f32) + r1[...].astype(f32) + r2[...].astype(f32) + r3[...].astype(f32)
    out_ref[...] = total.astype(bf16)


def chip_sum(at, pieces):
    return call(chip_kernel, "chip_sum", sds(*pieces[0].shape), at, *pieces, flops=0, moved=0)


def rows_kernel(at, got, sums, out_ref):
    for s in range(4):
        total = got[s].astype(f32)
        for d in range(1, 4):
            total = total + got[4 * d + s].astype(f32)
        out_ref[:, 384 * s : 384 * (s + 1)] = total.astype(bf16)
    out_ref[:, 1536:1664] = sums[16:32, :].astype(bf16)
    out_ref[:, 1664:1792] = sums[0:16, :].astype(bf16)


def sum_rows(at, got, sums):
    return call(rows_kernel, "sum_rows", sds(16, 1792), at, got, sums, flops=0, moved=0)


def join_kernel(at, mine, theirs, *outs):
    skipped = 4 - len(outs)
    for k, ref in enumerate(outs):
        ref[...] = (mine[k + skipped].astype(f32) + theirs[k + skipped].astype(f32)).astype(bf16)


def join(at, mine, theirs, count=3):
    return call(join_kernel, "join", [sds(*mine.shape[1:])] * count, at, mine, theirs, flops=0, moved=0)


def swap(array, axis):
    return lax.all_to_all(array, axis, split_axis=0, concat_axis=0, tiled=True)


def spread(array, axis, ways):
    return swap(jnp.broadcast_to(array[None], (ways,) + array.shape), axis)


def along_seq(array, k):
    return lax.ppermute(array, "seq", [(i, (i + k) % 4) for i in range(4)])


def along_dp(array, k):
    return lax.ppermute(array, "dp", [(i, (i + k) % 4) for i in range(4)])


def along_x(array, k):
    return lax.ppermute(array, "expert", [(i, (i + 2 * k) % 8) for i in range(8)])


def other_core(array):
    return lax.ppermute(array, "expert", [(i, i ^ 1) for i in range(8)])


def gather_x(array):
    return [array] + [along_x(array, k) for k in range(1, 4)]


def return_x(mine, joined, sums):
    return [mine, joined] + [along_x(sums[k - 1], -k) for k in range(1, 4)]


def after(values, *others):
    return lax.optimization_barrier((values, others))[0]


def shards(tokens, cotangent, doc_lengths, routes, route_rank, w_qkv, w_o, norm_gains, key_gain, w_router, w_in, w_out):
    d_index = lax.axis_index("dp")
    s_index = lax.axis_index("seq")
    e_index = lax.axis_index("expert")
    lengths = doc_lengths[0]
    tok = tokens[0]
    place = jnp.stack([d_index, s_index, e_index]).astype(jnp.int32)
    ends = [lengths[0]]
    for i in range(1, 4):
        ends.append(ends[-1] + lengths[i])
    at = jnp.concatenate([place, jnp.stack(ends)])
    w_send, moe_shard = pack(
        place, w_qkv, w_o, w_router.T, norm_gains, key_gain[None], w_in.reshape(4, 64, 1024), w_out
    )
    w_mine = swap(w_send, GROUP)
    tok_pieces = [tok] + [along_seq(tok, k) for k in range(1, 4)]
    cot = jnp.concatenate(
        [cotangent[0], routes[0].astype(bf16), route_rank[0].astype(bf16)[:, None], jnp.zeros((128, 119), bf16)], axis=1
    )
    cots = gather_x(cot)
    places = d_index * 512 - HALF + jnp.arange(1536, dtype=jnp.int32)
    starts = [jnp.zeros((), jnp.int32)] + ends
    begins = jnp.zeros((1536,), jnp.int32)
    for start in starts:
        begins = jnp.maximum(begins, jnp.where(places >= start, start, 0))
    lane = jnp.arange(128, dtype=jnp.int32)
    frequency = 10000.0 ** (-(lane % 32).astype(f32) / 32)
    angles = (places - begins).astype(f32)[:, None] * frequency[None, :]
    cos = jnp.cos(angles)
    sin = jnp.sin(angles) * jnp.where(lane % 64 < 32, -1.0, 1.0)[None, :]

    moe_shard = after(moe_shard, tok_pieces[1], tok_pieces[3])
    moe_all = lax.all_gather(moe_shard, GROUP, axis=0, tiled=False)
    w_mine, cots = after((w_mine, cots), cos, sin, tok_pieces)
    cots = cots + [other_core(c) for c in cots]
    w_theirs = after(other_core(w_mine), cots)
    n1, raw, kv, parts, small, w_cols, o_pair = project(at, tok_pieces, w_mine, w_theirs)
    up = [(i, i + 1) for i in range(3)]
    down = [(i + 1, i) for i in range(3)]
    kv_before = lax.ppermute(kv, "dp", up)
    kv_after = lax.ppermute(kv, "dp", down)
    parts = swap(parts, GROUP)
    o_parts = gather_x(after(o_pair, kv_before, kv_after))
    *attn_send, attn, qb, kb, vb, lse, uq, uk, qinv, kinv = attend(at, raw, [kv_before, kv, kv_after], parts, small, cos, sin)
    attn_got = [attn_send[0]] + [along_seq(attn_send[k], k) for k in range(1, 4)]
    middle, n2, inverse = make_middle(at, tok, attn_got, o_parts, small)
    routed = route(at, after(cots, n2))
    n2s = after(gather_x(n2), routed)
    n2s = n2s + [other_core(n) for n in n2s]
    made = experts(e_index[None].astype(jnp.int32), n2s, *routed, small, moe_all)
    attns = [attn] + [along_seq(attn, k) for k in range(1, 4)]
    made = after(made, attns)
    joined = other_core(made[1])
    sums = join(at, made[0], joined)
    n1_theirs = other_core(after(n1, sums))
    out_joined = other_core(after(made[3], sums))
    out_sums = join(at, made[2], out_joined)
    dn_pieces = after(return_x(made[0], joined, sums), n1_theirs, out_sums)
    moe_own = lax.psum_scatter(made[4].reshape(16 * 384, 1024), GROUP, scatter_dimension=0, tiled=True)
    moe_own = moe_own.reshape(4, 96, 1024).astype(f32)
    in_own = moe_own[:, :64].reshape(4, 64, 2, 512)
    down_own = moe_own[:, 64:]
    middle_grad, *grad_send, base = middle_back(at, dn_pieces, middle, inverse, n2, cot, small, o_parts)
    grad_got = [grad_send[0]] + [along_seq(grad_send[k], k) for k in range(1, 4)]
    out_pieces = [along_x(out_sums[k - 1], -k) for k in range(1, 4)]
    wq, dkv_own, dkv_up, dkv_down, sums = attend_back(at, grad_got, qb, kb, vb, lse, uq, uk, cos, sin, base)
    from_before = lax.ppermute(dkv_up, "dp", up)
    from_after = lax.ppermute(dkv_down, "dp", down)
    sums = swap(after(sums, out_pieces), GROUP)
    o_part = out_grads(at, attns, after(grad_got, wq))
    output = middle + made[2][0].astype(f32) + out_joined[0].astype(f32)
    for piece in out_pieces:
        output = output + piece.astype(f32)
    output = output.astype(bf16)
    done = finish(
        at, wq, dkv_own, from_before, from_after, sums, uq, uk, qinv, kinv, small, cos, sin, w_cols
    )
    dn1_pieces = [done[0]] + [along_seq(done[k], k) for k in range(1, 4)]
    keep, send, summed = done[4:]
    o_theirs = other_core(after(o_part, send))
    parts = weight_grads(at, after(n1, output), n1_theirs, keep, other_core(send), o_part, o_theirs)
    halves = chip_sum(at, [parts[0]] + [along_x(parts[k], k) for k in range(1, 4)])
    halves = swap(halves, GROUP)
    input_grad = input_back(at, dn1_pieces, tok, middle_grad, small)
    own = sum_rows(at, after(halves, in_own, down_own, input_grad), summed)
    pieces = gather_x(jnp.concatenate([own, other_core(own)], axis=1))
    qkv_own, o_own, gains_own, key_own, router_own = last(at, pieces, w_qkv, norm_gains)
    return (output[None], input_grad[None], qkv_own, o_own, gains_own, key_own[0], router_own.T, in_own, down_own)


def solution(mesh):
    both = P("expert", GROUP, None)
    rows = P(GROUP, None)
    return jax.shard_map(
        shards,
        mesh=mesh,
        in_specs=(
            both,
            both,
            P("expert", None),
            both,
            P("expert", GROUP),
            rows,
            rows,
            P(None, GROUP),
            P(GROUP),
            rows,
            P("expert", GROUP, None, None),
            P("expert", GROUP, None),
        ),
        out_specs=(
            both,
            both,
            rows,
            rows,
            P(None, GROUP),
            P(GROUP),
            rows,
            P("expert", GROUP, None, None),
            P("expert", GROUP, None),
        ),
        check_vma=False,
    )
```

```python
import jax
import jax.numpy as jnp
from jax import lax
from jax.experimental import pallas as pl
from jax.experimental.pallas import tpu as pltpu
from jax.sharding import PartitionSpec as P

HEADS = 16
KV_HEADS = 8
HEAD_DIM = 64
TOPK = 8
HALF = 512
CAP = 40
PAIR = 2 * CAP
ROWS = 8 * CAP
VMEM_BYTES = 64 * 1024 * 1024

GROUP = ("dp", "seq")
ALL = ("dp", "seq", "expert")
epsilon = 1e-05
highest = lax.Precision.HIGHEST
bf16 = jnp.bfloat16
f32 = jnp.float32


def dot(a, b, dims, **kw):
    return lax.dot_general(a, b, ((dims[0], dims[1]), ((), ())), preferred_element_type=f32, **kw)


def call(kernel, name, out_shape, *args, flops=10**8, scratch=(), moved=10**6, middle=(), stepped={}):
    whole = lambda a: pl.BlockSpec(a.shape, lambda _: (0,) * len(a.shape))
    specs = [pl.BlockSpec(memory_space=pltpu.SMEM)] + [whole(a) for a in args[1:]]
    for i in middle:
        specs[i] = pl.BlockSpec((512, 128), lambda _: (1, 0))
    for i, spec in stepped.items():
        specs[i] = spec
    return pl.pallas_call(
        kernel,
        grid=(1,),
        in_specs=specs,
        out_specs=jax.tree.map(whole, out_shape),
        out_shape=out_shape,
        scratch_shapes=list(scratch),
        compiler_params=pltpu.CompilerParams(vmem_limit_bytes=VMEM_BYTES),
        cost_estimate=pl.CostEstimate(flops=flops, bytes_accessed=moved, transcendentals=0),
        name=name,
    )(*args)


def sds(*shape, dtype=bf16):
    return jax.ShapeDtypeStruct(shape, dtype)


def block(index):
    return pl.ds(pl.multiple_of(index * 128, 128), 128)


def column(row):
    return jnp.broadcast_to(row, (128, 128)).T


def partner(x):
    lane = lax.broadcasted_iota(jnp.int32, x.shape, 1)
    return jnp.where(lane % 64 < 32, pltpu.roll(x, 96, 1), pltpu.roll(x, 32, 1))


def row_sums(x):
    ones = jnp.ones((8, x.shape[1]), f32)
    return dot(ones, x, ((1,), (1,)), precision=highest)[0:1]


def project_kernel(at, t0, t1, t2, t3, mine, theirs, n1_ref, raw_ref, kv_ref, parts_ref, small_ref, w_ref, o_ref, rows):
    s = at[1]
    even = lax.rem(at[2], 2) == 0
    here, there = mine[:, :, :256].reshape(1024, 256), theirs[:, :, :256].reshape(1024, 256)
    w_ref[:, :256] = jnp.where(even, here, there)
    w_ref[:, 256:] = jnp.where(even, there, here)
    o_ref[:, :128] = mine[:, :, 384:].reshape(1024, 128)
    o_ref[:, 128:] = theirs[:, :, 384:].reshape(1024, 128)
    w = w_ref[...]
    lane = lax.broadcasted_iota(jnp.int32, (48, 128), 1)
    for i in range(8):
        low, high = mine[2 * i, :48, 256:384].astype(f32), mine[2 * i + 1, :48, 256:384].astype(f32)
        small_ref[:, 128 * i : 128 * (i + 1)] = jnp.where(lane < 64, low, pltpu.roll(high, 64, 1))
    gain = small_ref[32:33, :]
    for ds, t in enumerate((t0, t1, t2, t3)):
        x = t[...].astype(f32)
        low = (x * lax.rsqrt(jnp.mean(x * x, axis=1, keepdims=True) + epsilon) * gain).astype(bf16)
        turned = low.astype(f32).T.astype(bf16)
        raw = dot(low, w, ((1,), (0,)))
        place = lax.rem(s - ds + 4, 4)
        n1_ref[:, block(place)] = turned
        raw_ref[block(place), :] = raw
        kv_ref[block(place), :] = raw[:, 256:].astype(bf16)
        rows[pl.ds(place, 1), :] = row_sums(raw[:, :256] * raw[:, :256])
        rows[pl.ds(place + 4, 1), :] = row_sums(raw[:, 256:384] * raw[:, 256:384])
    parts_ref[...] = jnp.broadcast_to(rows[...][None], (16, 8, 128))
    start = pl.multiple_of(s * 256, 256)
    chunk = small_ref[35:36, pl.ds(start, 256)]
    at_row = lax.broadcasted_iota(jnp.int32, (256, 128), 0)
    at_col = lax.broadcasted_iota(jnp.int32, (256, 128), 1)
    pick = jnp.where(at_row == 64 * (at_col // 32) + at_col % 32, 1.0, 0.0)
    small_ref[40:41, 0:256] = small_ref[34:35, pl.ds(start, 256)]
    small_ref[40:41, 256:384] = dot(jnp.broadcast_to(chunk, (8, 256)), pick, ((1,), (0,)), precision=highest)[0:1]


def project(at, pieces, mine, theirs):
    return call(
        project_kernel,
        "project",
        [
            sds(1024, 512),
            sds(512, 512, dtype=f32),
            sds(512, 256),
            sds(16, 8, 128, dtype=f32),
            sds(48, 1024, dtype=f32),
            sds(1024, 512),
            sds(1024, 256),
        ],
        at,
        *pieces,
        mine,
        theirs,
        flops=8 * 10**9,
        scratch=[pltpu.VMEM((8, 128), f32)],
    )


def document_of(places, at):
    found = jnp.zeros(places.shape, f32)
    for i in range(4):
        found = found + jnp.where(places >= at[3 + i], 1.0, 0.0)
    return jnp.where((places >= 0) & (places < 2048), found, -1.0)


def mark_documents(at, docs):
    docs[...] = document_of(at[0] * 512 - HALF + lax.broadcasted_iota(jnp.int32, (1536, 128), 0), at)
    apart = lax.broadcasted_iota(jnp.int32, (1152, 128), 0) - lax.broadcasted_iota(jnp.int32, (1152, 128), 1)
    return jnp.where((apart >= 0) & (apart < 2 * HALF), 0.0, -1e30)


def seen_bias(at, b, docs, near):
    first = at[0] * 512 + 128 * b
    query_doc = document_of(first + lax.broadcasted_iota(jnp.int32, (1, 128), 1), at)
    return jnp.where(docs[128 * b : 128 * b + 1152, :] == query_doc, near, -1e30)


def stacked_heads(tile, kh):
    lane = lax.broadcasted_iota(jnp.int32, (128, 128), 1)
    mine = (lane < 64) if kh == 0 else (lane >= 64)
    other = pltpu.roll(tile, 64, 1)
    first, second = (tile, other) if kh == 0 else (other, tile)
    return jnp.concatenate([jnp.where(mine, first, 0.0), jnp.where(mine, second, 0.0)], axis=0).astype(bf16)


def attend_kernel(at, raw, kv0, kv1, kv2, parts, small, cos, sin, p0, p1, p2, p3, attn, qb, kb, vb, lse, uq, uk, qinv, kinv, vt, docs):
    d = at[0]
    near = mark_documents(at, docs)
    for i in range(12):
        there = jnp.clip(d - 1 + i // 4, 0, 3)
        row = parts[4 * there][4 + i % 4 : 5 + i % 4]
        for s in range(1, 4):
            row = row + parts[4 * there + s][4 + i % 4 : 5 + i % 4]
        inverse = column(lax.rsqrt(row * (1.0 / 512) + epsilon))
        span = slice(128 * i, 128 * (i + 1))
        part = slice(128 * (i % 4), 128 * (i % 4 + 1))
        kv = (kv0, kv1, kv2)[i // 4]
        unit = kv[part, :128].astype(f32) * inverse
        key = unit * small[40:41, 256:384]
        uk[span, :] = unit
        kb[span, :] = (key * cos[span, :] + partner(key) * sin[span, :]).astype(bf16)
        value = kv[part, 128:]
        vb[span, :] = value
        vt[:, span] = value.T
        if i // 4 == 1:
            kinv[part, :] = inverse
            row = parts[4 * d][i % 4 : i % 4 + 1]
            for s in range(1, 4):
                row = row + parts[4 * d + s][i % 4 : i % 4 + 1]
            inverse = column(lax.rsqrt(row * (1.0 / 1024) + epsilon))
            qinv[part, :] = inverse
            for m in range(2):
                lanes = slice(128 * m, 128 * (m + 1))
                unit = raw[part, lanes] * inverse
                uq[part, lanes] = unit
                query = unit * small[40:41, lanes]
                qb[part, lanes] = (query * cos[span, :] + partner(query) * sin[span, :]).astype(bf16)
    for b in range(4):
        bias = seen_bias(at, b, docs, near)
        bias = jnp.concatenate([bias, bias], axis=1)
        window = slice(128 * b, 128 * b + 1152)
        for kh in range(2):
            lanes = slice(128 * kh, 128 * (kh + 1))
            heads = stacked_heads(qb[128 * b : 128 * (b + 1), lanes].astype(f32), kh)
            scores = dot(kb[window, :], heads, ((1,), (1,))) * 0.125 + bias
            top = jnp.max(scores, axis=0, keepdims=True)
            weights = jnp.exp(scores - top)
            total = jnp.sum(weights, axis=0, keepdims=True)
            lse[2 * b + kh : 2 * b + kh + 1, :] = top + jnp.log(total)
            mixed = dot(vt[64 * kh : 64 * kh + 64, window], weights.astype(bf16), ((1,), (0,))) / total
            tile = jnp.concatenate([mixed[:, :128], mixed[:, 128:]], axis=0).T
            attn[b, :, lanes] = tile.astype(bf16)
    for k, ref in enumerate((p0, p1, p2, p3)):
        ref[...] = attn[lax.rem(at[1] + k, 4)]


def attend(at, raw, kvs, parts, small, cos, sin):
    return call(
        attend_kernel,
        "attend",
        [sds(128, 256)] * 4
        + [
            sds(4, 128, 256),
            sds(512, 256),
            sds(1536, 128),
            sds(1536, 128),
            sds(8, 256, dtype=f32),
            sds(512, 256, dtype=f32),
            sds(1536, 128, dtype=f32),
            sds(512, 128, dtype=f32),
            sds(512, 128, dtype=f32),
        ],
        at,
        raw,
        *kvs,
        parts,
        small,
        cos,
        sin,
        flops=15 * 10**9,
        scratch=[pltpu.VMEM((128, 1536), bf16), pltpu.VMEM((1536, 128), f32)],
    )


def attend_back_kernel(
    at, g0, g1, g2, g3, qb, kb, vb, lse, uq, uk, cos, sin, base, wq, dkv_own, dkv_up, dkv_down, sums, kt, dk, dv, qgain, qrows, got, docs
):
    near = mark_documents(at, docs)
    for k, ref in enumerate((g0, g1, g2, g3)):
        got[lax.rem(at[1] - k + 4, 4)] = ref[...]
    for i in range(12):
        span = slice(128 * i, 128 * (i + 1))
        kt[:, span] = kb[span, :].T
    dk[...] = jnp.zeros_like(dk)
    dv[...] = jnp.zeros_like(dv)
    qgain[...] = jnp.zeros_like(qgain)
    for b in range(4):
        bias = seen_bias(at, b, docs, near)
        bias = jnp.concatenate([bias, bias], axis=1)
        window = slice(128 * b, 128 * b + 1152)
        own = slice(128 * b, 128 * (b + 1))
        table = slice(HALF + 128 * b, HALF + 128 * (b + 1))
        total = jnp.zeros((128, 1), f32)
        for kh in range(2):
            lanes = slice(128 * kh, 128 * (kh + 1))
            query = qb[own, lanes].astype(f32)
            heads = stacked_heads(query, kh)
            grads = stacked_heads(got[b, :, lanes].astype(f32), kh)
            scores = dot(kb[window, :], heads, ((1,), (1,))) * 0.125 + bias
            probs = jnp.exp(scores - lse[2 * b + kh : 2 * b + kh + 1, :])
            prob_grad = dot(vb[window, :], grads, ((1,), (1,)))
            centre = jnp.sum(probs * prob_grad, axis=0, keepdims=True)
            score_grad = (probs * (prob_grad - centre)).astype(bf16)
            dv[window, :] += dot(probs.astype(bf16), grads, ((1,), (0,)))
            dk[window, :] += dot(score_grad, heads, ((1,), (0,))) * 0.125
            flat = dot(kt[64 * kh : 64 * kh + 64, window], score_grad, ((1,), (0,))) * 0.125
            dq = jnp.concatenate([flat[:, :128], flat[:, 128:]], axis=0).T.astype(bf16).astype(f32)
            total = total + jnp.sum(dq * query, axis=1, keepdims=True)
            turned = dq * cos[table, :] - partner(dq) * sin[table, :]
            wq[own, lanes] = turned
            qgain[0:1, lanes] += jnp.sum(turned * uq[own, lanes], axis=0, keepdims=True)
        qrows[b : b + 1, :] = jnp.broadcast_to(total, (128, 128)).T[0:1]
    kgain = jnp.zeros((1, 128), f32)
    krows = []
    for i in range(12):
        span = slice(128 * i, 128 * (i + 1))
        part = slice(128 * (i % 4), 128 * (i % 4 + 1))
        grad = dk[span, :]
        spot = jnp.sum(grad * kb[span, :].astype(f32), axis=1, keepdims=True)
        krows.append(jnp.broadcast_to(spot, (128, 128)).T[0:1])
        turned = grad * cos[span, :] - partner(grad) * sin[span, :]
        kgain = kgain + jnp.sum(turned * uk[span, :], axis=0, keepdims=True)
        target = (dkv_down, dkv_own, dkv_up)[i // 4]
        target[part, :128] = grad.astype(target.dtype)
        target[part, 128:] = dv[span, :].astype(target.dtype)
    lane = lax.broadcasted_iota(jnp.int32, (1, 128), 1)
    none = jnp.zeros((6, 128), f32)
    for there in range(4):
        here = jnp.where(at[0] == there, 1.0, 0.0)
        mine = jnp.where(at[1] == there, 1.0, 0.0)
        rows = [qrows[0:4, :] * here]
        for i in range(4):
            row = jnp.zeros((1, 128), f32)
            for part in range(3):
                row = row + krows[4 * part + i] * jnp.where(at[0] - 1 + part == there, 1.0, 0.0)
            rows.append(row)
        for s in range(4):
            q_tile = qgain[0:1, 128 * (s // 2) : 128 * (s // 2 + 1)]
            if s % 2:
                q_tile = pltpu.roll(q_tile, 64, 1)
            k_tile = pltpu.roll(kgain, (64 - 32 * s) % 128, 1)
            gains = jnp.where(lane < 64, q_tile, jnp.where(lane < 96, k_tile, 0.0)) * mine
            more = base[4 * there + s]
            sums[4 * there + s] = jnp.concatenate(rows + [gains, more[0:1], none, more[8:24]], axis=0).astype(bf16)


def attend_back(at, gots, qb, kb, vb, lse, uq, uk, cos, sin, base):
    return call(
        attend_back_kernel,
        "attend_back",
        [
            sds(512, 256, dtype=f32),
            sds(512, 256, dtype=f32),
            sds(512, 256),
            sds(512, 256),
            sds(16, 32, 128),
        ],
        at,
        *gots,
        qb,
        kb,
        vb,
        lse,
        uq,
        uk,
        cos,
        sin,
        base,
        flops=30 * 10**9,
        scratch=[
            pltpu.VMEM((128, 1536), bf16),
            pltpu.VMEM((1536, 128), f32),
            pltpu.VMEM((1536, 128), f32),
            pltpu.VMEM((8, 256), f32),
            pltpu.VMEM((8, 128), f32),
            pltpu.VMEM((4, 128, 512), bf16),
            pltpu.VMEM((1536, 128), f32),
        ],
    )


def route_kernel(at, *refs):
    place_ref, used_ref, gs_ref = refs[8:]
    ids = lax.broadcasted_iota(jnp.int32, (32, 128), 0) + 4 * at[2]
    ids = jnp.where(ids >= 32, ids - 32, ids).astype(f32)
    slot = lax.broadcasted_iota(jnp.int32, (CAP, 128), 0).astype(f32)
    empty = jnp.zeros((CAP, 128), f32)
    hits = []
    for j, ref in enumerate(refs[:8]):
        meta = ref[:, 1024:].astype(f32)
        turned = meta.T
        used = turned[0:1] == ids
        for k in range(1, TOPK):
            used = used | (turned[k : k + 1] == ids)
        used_ref[j] = jnp.where(used, 1.0, 0.0)
        earlier = jnp.where(meta[:, 8:9] < turned[8:9], 1.0, 0.0).astype(bf16)
        before = dot(jnp.where(used, 1.0, 0.0).astype(bf16), earlier, ((1,), (0,)))
        spot = jnp.where(used & (before < CAP), before, 1000.0)
        hits.append([jnp.where(slot == spot[l : l + 1], 1.0, 0.0) for l in range(4)])
    for p in range(4):
        rows = []
        for l in range(4):
            rows.append(jnp.concatenate([hits[2 * p][l], empty], axis=1))
            rows.append(jnp.concatenate([empty, hits[2 * p + 1][l]], axis=1))
        chosen = jnp.concatenate(rows, axis=0).astype(bf16)
        place_ref[p] = chosen
        both = jnp.concatenate([refs[2 * p][:, :1024], refs[2 * p + 1][:, :1024]], axis=0)
        ups = dot(chosen, both, ((1,), (0,))).astype(bf16)
        for l in range(4):
            gs_ref[l, PAIR * p : PAIR * (p + 1), :] = ups[PAIR * l : PAIR * (l + 1)]


def route(at, cots):
    return call(
        route_kernel,
        "route",
        [sds(4, 4 * PAIR, 256), sds(8, 32, 128, dtype=f32), sds(4, ROWS, 1024)],
        at,
        *cots,
        flops=0,
        moved=0,
    )


def expert_step(where_ref, *refs):
    n2_refs = refs[0:8]
    place, used_ref, gs, small, weights = refs[8:13]
    results, grads_ref = refs[13:17], refs[17]
    xs, gate, ys, dxs, dgs, held = refs[18:24]
    staged, load_sems, store_sems = refs[24:28], refs[28], refs[29]
    dn_refs = tuple(ref.at[i] for ref in staged[:2] for i in range(4))
    out_refs = tuple(ref.at[i] for ref in staged[2:] for i in range(4))
    step = pl.program_id(0)
    slot = lax.rem(step, 2)
    load = lambda l, s: pltpu.make_async_copy(weights.at[:, l], held.at[s], load_sems.at[s])
    stores = [pltpu.make_async_copy(staged[i], results[i], store_sems.at[i]) for i in range(4)]

    @pl.when(step == 0)
    def _():
        load(0, 0).start()
        load(1, 1).start()
        router_t = small[0:32, :].astype(bf16)
        back = lax.rem(32 - 4 * where_ref[0], 32)
        for p in range(4):
            both = jnp.concatenate([n2_refs[2 * p][...], n2_refs[2 * p + 1][...]], axis=0)
            used = jnp.concatenate([used_ref[2 * p], used_ref[2 * p + 1]], axis=1) > 0.5
            logits = pltpu.roll(dot(router_t, both, ((1,), (1,))), back, 0)
            masked = jnp.where(used, logits, -1e30)
            grown = jnp.where(used, jnp.exp(masked - jnp.max(masked, axis=0, keepdims=True)), 0.0)
            gates = grown / jnp.sum(grown, axis=0, keepdims=True)
            chosen = place[p]
            rows = dot(chosen, both, ((1,), (0,))).astype(bf16)
            hit = chosen.astype(f32)
            span = slice(PAIR * p, PAIR * (p + 1))
            for l in range(4):
                part = slice(PAIR * l, PAIR * (l + 1))
                share = jnp.sum(hit[part] * gates[l : l + 1], axis=1, keepdims=True)
                gate[l, span, :] = jnp.broadcast_to(share, (PAIR, 128))
                xs[l, span, :] = rows[part]

    load(step, slot).wait()
    w_in = held[slot, :, :64, :].reshape(1024, 1024)
    w_out = held[slot, :, 64:, :].reshape(512, 1024)
    x = xs[step]
    both = dot(x, w_in, ((1,), (0,)))
    gate_part, up_part = both[:, :512], both[:, 512:]
    sig = jax.nn.sigmoid(gate_part)
    silu = gate_part * sig
    hidden = (silu * up_part).astype(bf16)
    g = gs[0].astype(f32)
    share = gate[step][:, 0:1]
    dy = (g * share).astype(bf16)
    dh = dot(dy, w_out, ((1,), (1,)))
    dgu = jnp.concatenate(
        [dh * up_part * (sig * (1.0 + gate_part * (1.0 - sig))), dh * silu], axis=1
    ).astype(bf16)
    dxs[step] = dot(dgu, w_in, ((1,), (1,))).astype(bf16)
    y = dot(hidden, w_out, ((1,), (0,))).astype(bf16).astype(f32)
    ys[step] = (y * share).astype(bf16)
    lane = lax.broadcasted_iota(jnp.int32, (ROWS, 128), 1)
    dgate = jnp.sum(g * y, axis=1, keepdims=True)
    dgs[step] = jnp.where(lane == 4 * where_ref[0] + step, dgate, 0.0).astype(bf16)

    @pl.when(step == 3)
    def _():
        for p in range(4):
            chosen = place[p]
            span = slice(PAIR * p, PAIR * (p + 1))
            for source, targets, lo, hi in ((dxs, dn_refs, 0, 1024), (dgs, dn_refs, 1024, 1152), (ys, out_refs, 0, 1024)):
                stacked = jnp.concatenate([source[l, span, :] for l in range(4)], axis=0)
                total = dot(chosen, stacked, ((0,), (0,))).astype(bf16)
                targets[2 * p][:, lo:hi] = total[:128]
                targets[2 * p + 1][:, lo:hi] = total[128:]
        for store in stores:
            store.start()

    @pl.when(step < 2)
    def _():
        load(step + 2, slot).start()

    grads_ref[:, 0, :64, :] = dot(x, dgu, ((0,), (0,))).astype(bf16).reshape(16, 64, 1024)
    grads_ref[:, 0, 64:, :] = dot(hidden, dy, ((0,), (0,))).astype(bf16).reshape(16, 32, 1024)

    @pl.when(step == 3)
    def _():
        for store in stores:
            store.wait()


def experts(e_index, n2s, place, used, gs, small, weights):
    whole = lambda *s: pl.BlockSpec(s, lambda i, *_: (0,) * len(s))
    each = lambda cols: pl.BlockSpec((1, ROWS, cols), lambda i, *_: (i, 0, 0))
    owned = pl.BlockSpec((16, 1, 96, 1024), lambda i, *_: (0, i, 0, 0))
    shape = lambda *s: jax.ShapeDtypeStruct(s, bf16)
    return pl.pallas_call(
        expert_step,
        grid_spec=pltpu.PrefetchScalarGridSpec(
            num_scalar_prefetch=1,
            grid=(4,),
            in_specs=[whole(128, 1024)] * 8
            + [
                whole(4, 4 * PAIR, 256),
                whole(8, 32, 128),
                each(1024),
                whole(48, 1024),
                pl.BlockSpec(memory_space=pl.ANY),
            ],
            out_specs=[pl.BlockSpec(memory_space=pl.ANY)] * 4 + [owned],
            scratch_shapes=[
                pltpu.VMEM((4, ROWS, 1024), bf16),
                pltpu.VMEM((4, ROWS, 128), f32),
                pltpu.VMEM((4, ROWS, 1024), bf16),
                pltpu.VMEM((4, ROWS, 1024), bf16),
                pltpu.VMEM((4, ROWS, 128), bf16),
                pltpu.VMEM((2, 16, 96, 1024), bf16),
                pltpu.VMEM((4, 128, 1152), bf16),
                pltpu.VMEM((4, 128, 1152), bf16),
                pltpu.VMEM((4, 128, 1024), bf16),
                pltpu.VMEM((4, 128, 1024), bf16),
                pltpu.SemaphoreType.DMA((2,)),
                pltpu.SemaphoreType.DMA((4,)),
            ],
        ),
        out_shape=[shape(4, 128, 1152)] * 2
        + [shape(4, 128, 1024)] * 2
        + [shape(16, 4, 96, 1024)],
        compiler_params=pltpu.CompilerParams(vmem_limit_bytes=VMEM_BYTES),
        cost_estimate=pl.CostEstimate(flops=28 * 10**9, bytes_accessed=40 * 10**6, transcendentals=10**6),
        name="experts",
    )(e_index, *n2s, place, used, gs, small, weights)


def split(x):
    high = x.astype(bf16)
    return high, (x - high.astype(f32)).astype(bf16)


def o_pieces(at, refs):
    core = lax.rem(at[2], 2)
    for k, ref in enumerate(refs):
        chip = lax.rem(at[2] // 2 - k + 4, 4)
        yield block(2 * chip + core), ref[:, :128]
        yield block(2 * chip + 1 - core), ref[:, 128:]


def quarter(index):
    return pl.ds(pl.multiple_of(256 * index, 256), 256)


def middle_kernel(at, tok, a0, a1, a2, a3, o0, o1, o2, o3, small, middle_ref, low_ref, inverse_ref, rows_ref):
    for k, ref in enumerate((a0, a1, a2, a3)):
        rows_ref[:, quarter(lax.rem(at[1] - k + 4, 4))] = ref[...]
    rows = rows_ref[...]
    for lanes, piece in o_pieces(at, (o0, o1, o2, o3)):
        middle_ref[:, lanes] = tok[:, lanes].astype(f32) + dot(rows, piece, ((1,), (0,)))
    total = middle_ref[...]
    inverse = lax.rsqrt(jnp.mean(total * total, axis=1, keepdims=True) + epsilon)
    low_ref[...] = (total * inverse * small[33:34]).astype(bf16)
    inverse_ref[...] = jnp.broadcast_to(inverse, (128, 128))


def make_middle(at, tok, attns, parts, small):
    return call(
        middle_kernel,
        "middle",
        [sds(128, 1024, dtype=f32), sds(128, 1024), sds(128, 128, dtype=f32)],
        at,
        tok,
        *attns,
        *parts,
        small,
        flops=6 * 10**9,
        scratch=[pltpu.VMEM((128, 1024), bf16)],
    )


def middle_back_kernel(
    at, p0a, p0b, p1, p2, p3, middle, inverse_ref, low, cot, small, o0, o1, o2, o3, grad_ref, s0, s1, s2, s3, sums_ref, branch_ref, back_ref
):
    total = p0a[0].astype(f32) + p0b[0].astype(f32) + p1[...].astype(f32) + p2[...].astype(f32) + p3[...].astype(f32)
    dgates = total[:, 1024:1056]
    router_t = small[0:32].astype(bf16)
    logits = dot(low[...], router_t, ((1,), (1,)))
    ids = lax.broadcasted_iota(jnp.int32, (128, 32), 1).astype(f32)
    named = cot[:, 1024:].astype(f32)
    used = named[:, 0:1] == ids
    for k in range(1, TOPK):
        used = used | (named[:, k : k + 1] == ids)
    masked = jnp.where(used, logits, -1e30)
    grown = jnp.where(used, jnp.exp(masked - jnp.max(masked, axis=1, keepdims=True)), 0.0)
    gates = grown / jnp.sum(grown, axis=1, keepdims=True)
    logit_grad = gates * (dgates - jnp.sum(gates * dgates, axis=1, keepdims=True))
    high, rest = split(logit_grad)
    dn2 = total[:, :1024] + dot(high, router_t, ((1,), (0,))) + dot(rest, router_t, ((1,), (0,)))
    inverse = inverse_ref[:, 0:1]
    unit = middle[...] * inverse
    scaled = dn2 * small[33:34]
    grad = cot[:, :1024].astype(f32) + inverse * (scaled - unit * jnp.mean(scaled * unit, axis=1, keepdims=True))
    grad_ref[...] = grad
    branch = grad.astype(bf16)
    branch_ref[...] = branch
    back = jnp.zeros((128, 1024), f32)
    for lanes, piece in o_pieces(at, (o0, o1, o2, o3)):
        back = back + dot(branch_ref[:, lanes], piece, ((1,), (1,)))
    back_ref[...] = back.astype(bf16)
    for k, ref in enumerate((s0, s1, s2, s3)):
        lanes = quarter(lax.rem(at[1] + k, 4))
        ref[:, 0:256] = back_ref[:, lanes]
        ref[:, 256:512] = branch_ref[:, lanes]
    routers = dot(high, low[...], ((0,), (0,))) + dot(rest, low[...], ((0,), (0,)))
    second = jnp.sum(dn2 * unit, axis=0, keepdims=True)
    lane = lax.broadcasted_iota(jnp.int32, (16, 128), 1)
    for i in range(16):
        lanes = slice(128 * (i // 2), 128 * (i // 2 + 1))
        upper, lower, row = routers[0:16, lanes], routers[16:32, lanes], second[:, lanes]
        if i % 2 == 0:
            tile = jnp.where(lane < 64, upper, pltpu.roll(lower, 64, 1))
        else:
            tile = jnp.where(lane < 64, pltpu.roll(upper, 64, 1), lower)
            row = pltpu.roll(row, 64, 1)
        sums_ref[i] = jnp.concatenate([row, jnp.zeros((7, 128), f32), tile], axis=0)


def middle_back(at, pieces, middle, inverse, low, cot, small, parts):
    return call(
        middle_back_kernel,
        "middle_back",
        [sds(128, 1024, dtype=f32)] + [sds(128, 512)] * 4 + [sds(16, 24, 128, dtype=f32)],
        at,
        *pieces,
        middle,
        inverse,
        low,
        cot,
        small,
        *parts,
        flops=12 * 10**9,
        scratch=[pltpu.VMEM((128, 1024), bf16)] * 2,
    )


def out_grad_kernel(at, a0, a1, a2, a3, g0, g1, g2, g3, out_ref, cols):
    for k, ref in enumerate((g0, g1, g2, g3)):
        cols[block(lax.rem(at[1] - k + 4, 4)), :] = ref[:, 256:512]
    for k, part in enumerate((a0, a1, a2, a3)):
        rows = jnp.concatenate([part[i] for i in range(4)], axis=0)
        out_ref[quarter(lax.rem(at[1] - k + 4, 4)), :] = dot(rows, cols[...], ((0,), (0,))).astype(bf16)


def out_grads(at, attns, gots):
    scratch = [pltpu.VMEM((512, 256), bf16)]
    return call(out_grad_kernel, "out_grads", sds(1024, 256), at, *attns, *gots, flops=0, moved=0, scratch=scratch)


def finish_kernel(
    at, wq, own, up, down, sums, uq, uk, qinv, kinv, small, cos, sin, w_ref,
    dn0, dn1, dn2, dn3, keep_ref, send_ref, sums_ref, dqkv,
):
    got = sums[0].astype(f32)
    for i in range(1, 16):
        got = got + sums[i].astype(f32)
    sums_ref[...] = got
    for i in range(4):
        part = slice(128 * i, 128 * (i + 1))
        q_mean = column(got[i : i + 1]) * (1.0 / 1024)
        for m in range(2):
            lanes = slice(128 * m, 128 * (m + 1))
            grad = wq[part, lanes] * small[40:41, lanes] - uq[part, lanes] * q_mean
            dqkv[part, lanes] = (qinv[part, :] * grad).astype(bf16)
        total = own[part, :] + up[part, :].astype(f32) + down[part, :].astype(f32)
        dk = total[:, :128].astype(bf16).astype(f32)
        turned = dk * cos[part, :] - partner(dk) * sin[part, :]
        k_mean = column(got[4 + i : 5 + i]) * (1.0 / 512)
        grad = turned * small[40:41, 256:384] - uk[part, :] * k_mean
        dqkv[part, 256:384] = (kinv[part, :] * grad).astype(bf16)
        dqkv[part, 384:512] = total[:, 128:].astype(bf16)
    w = w_ref[...]
    for k, ref in enumerate((dn0, dn1, dn2, dn3)):
        ref[...] = dot(dqkv[block(lax.rem(at[1] + k, 4)), :], w, ((1,), (1,))).astype(bf16)
    even = lax.rem(at[2], 2) == 0
    left = dqkv[:, :384]
    right = jnp.concatenate([dqkv[:, 384:], jnp.zeros((512, 256), bf16)], axis=1)
    keep_ref[...] = jnp.where(even, left, right)
    send_ref[...] = jnp.where(even, right, left)


def finish(at, wq, own, up, down, sums, uq, uk, qinv, kinv, small, cos, sin, w_cols):
    return call(
        finish_kernel,
        "finish",
        [sds(128, 1024)] * 4 + [sds(512, 384)] * 2 + [sds(sums.shape[1], 128, dtype=f32)],
        at, wq, own, up, down, sums, uq, uk, qinv, kinv, small, cos, sin, w_cols,
        middle=(7, 11, 12),
        flops=10 * 10**9,
        scratch=[pltpu.VMEM((512, 512), bf16)],
    )


def weight_kernel(at, n1, n1_theirs, keep, got, o_part, o_theirs, r0, r1, r2, r3, grads):
    total = dot(n1[...], keep[...], ((1,), (0,))) + dot(n1_theirs[...], got[...], ((1,), (0,)))
    odd = lax.rem(at[2], 2).astype(f32)
    outs = (o_part[...].astype(f32) + o_theirs[...].astype(f32)) * odd
    grads[:, :, :128] = total[:, :128].astype(bf16).reshape(16, 64, 128)
    grads[:, :, 128:] = (total[:, 128:] + outs).astype(bf16).reshape(16, 64, 256)
    for k, ref in enumerate((r0, r1, r2, r3)):
        ref[...] = grads[:, pl.ds(pl.multiple_of(16 * lax.rem(at[2] // 2 + k, 4), 16), 16), :]


def weight_grads(at, *args):
    return call(
        weight_kernel,
        "weight_grads",
        [sds(16, 16, 384)] * 4,
        at,
        *args,
        flops=8 * 10**9,
        scratch=[pltpu.VMEM((16, 64, 384), bf16)],
    )


def input_kernel(at, p0, p1, p2, p3, tok, grad_ref, small, out_ref):
    dn1 = p0[...].astype(f32) + p1[...].astype(f32) + p2[...].astype(f32) + p3[...].astype(f32)
    x = tok[...].astype(f32)
    inverse = lax.rsqrt(jnp.mean(x * x, axis=1, keepdims=True) + epsilon)
    unit = x * inverse
    scaled = dn1 * small[32:33]
    out_ref[...] = grad_ref[...] + inverse * (scaled - unit * jnp.mean(scaled * unit, axis=1, keepdims=True))


def input_back(at, pieces, tok, grad, small):
    return call(input_kernel, "input_back", sds(128, 1024, dtype=f32), at, *pieces, tok, grad, small, flops=0, moved=0)


def pack_kernel(at, w_ref, o_ref, router_ref, gain_ref, key_ref, in_ref, down_ref, out_ref, moe_ref):
    moe_ref[:, :64, :] = in_ref[...]
    moe_ref[:, 64:, :] = down_ref[...]
    even = lax.rem(at[2], 2) == 0
    piece = o_ref[:, block(at[2])]
    key = jnp.concatenate([key_ref[...].astype(f32), jnp.zeros((1, 32), f32)], axis=1)
    extra = jnp.concatenate(
        [router_ref[...].astype(f32), gain_ref[...].astype(f32), key, jnp.zeros((28, 64), f32)], axis=0
    )
    extra = jnp.concatenate([extra, jnp.zeros((64, 64), f32)], axis=1).astype(bf16)
    for s in range(4):
        queries = w_ref[:, 256 * s : 256 * (s + 1)]
        keys = w_ref[:, 1024 + 128 * s : 1024 + 128 * (s + 1)]
        values = w_ref[:, 1536 + 128 * s : 1536 + 128 * (s + 1)]
        half = jnp.where(even, queries, jnp.concatenate([keys, values], axis=1))
        for d in range(4):
            out_ref[4 * d + s, :, 0:256] = half
            out_ref[4 * d + s, :, 256:384] = extra
            out_ref[4 * d + s, :, 384:512] = piece


def pack(at, *args):
    return call(pack_kernel, "pack", [sds(16, 64, 512), sds(4, 96, 1024)], at, *args, flops=10**9)


def last_kernel(at, *refs):
    pieces, (w_ref, gain_ref, qkv_ref, o_ref, gains_ref, key_ref, router_ref) = refs[:4], refs[4:]
    even = lax.rem(at[2], 2) == 0
    sums = jnp.zeros((16, 256), f32)
    for k in range(4):
        rows = pl.ds(pl.multiple_of(16 * lax.rem(at[2] // 2 - k + 4, 4), 16), 16)
        mine, theirs = pieces[k][:, :1792].astype(f32), pieces[k][:, 1792:].astype(f32)
        sums = sums + mine[:, 1536:] + theirs[:, 1536:]
        first, later = jnp.where(even, mine, theirs), jnp.where(even, theirs, mine)
        for s in range(4):
            lanes = 384 * s
            qkv_ref[rows, 256 * s : 256 * (s + 1)] = first[:, lanes : lanes + 256]
            qkv_ref[rows, 1024 + 128 * s : 1024 + 128 * (s + 1)] = first[:, lanes + 256 : lanes + 384]
            qkv_ref[rows, 1536 + 128 * s : 1536 + 128 * (s + 1)] = later[:, lanes : lanes + 128]
            o_ref[rows, 256 * s : 256 * (s + 1)] = later[:, lanes + 128 : lanes + 384]
    first_gain = row_sums(qkv_ref[...] * w_ref[...].astype(f32)) / gain_ref[...].astype(f32)[0:1, :]
    gains_ref[0:1, :] = first_gain
    gains_ref[1:2, :] = sums[9:10, 128:192]
    gains_ref[2:3, :] = sums[8:9, 128:192]
    key_ref[...] = sums[8:9, 192:224]
    router_ref[...] = jnp.concatenate([sums[:, :64], sums[:, 64:128]], axis=0)


def last(at, pieces, w_qkv, norm_gains):
    return call(
        last_kernel,
        "last",
        [
            sds(64, 2048, dtype=f32),
            sds(64, 1024, dtype=f32),
            sds(3, 64, dtype=f32),
            sds(1, 32, dtype=f32),
            sds(32, 64, dtype=f32),
        ],
        at, *pieces, w_qkv, norm_gains,
    )


def chip_kernel(at, r0, r1, r2, r3, out_ref):
    total = r0[...].astype(f32) + r1[...].astype(f32) + r2[...].astype(f32) + r3[...].astype(f32)
    out_ref[...] = total.astype(bf16)


def chip_sum(at, pieces):
    return call(chip_kernel, "chip_sum", sds(*pieces[0].shape), at, *pieces, flops=0, moved=0)


def rows_kernel(at, got, sums, out_ref):
    for s in range(4):
        total = got[s].astype(f32)
        for d in range(1, 4):
            total = total + got[4 * d + s].astype(f32)
        out_ref[:, 384 * s : 384 * (s + 1)] = total.astype(bf16)
    out_ref[:, 1536:1664] = sums[16:32, :].astype(bf16)
    out_ref[:, 1664:1792] = sums[0:16, :].astype(bf16)


def sum_rows(at, got, sums):
    return call(rows_kernel, "sum_rows", sds(16, 1792), at, got, sums, flops=0, moved=0)


def join_kernel(at, *refs):
    for k in range(3):
        refs[6 + k][...] = (refs[k][0].astype(f32) + refs[3 + k][0].astype(f32)).astype(bf16)


def join(at, mine, theirs):
    shape = mine.shape[1:]
    specs = [pl.BlockSpec((1,) + shape, lambda _, k=k: (k, 0, 0)) for k in range(1, 4)] * 2
    args = [mine] * 3 + [theirs] * 3
    stepped = dict(enumerate(specs, 1))
    return call(join_kernel, "join", [sds(*shape)] * 3, at, *args, stepped=stepped, flops=0, moved=0)


def swap(array, axis):
    return lax.all_to_all(array, axis, split_axis=0, concat_axis=0, tiled=True)


def spread(array, axis, ways):
    return swap(jnp.broadcast_to(array[None], (ways,) + array.shape), axis)


def along_seq(array, k):
    return lax.ppermute(array, "seq", [(i, (i + k) % 4) for i in range(4)])


def along_dp(array, k):
    return lax.ppermute(array, "dp", [(i, (i + k) % 4) for i in range(4)])


def along_x(array, k):
    return lax.ppermute(array, "expert", [(i, (i + 2 * k) % 8) for i in range(8)])


def other_core(array):
    return lax.ppermute(array, "expert", [(i, i ^ 1) for i in range(8)])


def gather_x(array):
    return [array] + [along_x(array, k) for k in range(1, 4)]


def return_x(mine, joined, sums):
    return [mine, joined] + [along_x(sums[k - 1], -k) for k in range(1, 4)]


def after(values, *others):
    return lax.optimization_barrier((values, others))[0]


def shards(tokens, cotangent, doc_lengths, routes, route_rank, w_qkv, w_o, norm_gains, key_gain, w_router, w_in, w_out):
    d_index = lax.axis_index("dp")
    s_index = lax.axis_index("seq")
    e_index = lax.axis_index("expert")
    lengths = doc_lengths[0]
    tok = tokens[0]
    place = jnp.stack([d_index, s_index, e_index]).astype(jnp.int32)
    ends = [lengths[0]]
    for i in range(1, 4):
        ends.append(ends[-1] + lengths[i])
    at = jnp.concatenate([place, jnp.stack(ends)])
    w_send, moe_shard = pack(
        place, w_qkv, w_o, w_router.T, norm_gains, key_gain[None], w_in.reshape(4, 64, 1024), w_out
    )
    w_mine = swap(w_send, GROUP)
    tok_pieces = [tok] + [along_seq(tok, k) for k in range(1, 4)]
    cot = jnp.concatenate(
        [cotangent[0], routes[0].astype(bf16), route_rank[0].astype(bf16)[:, None], jnp.zeros((128, 119), bf16)], axis=1
    )
    cots = gather_x(cot)
    places = d_index * 512 - HALF + jnp.arange(1536, dtype=jnp.int32)
    starts = [jnp.zeros((), jnp.int32)] + ends
    begins = jnp.zeros((1536,), jnp.int32)
    for start in starts:
        begins = jnp.maximum(begins, jnp.where(places >= start, start, 0))
    lane = jnp.arange(128, dtype=jnp.int32)
    frequency = 10000.0 ** (-(lane % 32).astype(f32) / 32)
    angles = (places - begins).astype(f32)[:, None] * frequency[None, :]
    cos = jnp.cos(angles)
    sin = jnp.sin(angles) * jnp.where(lane % 64 < 32, -1.0, 1.0)[None, :]

    moe_shard = after(moe_shard, tok_pieces[1], tok_pieces[3])
    moe_all = lax.all_gather(moe_shard, GROUP, axis=0, tiled=False)
    w_mine, cots = after((w_mine, cots), cos, sin, tok_pieces)
    cots = cots + [other_core(c) for c in cots]
    w_theirs = after(other_core(w_mine), cots)
    n1, raw, kv, parts, small, w_cols, o_pair = project(at, tok_pieces, w_mine, w_theirs)
    up = [(i, i + 1) for i in range(3)]
    down = [(i + 1, i) for i in range(3)]
    kv_before = lax.ppermute(kv, "dp", up)
    kv_after = lax.ppermute(kv, "dp", down)
    parts = swap(parts, GROUP)
    o_parts = gather_x(after(o_pair, kv_before, kv_after))
    *attn_send, attn, qb, kb, vb, lse, uq, uk, qinv, kinv = attend(at, raw, [kv_before, kv, kv_after], parts, small, cos, sin)
    attn_got = [attn_send[0]] + [along_seq(attn_send[k], k) for k in range(1, 4)]
    middle, n2, inverse = make_middle(at, tok, attn_got, o_parts, small)
    routed = route(at, after(cots, n2))
    n2s = after(gather_x(n2), routed)
    n2s = n2s + [other_core(n) for n in n2s]
    made = experts(e_index[None].astype(jnp.int32), n2s, *routed, small, moe_all)
    attns = [attn] + [along_seq(attn, k) for k in range(1, 4)]
    made = after(made, attns)
    joined = other_core(made[1])
    sums = join(at, made[0], joined)
    n1_theirs = other_core(after(n1, sums))
    out_joined = other_core(after(made[3], sums))
    out_sums = join(at, made[2], out_joined)
    dn_pieces = after(return_x(made[0], joined, sums), n1_theirs, out_sums)
    moe_own = lax.psum_scatter(made[4].reshape(16 * 384, 1024), GROUP, scatter_dimension=0, tiled=True)
    moe_own = moe_own.reshape(4, 96, 1024).astype(f32)
    in_own = moe_own[:, :64].reshape(4, 64, 2, 512)
    down_own = moe_own[:, 64:]
    middle_grad, *grad_send, base = middle_back(at, dn_pieces, middle, inverse, n2, cot, small, o_parts)
    grad_got = [grad_send[0]] + [along_seq(grad_send[k], k) for k in range(1, 4)]
    out_pieces = [along_x(out_sums[k - 1], -k) for k in range(1, 4)]
    wq, dkv_own, dkv_up, dkv_down, sums = attend_back(at, grad_got, qb, kb, vb, lse, uq, uk, cos, sin, base)
    from_before = lax.ppermute(dkv_up, "dp", up)
    from_after = lax.ppermute(dkv_down, "dp", down)
    sums = swap(after(sums, out_pieces), GROUP)
    o_part = out_grads(at, attns, after(grad_got, wq))
    output = middle + made[2][0].astype(f32) + out_joined[0].astype(f32)
    for piece in out_pieces:
        output = output + piece.astype(f32)
    output = output.astype(bf16)
    done = finish(
        at, wq, dkv_own, from_before, from_after, sums, uq, uk, qinv, kinv, small, cos, sin, w_cols
    )
    dn1_pieces = [done[0]] + [along_seq(done[k], k) for k in range(1, 4)]
    keep, send, summed = done[4:]
    o_theirs = other_core(after(o_part, send))
    parts = weight_grads(at, after(n1, output), n1_theirs, keep, other_core(send), o_part, o_theirs)
    halves = chip_sum(at, [parts[0]] + [along_x(parts[k], k) for k in range(1, 4)])
    halves = swap(halves, GROUP)
    input_grad = input_back(at, dn1_pieces, tok, middle_grad, small)
    own = sum_rows(at, after(halves, in_own, down_own, input_grad), summed)
    pieces = gather_x(jnp.concatenate([own, other_core(own)], axis=1))
    qkv_own, o_own, gains_own, key_own, router_own = last(at, pieces, w_qkv, norm_gains)
    return (output[None], input_grad[None], qkv_own, o_own, gains_own, key_own[0], router_own.T, in_own, down_own)


def solution(mesh):
    both = P("expert", GROUP, None)
    rows = P(GROUP, None)
    return jax.shard_map(
        shards,
        mesh=mesh,
        in_specs=(
            both,
            both,
            P("expert", None),
            both,
            P("expert", GROUP),
            rows,
            rows,
            P(None, GROUP),
            P(GROUP),
            rows,
            P("expert", GROUP, None, None),
            P("expert", GROUP, None),
        ),
        out_specs=(
            both,
            both,
            rows,
            rows,
            P(None, GROUP),
            P(GROUP),
            rows,
            P("expert", GROUP, None, None),
            P("expert", GROUP, None),
        ),
        check_vma=False,
    )
```

```python
import jax
import jax.numpy as jnp
from jax import lax
from jax.experimental import pallas as pl
from jax.experimental.pallas import tpu as pltpu
from jax.sharding import PartitionSpec as P

HEADS = 16
KV_HEADS = 8
HEAD_DIM = 64
TOPK = 8
HALF = 512
CAP = 40
PAIR = 2 * CAP
ROWS = 8 * CAP
VMEM_BYTES = 64 * 1024 * 1024

GROUP = ("dp", "seq")
ALL = ("dp", "seq", "expert")
epsilon = 1e-05
highest = lax.Precision.HIGHEST
bf16 = jnp.bfloat16
f32 = jnp.float32


def dot(a, b, dims, **kw):
    return lax.dot_general(a, b, ((dims[0], dims[1]), ((), ())), preferred_element_type=f32, **kw)


def call(kernel, name, out_shape, *args, flops=10**8, scratch=(), moved=10**6, middle=(), stepped={}):
    whole = lambda a: pl.BlockSpec(a.shape, lambda _: (0,) * len(a.shape))
    specs = [pl.BlockSpec(memory_space=pltpu.SMEM)] + [whole(a) for a in args[1:]]
    for i in middle:
        specs[i] = pl.BlockSpec((512, 128), lambda _: (1, 0))
    for i, spec in stepped.items():
        specs[i] = spec
    return pl.pallas_call(
        kernel,
        grid=(1,),
        in_specs=specs,
        out_specs=jax.tree.map(whole, out_shape),
        out_shape=out_shape,
        scratch_shapes=list(scratch),
        compiler_params=pltpu.CompilerParams(vmem_limit_bytes=VMEM_BYTES),
        cost_estimate=pl.CostEstimate(flops=flops, bytes_accessed=moved, transcendentals=0),
        name=name,
    )(*args)


def sds(*shape, dtype=bf16):
    return jax.ShapeDtypeStruct(shape, dtype)


def block(index):
    return pl.ds(pl.multiple_of(index * 128, 128), 128)


def column(row):
    return jnp.broadcast_to(row, (128, 128)).T


def partner(x):
    lane = lax.broadcasted_iota(jnp.int32, x.shape, 1)
    return jnp.where(lane % 64 < 32, pltpu.roll(x, 96, 1), pltpu.roll(x, 32, 1))


def row_sums(x):
    ones = jnp.ones((8, x.shape[1]), f32)
    return dot(ones, x, ((1,), (1,)), precision=highest)[0:1]


def project_kernel(at, t0, t1, t2, t3, mine, theirs, n1_ref, raw_ref, kv_ref, parts_ref, small_ref, w_ref, o_ref, rows):
    s = at[1]
    even = lax.rem(at[2], 2) == 0
    here, there = mine[:, :, :256].reshape(1024, 256), theirs[:, :, :256].reshape(1024, 256)
    w_ref[:, :256] = jnp.where(even, here, there)
    w_ref[:, 256:] = jnp.where(even, there, here)
    o_ref[:, :128] = mine[:, :, 384:].reshape(1024, 128)
    o_ref[:, 128:] = theirs[:, :, 384:].reshape(1024, 128)
    w = w_ref[...]
    lane = lax.broadcasted_iota(jnp.int32, (48, 128), 1)
    for i in range(8):
        low, high = mine[2 * i, :48, 256:384].astype(f32), mine[2 * i + 1, :48, 256:384].astype(f32)
        small_ref[:, 128 * i : 128 * (i + 1)] = jnp.where(lane < 64, low, pltpu.roll(high, 64, 1))
    gain = small_ref[32:33, :]
    for ds, t in enumerate((t0, t1, t2, t3)):
        x = t[...].astype(f32)
        low = (x * lax.rsqrt(jnp.mean(x * x, axis=1, keepdims=True) + epsilon) * gain).astype(bf16)
        turned = low.astype(f32).T.astype(bf16)
        raw = dot(low, w, ((1,), (0,)))
        place = lax.rem(s - ds + 4, 4)
        n1_ref[:, block(place)] = turned
        raw_ref[block(place), :] = raw
        kv_ref[block(place), :] = raw[:, 256:].astype(bf16)
        rows[pl.ds(place, 1), :] = row_sums(raw[:, :256] * raw[:, :256])
        rows[pl.ds(place + 4, 1), :] = row_sums(raw[:, 256:384] * raw[:, 256:384])
    parts_ref[...] = jnp.broadcast_to(rows[...][None], (16, 8, 128))
    start = pl.multiple_of(s * 256, 256)
    chunk = small_ref[35:36, pl.ds(start, 256)]
    at_row = lax.broadcasted_iota(jnp.int32, (256, 128), 0)
    at_col = lax.broadcasted_iota(jnp.int32, (256, 128), 1)
    pick = jnp.where(at_row == 64 * (at_col // 32) + at_col % 32, 1.0, 0.0)
    small_ref[40:41, 0:256] = small_ref[34:35, pl.ds(start, 256)]
    small_ref[40:41, 256:384] = dot(jnp.broadcast_to(chunk, (8, 256)), pick, ((1,), (0,)), precision=highest)[0:1]


def project(at, pieces, mine, theirs):
    return call(
        project_kernel,
        "project",
        [
            sds(1024, 512),
            sds(512, 512, dtype=f32),
            sds(512, 256),
            sds(16, 8, 128, dtype=f32),
            sds(48, 1024, dtype=f32),
            sds(1024, 512),
            sds(1024, 256),
        ],
        at,
        *pieces,
        mine,
        theirs,
        flops=8 * 10**9,
        scratch=[pltpu.VMEM((8, 128), f32)],
    )


def document_of(places, at):
    found = jnp.zeros(places.shape, f32)
    for i in range(4):
        found = found + jnp.where(places >= at[3 + i], 1.0, 0.0)
    return jnp.where((places >= 0) & (places < 2048), found, -1.0)


def mark_documents(at, docs):
    docs[...] = document_of(at[0] * 512 - HALF + lax.broadcasted_iota(jnp.int32, (1536, 128), 0), at)
    apart = lax.broadcasted_iota(jnp.int32, (1152, 128), 0) - lax.broadcasted_iota(jnp.int32, (1152, 128), 1)
    return jnp.where((apart >= 0) & (apart < 2 * HALF), 0.0, -1e30)


def seen_bias(at, b, docs, near):
    first = at[0] * 512 + 128 * b
    query_doc = document_of(first + lax.broadcasted_iota(jnp.int32, (1, 128), 1), at)
    return jnp.where(docs[128 * b : 128 * b + 1152, :] == query_doc, near, -1e30)


def stacked_heads(tile, kh):
    lane = lax.broadcasted_iota(jnp.int32, (128, 128), 1)
    mine = (lane < 64) if kh == 0 else (lane >= 64)
    other = pltpu.roll(tile, 64, 1)
    first, second = (tile, other) if kh == 0 else (other, tile)
    return jnp.concatenate([jnp.where(mine, first, 0.0), jnp.where(mine, second, 0.0)], axis=0).astype(bf16)


def attend_kernel(at, raw, kv0, kv1, kv2, parts, small, cos, sin, p0, p1, p2, p3, attn, qb, kb, vb, lse, uq, uk, qinv, kinv, vt, docs):
    d = at[0]
    near = mark_documents(at, docs)
    for i in range(12):
        there = jnp.clip(d - 1 + i // 4, 0, 3)
        row = parts[4 * there][4 + i % 4 : 5 + i % 4]
        for s in range(1, 4):
            row = row + parts[4 * there + s][4 + i % 4 : 5 + i % 4]
        inverse = column(lax.rsqrt(row * (1.0 / 512) + epsilon))
        span = slice(128 * i, 128 * (i + 1))
        part = slice(128 * (i % 4), 128 * (i % 4 + 1))
        kv = (kv0, kv1, kv2)[i // 4]
        unit = kv[part, :128].astype(f32) * inverse
        key = unit * small[40:41, 256:384]
        uk[span, :] = unit
        kb[span, :] = (key * cos[span, :] + partner(key) * sin[span, :]).astype(bf16)
        value = kv[part, 128:]
        vb[span, :] = value
        vt[:, span] = value.T
        if i // 4 == 1:
            kinv[part, :] = inverse
            row = parts[4 * d][i % 4 : i % 4 + 1]
            for s in range(1, 4):
                row = row + parts[4 * d + s][i % 4 : i % 4 + 1]
            inverse = column(lax.rsqrt(row * (1.0 / 1024) + epsilon))
            qinv[part, :] = inverse
            for m in range(2):
                lanes = slice(128 * m, 128 * (m + 1))
                unit = raw[part, lanes] * inverse
                uq[part, lanes] = unit
                query = unit * small[40:41, lanes]
                qb[part, lanes] = (query * cos[span, :] + partner(query) * sin[span, :]).astype(bf16)
    for b in range(4):
        bias = seen_bias(at, b, docs, near)
        bias = jnp.concatenate([bias, bias], axis=1)
        window = slice(128 * b, 128 * b + 1152)
        for kh in range(2):
            lanes = slice(128 * kh, 128 * (kh + 1))
            heads = stacked_heads(qb[128 * b : 128 * (b + 1), lanes].astype(f32), kh)
            scores = dot(kb[window, :], heads, ((1,), (1,))) * 0.125 + bias
            top = jnp.max(scores, axis=0, keepdims=True)
            weights = jnp.exp(scores - top)
            total = jnp.sum(weights, axis=0, keepdims=True)
            lse[2 * b + kh : 2 * b + kh + 1, :] = top + jnp.log(total)
            mixed = dot(vt[64 * kh : 64 * kh + 64, window], weights.astype(bf16), ((1,), (0,))) / total
            tile = jnp.concatenate([mixed[:, :128], mixed[:, 128:]], axis=0).T
            attn[b, :, lanes] = tile.astype(bf16)
    for k, ref in enumerate((p0, p1, p2, p3)):
        ref[...] = attn[lax.rem(at[1] + k, 4)]


def attend(at, raw, kvs, parts, small, cos, sin):
    return call(
        attend_kernel,
        "attend",
        [sds(128, 256)] * 4
        + [
            sds(4, 128, 256),
            sds(512, 256),
            sds(1536, 128),
            sds(1536, 128),
            sds(8, 256, dtype=f32),
            sds(512, 256, dtype=f32),
            sds(1536, 128, dtype=f32),
            sds(512, 128, dtype=f32),
            sds(512, 128, dtype=f32),
        ],
        at,
        raw,
        *kvs,
        parts,
        small,
        cos,
        sin,
        flops=15 * 10**9,
        scratch=[pltpu.VMEM((128, 1536), bf16), pltpu.VMEM((1536, 128), f32)],
    )


def attend_back_kernel(
    at, g0, g1, g2, g3, qb, kb, vb, lse, uq, uk, cos, sin, base, wq, dkv_own, dkv_up, dkv_down, sums, kt, dk, dv, qgain, qrows, got, docs
):
    near = mark_documents(at, docs)
    for k, ref in enumerate((g0, g1, g2, g3)):
        got[lax.rem(at[1] - k + 4, 4)] = ref[...]
    for i in range(12):
        span = slice(128 * i, 128 * (i + 1))
        kt[:, span] = kb[span, :].T
    dk[...] = jnp.zeros_like(dk)
    dv[...] = jnp.zeros_like(dv)
    qgain[...] = jnp.zeros_like(qgain)
    for b in range(4):
        bias = seen_bias(at, b, docs, near)
        bias = jnp.concatenate([bias, bias], axis=1)
        window = slice(128 * b, 128 * b + 1152)
        own = slice(128 * b, 128 * (b + 1))
        table = slice(HALF + 128 * b, HALF + 128 * (b + 1))
        total = jnp.zeros((128, 1), f32)
        for kh in range(2):
            lanes = slice(128 * kh, 128 * (kh + 1))
            query = qb[own, lanes].astype(f32)
            heads = stacked_heads(query, kh)
            grads = stacked_heads(got[b, :, lanes].astype(f32), kh)
            scores = dot(kb[window, :], heads, ((1,), (1,))) * 0.125 + bias
            probs = jnp.exp(scores - lse[2 * b + kh : 2 * b + kh + 1, :])
            prob_grad = dot(vb[window, :], grads, ((1,), (1,)))
            centre = jnp.sum(probs * prob_grad, axis=0, keepdims=True)
            score_grad = (probs * (prob_grad - centre)).astype(bf16)
            dv[window, :] += dot(probs.astype(bf16), grads, ((1,), (0,)))
            dk[window, :] += dot(score_grad, heads, ((1,), (0,))) * 0.125
            flat = dot(kt[64 * kh : 64 * kh + 64, window], score_grad, ((1,), (0,))) * 0.125
            dq = jnp.concatenate([flat[:, :128], flat[:, 128:]], axis=0).T.astype(bf16).astype(f32)
            total = total + jnp.sum(dq * query, axis=1, keepdims=True)
            turned = dq * cos[table, :] - partner(dq) * sin[table, :]
            wq[own, lanes] = turned
            qgain[0:1, lanes] += jnp.sum(turned * uq[own, lanes], axis=0, keepdims=True)
        qrows[b : b + 1, :] = jnp.broadcast_to(total, (128, 128)).T[0:1]
    kgain = jnp.zeros((1, 128), f32)
    krows = []
    for i in range(12):
        span = slice(128 * i, 128 * (i + 1))
        part = slice(128 * (i % 4), 128 * (i % 4 + 1))
        grad = dk[span, :]
        spot = jnp.sum(grad * kb[span, :].astype(f32), axis=1, keepdims=True)
        krows.append(jnp.broadcast_to(spot, (128, 128)).T[0:1])
        turned = grad * cos[span, :] - partner(grad) * sin[span, :]
        kgain = kgain + jnp.sum(turned * uk[span, :], axis=0, keepdims=True)
        target = (dkv_down, dkv_own, dkv_up)[i // 4]
        target[part, :128] = grad.astype(target.dtype)
        target[part, 128:] = dv[span, :].astype(target.dtype)
    lane = lax.broadcasted_iota(jnp.int32, (1, 128), 1)
    none = jnp.zeros((6, 128), f32)
    for there in range(4):
        here = jnp.where(at[0] == there, 1.0, 0.0)
        mine = jnp.where(at[1] == there, 1.0, 0.0)
        rows = [qrows[0:4, :] * here]
        for i in range(4):
            row = jnp.zeros((1, 128), f32)
            for part in range(3):
                row = row + krows[4 * part + i] * jnp.where(at[0] - 1 + part == there, 1.0, 0.0)
            rows.append(row)
        for s in range(4):
            q_tile = qgain[0:1, 128 * (s // 2) : 128 * (s // 2 + 1)]
            if s % 2:
                q_tile = pltpu.roll(q_tile, 64, 1)
            k_tile = pltpu.roll(kgain, (64 - 32 * s) % 128, 1)
            gains = jnp.where(lane < 64, q_tile, jnp.where(lane < 96, k_tile, 0.0)) * mine
            more = base[4 * there + s]
            sums[4 * there + s] = jnp.concatenate(rows + [gains, more[0:1], none, more[8:24]], axis=0).astype(bf16)


def attend_back(at, gots, qb, kb, vb, lse, uq, uk, cos, sin, base):
    return call(
        attend_back_kernel,
        "attend_back",
        [
            sds(512, 256, dtype=f32),
            sds(512, 256, dtype=f32),
            sds(512, 256),
            sds(512, 256),
            sds(16, 32, 128),
        ],
        at,
        *gots,
        qb,
        kb,
        vb,
        lse,
        uq,
        uk,
        cos,
        sin,
        base,
        flops=30 * 10**9,
        scratch=[
            pltpu.VMEM((128, 1536), bf16),
            pltpu.VMEM((1536, 128), f32),
            pltpu.VMEM((1536, 128), f32),
            pltpu.VMEM((8, 256), f32),
            pltpu.VMEM((8, 128), f32),
            pltpu.VMEM((4, 128, 512), bf16),
            pltpu.VMEM((1536, 128), f32),
        ],
    )


def route_kernel(at, *refs):
    place_ref, used_ref, gs_ref = refs[8:]
    ids = lax.broadcasted_iota(jnp.int32, (32, 128), 0) + 4 * at[2]
    ids = jnp.where(ids >= 32, ids - 32, ids).astype(f32)
    slot = lax.broadcasted_iota(jnp.int32, (CAP, 128), 0).astype(f32)
    empty = jnp.zeros((CAP, 128), f32)
    hits = []
    for j, ref in enumerate(refs[:8]):
        meta = ref[:, 1024:].astype(f32)
        turned = meta.T
        used = turned[0:1] == ids
        for k in range(1, TOPK):
            used = used | (turned[k : k + 1] == ids)
        used_ref[j] = jnp.where(used, 1.0, 0.0)
        earlier = jnp.where(meta[:, 8:9] < turned[8:9], 1.0, 0.0).astype(bf16)
        before = dot(jnp.where(used, 1.0, 0.0).astype(bf16), earlier, ((1,), (0,)))
        spot = jnp.where(used & (before < CAP), before, 1000.0)
        hits.append([jnp.where(slot == spot[l : l + 1], 1.0, 0.0) for l in range(4)])
    for p in range(4):
        rows = []
        for l in range(4):
            rows.append(jnp.concatenate([hits[2 * p][l], empty], axis=1))
            rows.append(jnp.concatenate([empty, hits[2 * p + 1][l]], axis=1))
        chosen = jnp.concatenate(rows, axis=0).astype(bf16)
        place_ref[p] = chosen
        both = jnp.concatenate([refs[2 * p][:, :1024], refs[2 * p + 1][:, :1024]], axis=0)
        ups = dot(chosen, both, ((1,), (0,))).astype(bf16)
        for l in range(4):
            gs_ref[l, PAIR * p : PAIR * (p + 1), :] = ups[PAIR * l : PAIR * (l + 1)]


def route(at, cots):
    return call(
        route_kernel,
        "route",
        [sds(4, 4 * PAIR, 256), sds(8, 32, 128, dtype=f32), sds(4, ROWS, 1024)],
        at,
        *cots,
        flops=0,
        moved=0,
    )


def expert_step(where_ref, *refs):
    n2_refs = refs[0:8]
    place, used_ref, gs, small, weights = refs[8:13]
    results, grads_ref = refs[13:17], refs[17]
    xs, gate, ys, dxs, dgs, held = refs[18:24]
    staged, load_sems, store_sems = refs[24:28], refs[28], refs[29]
    dn_refs = tuple(ref.at[i] for ref in staged[:2] for i in range(4))
    out_refs = tuple(ref.at[i] for ref in staged[2:] for i in range(4))
    step = pl.program_id(0)
    slot = lax.rem(step, 2)
    load = lambda l, s: pltpu.make_async_copy(weights.at[:, l], held.at[s], load_sems.at[s])
    stores = [pltpu.make_async_copy(staged[i], results[i], store_sems.at[i]) for i in range(4)]

    @pl.when(step == 0)
    def _():
        load(0, 0).start()
        load(1, 1).start()
        router_t = small[0:32, :].astype(bf16)
        back = lax.rem(32 - 4 * where_ref[0], 32)
        for p in range(4):
            both = jnp.concatenate([n2_refs[2 * p][...], n2_refs[2 * p + 1][...]], axis=0)
            used = jnp.concatenate([used_ref[2 * p], used_ref[2 * p + 1]], axis=1) > 0.5
            logits = pltpu.roll(dot(router_t, both, ((1,), (1,))), back, 0)
            masked = jnp.where(used, logits, -1e30)
            grown = jnp.where(used, jnp.exp(masked - jnp.max(masked, axis=0, keepdims=True)), 0.0)
            gates = grown / jnp.sum(grown, axis=0, keepdims=True)
            chosen = place[p]
            rows = dot(chosen, both, ((1,), (0,))).astype(bf16)
            hit = chosen.astype(f32)
            span = slice(PAIR * p, PAIR * (p + 1))
            for l in range(4):
                part = slice(PAIR * l, PAIR * (l + 1))
                share = jnp.sum(hit[part] * gates[l : l + 1], axis=1, keepdims=True)
                gate[l, span, :] = jnp.broadcast_to(share, (PAIR, 128))
                xs[l, span, :] = rows[part]

    load(step, slot).wait()
    w_in = held[slot, :, :64, :].reshape(1024, 1024)
    w_out = held[slot, :, 64:, :].reshape(512, 1024)
    x = xs[step]
    both = dot(x, w_in, ((1,), (0,)))
    gate_part, up_part = both[:, :512], both[:, 512:]
    sig = jax.nn.sigmoid(gate_part)
    silu = gate_part * sig
    hidden = (silu * up_part).astype(bf16)
    g = gs[0].astype(f32)
    share = gate[step][:, 0:1]
    dy = (g * share).astype(bf16)
    dh = dot(dy, w_out, ((1,), (1,)))
    dgu = jnp.concatenate(
        [dh * up_part * (sig * (1.0 + gate_part * (1.0 - sig))), dh * silu], axis=1
    ).astype(bf16)
    dxs[step] = dot(dgu, w_in, ((1,), (1,))).astype(bf16)
    y = dot(hidden, w_out, ((1,), (0,))).astype(bf16).astype(f32)
    ys[step] = (y * share).astype(bf16)
    lane = lax.broadcasted_iota(jnp.int32, (ROWS, 128), 1)
    dgate = jnp.sum(g * y, axis=1, keepdims=True)
    dgs[step] = jnp.where(lane == 4 * where_ref[0] + step, dgate, 0.0).astype(bf16)

    @pl.when(step == 3)
    def _():
        for p in range(4):
            chosen = place[p]
            span = slice(PAIR * p, PAIR * (p + 1))
            for source, targets, lo, hi in ((dxs, dn_refs, 0, 1024), (dgs, dn_refs, 1024, 1152), (ys, out_refs, 0, 1024)):
                stacked = jnp.concatenate([source[l, span, :] for l in range(4)], axis=0)
                total = dot(chosen, stacked, ((0,), (0,))).astype(bf16)
                targets[2 * p][:, lo:hi] = total[:128]
                targets[2 * p + 1][:, lo:hi] = total[128:]
        for store in stores:
            store.start()

    @pl.when(step < 2)
    def _():
        load(step + 2, slot).start()

    grads_ref[:, 0, :64, :] = dot(x, dgu, ((0,), (0,))).astype(bf16).reshape(16, 64, 1024)
    grads_ref[:, 0, 64:, :] = dot(hidden, dy, ((0,), (0,))).astype(bf16).reshape(16, 32, 1024)

    @pl.when(step == 3)
    def _():
        for store in stores:
            store.wait()


def experts(e_index, n2s, place, used, gs, small, weights):
    whole = lambda *s: pl.BlockSpec(s, lambda i, *_: (0,) * len(s))
    each = lambda cols: pl.BlockSpec((1, ROWS, cols), lambda i, *_: (i, 0, 0))
    owned = pl.BlockSpec((16, 1, 96, 1024), lambda i, *_: (0, i, 0, 0))
    shape = lambda *s: jax.ShapeDtypeStruct(s, bf16)
    return pl.pallas_call(
        expert_step,
        grid_spec=pltpu.PrefetchScalarGridSpec(
            num_scalar_prefetch=1,
            grid=(4,),
            in_specs=[whole(128, 1024)] * 8
            + [
                whole(4, 4 * PAIR, 256),
                whole(8, 32, 128),
                each(1024),
                whole(48, 1024),
                pl.BlockSpec(memory_space=pl.ANY),
            ],
            out_specs=[pl.BlockSpec(memory_space=pl.ANY)] * 4 + [owned],
            scratch_shapes=[
                pltpu.VMEM((4, ROWS, 1024), bf16),
                pltpu.VMEM((4, ROWS, 128), f32),
                pltpu.VMEM((4, ROWS, 1024), bf16),
                pltpu.VMEM((4, ROWS, 1024), bf16),
                pltpu.VMEM((4, ROWS, 128), bf16),
                pltpu.VMEM((2, 16, 96, 1024), bf16),
                pltpu.VMEM((4, 128, 1152), bf16),
                pltpu.VMEM((4, 128, 1152), bf16),
                pltpu.VMEM((4, 128, 1024), bf16),
                pltpu.VMEM((4, 128, 1024), bf16),
                pltpu.SemaphoreType.DMA((2,)),
                pltpu.SemaphoreType.DMA((4,)),
            ],
        ),
        out_shape=[shape(4, 128, 1152)] * 2
        + [shape(4, 128, 1024)] * 2
        + [shape(16, 4, 96, 1024)],
        compiler_params=pltpu.CompilerParams(vmem_limit_bytes=VMEM_BYTES),
        cost_estimate=pl.CostEstimate(flops=28 * 10**9, bytes_accessed=40 * 10**6, transcendentals=10**6),
        name="experts",
    )(e_index, *n2s, place, used, gs, small, weights)


def split(x):
    high = x.astype(bf16)
    return high, (x - high.astype(f32)).astype(bf16)


def o_pieces(at, refs):
    core = lax.rem(at[2], 2)
    for k, ref in enumerate(refs):
        chip = lax.rem(at[2] // 2 - k + 4, 4)
        yield block(2 * chip + core), ref[:, :128]
        yield block(2 * chip + 1 - core), ref[:, 128:]


def quarter(index):
    return pl.ds(pl.multiple_of(256 * index, 256), 256)


def middle_kernel(at, tok, a0, a1, a2, a3, o0, o1, o2, o3, small, middle_ref, low_ref, inverse_ref, rows_ref):
    for k, ref in enumerate((a0, a1, a2, a3)):
        rows_ref[:, quarter(lax.rem(at[1] - k + 4, 4))] = ref[...]
    rows = rows_ref[...]
    for lanes, piece in o_pieces(at, (o0, o1, o2, o3)):
        middle_ref[:, lanes] = tok[:, lanes].astype(f32) + dot(rows, piece, ((1,), (0,)))
    total = middle_ref[...]
    inverse = lax.rsqrt(jnp.mean(total * total, axis=1, keepdims=True) + epsilon)
    low_ref[...] = (total * inverse * small[33:34]).astype(bf16)
    inverse_ref[...] = jnp.broadcast_to(inverse, (128, 128))


def make_middle(at, tok, attns, parts, small):
    return call(
        middle_kernel,
        "middle",
        [sds(128, 1024, dtype=f32), sds(128, 1024), sds(128, 128, dtype=f32)],
        at,
        tok,
        *attns,
        *parts,
        small,
        flops=6 * 10**9,
        scratch=[pltpu.VMEM((128, 1024), bf16)],
    )


def middle_back_kernel(
    at, p0a, p0b, p1, p2, p3, middle, inverse_ref, low, cot, small, o0, o1, o2, o3, grad_ref, s0, s1, s2, s3, sums_ref, branch_ref, back_ref
):
    total = p0a[0].astype(f32) + p0b[0].astype(f32) + p1[...].astype(f32) + p2[...].astype(f32) + p3[...].astype(f32)
    dgates = total[:, 1024:1056]
    router_t = small[0:32].astype(bf16)
    logits = dot(low[...], router_t, ((1,), (1,)))
    ids = lax.broadcasted_iota(jnp.int32, (128, 32), 1).astype(f32)
    named = cot[:, 1024:].astype(f32)
    used = named[:, 0:1] == ids
    for k in range(1, TOPK):
        used = used | (named[:, k : k + 1] == ids)
    masked = jnp.where(used, logits, -1e30)
    grown = jnp.where(used, jnp.exp(masked - jnp.max(masked, axis=1, keepdims=True)), 0.0)
    gates = grown / jnp.sum(grown, axis=1, keepdims=True)
    logit_grad = gates * (dgates - jnp.sum(gates * dgates, axis=1, keepdims=True))
    high, rest = split(logit_grad)
    dn2 = total[:, :1024] + dot(high, router_t, ((1,), (0,))) + dot(rest, router_t, ((1,), (0,)))
    inverse = inverse_ref[:, 0:1]
    unit = middle[...] * inverse
    scaled = dn2 * small[33:34]
    grad = cot[:, :1024].astype(f32) + inverse * (scaled - unit * jnp.mean(scaled * unit, axis=1, keepdims=True))
    grad_ref[...] = grad
    branch = grad.astype(bf16)
    branch_ref[...] = branch
    back = jnp.zeros((128, 1024), f32)
    for lanes, piece in o_pieces(at, (o0, o1, o2, o3)):
        back = back + dot(branch_ref[:, lanes], piece, ((1,), (1,)))
    back_ref[...] = back.astype(bf16)
    for k, ref in enumerate((s0, s1, s2, s3)):
        lanes = quarter(lax.rem(at[1] + k, 4))
        ref[:, 0:256] = back_ref[:, lanes]
        ref[:, 256:512] = branch_ref[:, lanes]
    routers = dot(high, low[...], ((0,), (0,))) + dot(rest, low[...], ((0,), (0,)))
    second = jnp.sum(dn2 * unit, axis=0, keepdims=True)
    lane = lax.broadcasted_iota(jnp.int32, (16, 128), 1)
    for i in range(16):
        lanes = slice(128 * (i // 2), 128 * (i // 2 + 1))
        upper, lower, row = routers[0:16, lanes], routers[16:32, lanes], second[:, lanes]
        if i % 2 == 0:
            tile = jnp.where(lane < 64, upper, pltpu.roll(lower, 64, 1))
        else:
            tile = jnp.where(lane < 64, pltpu.roll(upper, 64, 1), lower)
            row = pltpu.roll(row, 64, 1)
        sums_ref[i] = jnp.concatenate([row, jnp.zeros((7, 128), f32), tile], axis=0)


def middle_back(at, pieces, middle, inverse, low, cot, small, parts):
    return call(
        middle_back_kernel,
        "middle_back",
        [sds(128, 1024, dtype=f32)] + [sds(128, 512)] * 4 + [sds(16, 24, 128, dtype=f32)],
        at,
        *pieces,
        middle,
        inverse,
        low,
        cot,
        small,
        *parts,
        flops=12 * 10**9,
        scratch=[pltpu.VMEM((128, 1024), bf16)] * 2,
    )


def out_grad_kernel(at, a0, a1, a2, a3, g0, g1, g2, g3, out_ref, cols):
    for k, ref in enumerate((g0, g1, g2, g3)):
        cols[block(lax.rem(at[1] - k + 4, 4)), :] = ref[:, 256:512]
    for k, part in enumerate((a0, a1, a2, a3)):
        rows = jnp.concatenate([part[i] for i in range(4)], axis=0)
        out_ref[quarter(lax.rem(at[1] - k + 4, 4)), :] = dot(rows, cols[...], ((0,), (0,))).astype(bf16)


def out_grads(at, attns, gots):
    scratch = [pltpu.VMEM((512, 256), bf16)]
    return call(out_grad_kernel, "out_grads", sds(1024, 256), at, *attns, *gots, flops=0, moved=0, scratch=scratch)


def finish_kernel(
    at, wq, own, up, down, sums, uq, uk, qinv, kinv, small, cos, sin, w_ref,
    dn0, dn1, dn2, dn3, keep_ref, send_ref, sums_ref, dqkv,
):
    got = sums[0].astype(f32)
    for i in range(1, 16):
        got = got + sums[i].astype(f32)
    sums_ref[...] = got
    for i in range(4):
        part = slice(128 * i, 128 * (i + 1))
        q_mean = column(got[i : i + 1]) * (1.0 / 1024)
        for m in range(2):
            lanes = slice(128 * m, 128 * (m + 1))
            grad = wq[part, lanes] * small[40:41, lanes] - uq[part, lanes] * q_mean
            dqkv[part, lanes] = (qinv[part, :] * grad).astype(bf16)
        total = own[part, :] + up[part, :].astype(f32) + down[part, :].astype(f32)
        dk = total[:, :128].astype(bf16).astype(f32)
        turned = dk * cos[part, :] - partner(dk) * sin[part, :]
        k_mean = column(got[4 + i : 5 + i]) * (1.0 / 512)
        grad = turned * small[40:41, 256:384] - uk[part, :] * k_mean
        dqkv[part, 256:384] = (kinv[part, :] * grad).astype(bf16)
        dqkv[part, 384:512] = total[:, 128:].astype(bf16)
    w = w_ref[...]
    for k, ref in enumerate((dn0, dn1, dn2, dn3)):
        ref[...] = dot(dqkv[block(lax.rem(at[1] + k, 4)), :], w, ((1,), (1,))).astype(bf16)
    even = lax.rem(at[2], 2) == 0
    left = dqkv[:, :384]
    right = jnp.concatenate([dqkv[:, 384:], jnp.zeros((512, 256), bf16)], axis=1)
    keep_ref[...] = jnp.where(even, left, right)
    send_ref[...] = jnp.where(even, right, left)


def finish(at, wq, own, up, down, sums, uq, uk, qinv, kinv, small, cos, sin, w_cols):
    return call(
        finish_kernel,
        "finish",
        [sds(128, 1024)] * 4 + [sds(512, 384)] * 2 + [sds(sums.shape[1], 128, dtype=f32)],
        at, wq, own, up, down, sums, uq, uk, qinv, kinv, small, cos, sin, w_cols,
        middle=(7, 11, 12),
        flops=10 * 10**9,
        scratch=[pltpu.VMEM((512, 512), bf16)],
    )


def weight_kernel(at, n1, n1_theirs, keep, got, o_part, o_theirs, r0, r1, r2, r3, grads):
    total = dot(n1[...], keep[...], ((1,), (0,))) + dot(n1_theirs[...], got[...], ((1,), (0,)))
    odd = lax.rem(at[2], 2).astype(f32)
    outs = (o_part[...].astype(f32) + o_theirs[...].astype(f32)) * odd
    grads[:, :, :128] = total[:, :128].astype(bf16).reshape(16, 64, 128)
    grads[:, :, 128:] = (total[:, 128:] + outs).astype(bf16).reshape(16, 64, 256)
    for k, ref in enumerate((r0, r1, r2, r3)):
        ref[...] = grads[:, pl.ds(pl.multiple_of(16 * lax.rem(at[2] // 2 + k, 4), 16), 16), :]


def weight_grads(at, *args):
    return call(
        weight_kernel,
        "weight_grads",
        [sds(16, 16, 384)] * 4,
        at,
        *args,
        flops=8 * 10**9,
        scratch=[pltpu.VMEM((16, 64, 384), bf16)],
    )


def input_kernel(at, p0, p1, p2, p3, tok, grad_ref, small, out_ref):
    dn1 = p0[...].astype(f32) + p1[...].astype(f32) + p2[...].astype(f32) + p3[...].astype(f32)
    x = tok[...].astype(f32)
    inverse = lax.rsqrt(jnp.mean(x * x, axis=1, keepdims=True) + epsilon)
    unit = x * inverse
    scaled = dn1 * small[32:33]
    out_ref[...] = grad_ref[...] + inverse * (scaled - unit * jnp.mean(scaled * unit, axis=1, keepdims=True))


def input_back(at, pieces, tok, grad, small):
    return call(input_kernel, "input_back", sds(128, 1024, dtype=f32), at, *pieces, tok, grad, small, flops=0, moved=0)


def pack_kernel(at, w_ref, o_ref, router_ref, gain_ref, key_ref, in_ref, down_ref, out_ref, moe_ref):
    moe_ref[:, :64, :] = in_ref[...]
    moe_ref[:, 64:, :] = down_ref[...]
    even = lax.rem(at[2], 2) == 0
    piece = o_ref[:, block(at[2])]
    key = jnp.concatenate([key_ref[...].astype(f32), jnp.zeros((1, 32), f32)], axis=1)
    extra = jnp.concatenate(
        [router_ref[...].astype(f32), gain_ref[...].astype(f32), key, jnp.zeros((28, 64), f32)], axis=0
    )
    extra = jnp.concatenate([extra, jnp.zeros((64, 64), f32)], axis=1).astype(bf16)
    for s in range(4):
        queries = w_ref[:, 256 * s : 256 * (s + 1)]
        keys = w_ref[:, 1024 + 128 * s : 1024 + 128 * (s + 1)]
        values = w_ref[:, 1536 + 128 * s : 1536 + 128 * (s + 1)]
        half = jnp.where(even, queries, jnp.concatenate([keys, values], axis=1))
        for d in range(4):
            out_ref[4 * d + s, :, 0:256] = half
            out_ref[4 * d + s, :, 256:384] = extra
            out_ref[4 * d + s, :, 384:512] = piece


def pack(at, *args):
    return call(pack_kernel, "pack", [sds(16, 64, 512), sds(4, 96, 1024)], at, *args, flops=10**9)


def last_kernel(at, *refs):
    pieces, (w_ref, gain_ref, qkv_ref, o_ref, gains_ref, key_ref, router_ref) = refs[:4], refs[4:]
    even = lax.rem(at[2], 2) == 0
    sums = jnp.zeros((16, 256), f32)
    for k in range(4):
        rows = pl.ds(pl.multiple_of(16 * lax.rem(at[2] // 2 - k + 4, 4), 16), 16)
        mine, theirs = pieces[k][:, :1792].astype(f32), pieces[k][:, 1792:].astype(f32)
        sums = sums + mine[:, 1536:] + theirs[:, 1536:]
        first, later = jnp.where(even, mine, theirs), jnp.where(even, theirs, mine)
        for s in range(4):
            lanes = 384 * s
            qkv_ref[rows, 256 * s : 256 * (s + 1)] = first[:, lanes : lanes + 256]
            qkv_ref[rows, 1024 + 128 * s : 1024 + 128 * (s + 1)] = first[:, lanes + 256 : lanes + 384]
            qkv_ref[rows, 1536 + 128 * s : 1536 + 128 * (s + 1)] = later[:, lanes : lanes + 128]
            o_ref[rows, 256 * s : 256 * (s + 1)] = later[:, lanes + 128 : lanes + 384]
    first_gain = row_sums(qkv_ref[...] * w_ref[...].astype(f32)) / gain_ref[...].astype(f32)[0:1, :]
    gains_ref[0:1, :] = first_gain
    gains_ref[1:2, :] = sums[9:10, 128:192]
    gains_ref[2:3, :] = sums[8:9, 128:192]
    key_ref[...] = sums[8:9, 192:224]
    router_ref[...] = jnp.concatenate([sums[:, :64], sums[:, 64:128]], axis=0)


def last(at, pieces, w_qkv, norm_gains):
    return call(
        last_kernel,
        "last",
        [
            sds(64, 2048, dtype=f32),
            sds(64, 1024, dtype=f32),
            sds(3, 64, dtype=f32),
            sds(1, 32, dtype=f32),
            sds(32, 64, dtype=f32),
        ],
        at, *pieces, w_qkv, norm_gains,
    )


def chip_kernel(at, r0, r1, r2, r3, out_ref):
    total = r0[...].astype(f32) + r1[...].astype(f32) + r2[...].astype(f32) + r3[...].astype(f32)
    out_ref[...] = total.astype(bf16)


def chip_sum(at, pieces):
    return call(chip_kernel, "chip_sum", sds(*pieces[0].shape), at, *pieces, flops=0, moved=0)


def rows_kernel(at, got, sums, out_ref):
    for s in range(4):
        total = got[s].astype(f32)
        for d in range(1, 4):
            total = total + got[4 * d + s].astype(f32)
        out_ref[:, 384 * s : 384 * (s + 1)] = total.astype(bf16)
    out_ref[:, 1536:1664] = sums[16:32, :].astype(bf16)
    out_ref[:, 1664:1792] = sums[0:16, :].astype(bf16)


def sum_rows(at, got, sums):
    return call(rows_kernel, "sum_rows", sds(16, 1792), at, got, sums, flops=0, moved=0)


def join_kernel(at, *refs):
    for k in range(3):
        refs[6 + k][...] = (refs[k][0].astype(f32) + refs[3 + k][0].astype(f32)).astype(bf16)


def join(at, mine, theirs):
    shape = mine.shape[1:]
    specs = [pl.BlockSpec((1,) + shape, lambda _, k=k: (k, 0, 0)) for k in range(1, 4)] * 2
    args = [mine] * 3 + [theirs] * 3
    stepped = dict(enumerate(specs, 1))
    return call(join_kernel, "join", [sds(*shape)] * 3, at, *args, stepped=stepped, flops=0, moved=0)


def swap(array, axis):
    return lax.all_to_all(array, axis, split_axis=0, concat_axis=0, tiled=True)


def spread(array, axis, ways):
    return swap(jnp.broadcast_to(array[None], (ways,) + array.shape), axis)


def along_seq(array, k):
    return lax.ppermute(array, "seq", [(i, (i + k) % 4) for i in range(4)])


def along_dp(array, k):
    return lax.ppermute(array, "dp", [(i, (i + k) % 4) for i in range(4)])


def along_x(array, k):
    return lax.ppermute(array, "expert", [(i, (i + 2 * k) % 8) for i in range(8)])


def other_core(array):
    return lax.ppermute(array, "expert", [(i, i ^ 1) for i in range(8)])


def gather_x(array):
    return [array] + [along_x(array, k) for k in range(1, 4)]


def return_x(mine, joined, sums):
    return [mine, joined] + [along_x(sums[k - 1], -k) for k in range(1, 4)]


def after(values, *others):
    return lax.optimization_barrier((values, others))[0]


def shards(tokens, cotangent, doc_lengths, routes, route_rank, w_qkv, w_o, norm_gains, key_gain, w_router, w_in, w_out):
    d_index = lax.axis_index("dp")
    s_index = lax.axis_index("seq")
    e_index = lax.axis_index("expert")
    lengths = doc_lengths[0]
    tok = tokens[0]
    place = jnp.stack([d_index, s_index, e_index]).astype(jnp.int32)
    ends = [lengths[0]]
    for i in range(1, 4):
        ends.append(ends[-1] + lengths[i])
    at = jnp.concatenate([place, jnp.stack(ends)])
    w_send, moe_shard = pack(
        place, w_qkv, w_o, w_router.T, norm_gains, key_gain[None], w_in.reshape(4, 64, 1024), w_out
    )
    w_mine = swap(w_send, GROUP)
    tok_pieces = [tok] + [along_seq(tok, k) for k in range(1, 4)]
    cot = jnp.concatenate(
        [cotangent[0], routes[0].astype(bf16), route_rank[0].astype(bf16)[:, None], jnp.zeros((128, 119), bf16)], axis=1
    )
    cots = gather_x(cot)
    places = d_index * 512 - HALF + jnp.arange(1536, dtype=jnp.int32)
    starts = [jnp.zeros((), jnp.int32)] + ends
    begins = jnp.zeros((1536,), jnp.int32)
    for start in starts:
        begins = jnp.maximum(begins, jnp.where(places >= start, start, 0))
    lane = jnp.arange(128, dtype=jnp.int32)
    frequency = 10000.0 ** (-(lane % 32).astype(f32) / 32)
    angles = (places - begins).astype(f32)[:, None] * frequency[None, :]
    cos = jnp.cos(angles)
    sin = jnp.sin(angles) * jnp.where(lane % 64 < 32, -1.0, 1.0)[None, :]

    moe_shard = after(moe_shard, tok_pieces[1], tok_pieces[3])
    moe_all = lax.all_gather(moe_shard, GROUP, axis=0, tiled=False)
    w_mine, cots = after((w_mine, cots), cos, sin, tok_pieces)
    cots = cots + [other_core(c) for c in cots]
    w_theirs = after(other_core(w_mine), cots)
    n1, raw, kv, parts, small, w_cols, o_pair = project(at, tok_pieces, w_mine, w_theirs)
    up = [(i, i + 1) for i in range(3)]
    down = [(i + 1, i) for i in range(3)]
    kv_before = lax.ppermute(kv, "dp", up)
    kv_after = lax.ppermute(kv, "dp", down)
    parts = swap(parts, GROUP)
    o_parts = gather_x(after(o_pair, kv_before))
    *attn_send, attn, qb, kb, vb, lse, uq, uk, qinv, kinv = attend(at, raw, [kv_before, kv, kv_after], parts, small, cos, sin)
    attn_got = [attn_send[0]] + [along_seq(attn_send[k], k) for k in range(1, 4)]
    middle, n2, inverse = make_middle(at, tok, attn_got, o_parts, small)
    routed = route(at, after(cots, n2))
    n2s = after(gather_x(n2), routed)
    n2s = n2s + [other_core(n) for n in n2s]
    made = experts(e_index[None].astype(jnp.int32), n2s, *routed, small, moe_all)
    attns = [attn] + [along_seq(attn, k) for k in range(1, 4)]
    made = after(made, attns)
    joined = other_core(made[1])
    sums = join(at, made[0], joined)
    n1_theirs = other_core(after(n1, sums))
    out_joined = other_core(after(made[3], sums))
    out_sums = join(at, made[2], out_joined)
    dn_pieces = after(return_x(made[0], joined, sums), n1_theirs, out_sums)
    moe_own = lax.psum_scatter(made[4].reshape(16 * 384, 1024), GROUP, scatter_dimension=0, tiled=True)
    moe_own = moe_own.reshape(4, 96, 1024).astype(f32)
    in_own = moe_own[:, :64].reshape(4, 64, 2, 512)
    down_own = moe_own[:, 64:]
    middle_grad, *grad_send, base = middle_back(at, dn_pieces, middle, inverse, n2, cot, small, o_parts)
    grad_got = [grad_send[0]] + [along_seq(grad_send[k], k) for k in range(1, 4)]
    out_pieces = [along_x(out_sums[k - 1], -k) for k in range(1, 4)]
    wq, dkv_own, dkv_up, dkv_down, sums = attend_back(at, grad_got, qb, kb, vb, lse, uq, uk, cos, sin, base)
    from_before = lax.ppermute(dkv_up, "dp", up)
    from_after = lax.ppermute(dkv_down, "dp", down)
    sums = swap(after(sums, out_pieces), GROUP)
    o_part = out_grads(at, attns, after(grad_got, wq))
    output = middle + made[2][0].astype(f32) + out_joined[0].astype(f32)
    for piece in out_pieces:
        output = output + piece.astype(f32)
    output = output.astype(bf16)
    done = finish(
        at, wq, dkv_own, from_before, from_after, sums, uq, uk, qinv, kinv, small, cos, sin, w_cols
    )
    dn1_pieces = [done[0]] + [along_seq(done[k], k) for k in range(1, 4)]
    keep, send, summed = done[4:]
    o_theirs = other_core(after(o_part, send))
    parts = weight_grads(at, after(n1, output), n1_theirs, keep, other_core(send), o_part, o_theirs)
    halves = chip_sum(at, [parts[0]] + [along_x(parts[k], k) for k in range(1, 4)])
    halves = swap(halves, GROUP)
    input_grad = input_back(at, dn1_pieces, tok, middle_grad, small)
    own = sum_rows(at, after(halves, in_own, down_own, input_grad), summed)
    pieces = gather_x(jnp.concatenate([own, other_core(own)], axis=1))
    qkv_own, o_own, gains_own, key_own, router_own = last(at, pieces, w_qkv, norm_gains)
    return (output[None], input_grad[None], qkv_own, o_own, gains_own, key_own[0], router_own.T, in_own, down_own)


def solution(mesh):
    both = P("expert", GROUP, None)
    rows = P(GROUP, None)
    return jax.shard_map(
        shards,
        mesh=mesh,
        in_specs=(
            both,
            both,
            P("expert", None),
            both,
            P("expert", GROUP),
            rows,
            rows,
            P(None, GROUP),
            P(GROUP),
            rows,
            P("expert", GROUP, None, None),
            P("expert", GROUP, None),
        ),
        out_specs=(
            both,
            both,
            rows,
            rows,
            P(None, GROUP),
            P(GROUP),
            rows,
            P("expert", GROUP, None, None),
            P("expert", GROUP, None),
        ),
        check_vma=False,
    )
```

```python
import jax
import jax.numpy as jnp
from jax import lax
from jax.experimental import pallas as pl
from jax.experimental.pallas import tpu as pltpu
from jax.sharding import PartitionSpec as P

HEADS = 16
KV_HEADS = 8
HEAD_DIM = 64
TOPK = 8
HALF = 512
CAP = 40
PAIR = 2 * CAP
ROWS = 8 * CAP
VMEM_BYTES = 64 * 1024 * 1024

GROUP = ("dp", "seq")
ALL = ("dp", "seq", "expert")
epsilon = 1e-05
highest = lax.Precision.HIGHEST
bf16 = jnp.bfloat16
f32 = jnp.float32


def dot(a, b, dims, **kw):
    return lax.dot_general(a, b, ((dims[0], dims[1]), ((), ())), preferred_element_type=f32, **kw)


def call(kernel, name, out_shape, *args, flops=10**8, scratch=(), moved=10**6, middle=(), stepped={}):
    whole = lambda a: pl.BlockSpec(a.shape, lambda _: (0,) * len(a.shape))
    specs = [pl.BlockSpec(memory_space=pltpu.SMEM)] + [whole(a) for a in args[1:]]
    for i in middle:
        specs[i] = pl.BlockSpec((512, 128), lambda _: (1, 0))
    for i, spec in stepped.items():
        specs[i] = spec
    return pl.pallas_call(
        kernel,
        grid=(1,),
        in_specs=specs,
        out_specs=jax.tree.map(whole, out_shape),
        out_shape=out_shape,
        scratch_shapes=list(scratch),
        compiler_params=pltpu.CompilerParams(vmem_limit_bytes=VMEM_BYTES),
        cost_estimate=pl.CostEstimate(flops=flops, bytes_accessed=moved, transcendentals=0),
        name=name,
    )(*args)


def sds(*shape, dtype=bf16):
    return jax.ShapeDtypeStruct(shape, dtype)


def block(index):
    return pl.ds(pl.multiple_of(index * 128, 128), 128)


def column(row):
    return jnp.broadcast_to(row, (128, 128)).T


def partner(x):
    lane = lax.broadcasted_iota(jnp.int32, x.shape, 1)
    return jnp.where(lane % 64 < 32, pltpu.roll(x, 96, 1), pltpu.roll(x, 32, 1))


def row_sums(x):
    ones = jnp.ones((8, x.shape[1]), f32)
    return dot(ones, x, ((1,), (1,)), precision=highest)[0:1]


def project_kernel(at, t0, t1, t2, t3, mine, theirs, n1_ref, raw_ref, kv_ref, parts_ref, small_ref, w_ref, o_ref, rows):
    s = at[1]
    even = lax.rem(at[2], 2) == 0
    here, there = mine[:, :, :256].reshape(1024, 256), theirs[:, :, :256].reshape(1024, 256)
    w_ref[:, :256] = jnp.where(even, here, there)
    w_ref[:, 256:] = jnp.where(even, there, here)
    o_ref[:, :128] = mine[:, :, 384:].reshape(1024, 128)
    o_ref[:, 128:] = theirs[:, :, 384:].reshape(1024, 128)
    w = w_ref[...]
    lane = lax.broadcasted_iota(jnp.int32, (48, 128), 1)
    for i in range(8):
        low, high = mine[2 * i, :48, 256:384].astype(f32), mine[2 * i + 1, :48, 256:384].astype(f32)
        small_ref[:, 128 * i : 128 * (i + 1)] = jnp.where(lane < 64, low, pltpu.roll(high, 64, 1))
    gain = small_ref[32:33, :]
    for ds, t in enumerate((t0, t1, t2, t3)):
        x = t[...].astype(f32)
        low = (x * lax.rsqrt(jnp.mean(x * x, axis=1, keepdims=True) + epsilon) * gain).astype(bf16)
        turned = low.astype(f32).T.astype(bf16)
        raw = dot(low, w, ((1,), (0,)))
        place = lax.rem(s - ds + 4, 4)
        n1_ref[:, block(place)] = turned
        raw_ref[block(place), :] = raw
        kv_ref[block(place), :] = raw[:, 256:].astype(bf16)
        rows[pl.ds(place, 1), :] = row_sums(raw[:, :256] * raw[:, :256])
        rows[pl.ds(place + 4, 1), :] = row_sums(raw[:, 256:384] * raw[:, 256:384])
    parts_ref[...] = jnp.broadcast_to(rows[...][None], (16, 8, 128))
    start = pl.multiple_of(s * 256, 256)
    chunk = small_ref[35:36, pl.ds(start, 256)]
    at_row = lax.broadcasted_iota(jnp.int32, (256, 128), 0)
    at_col = lax.broadcasted_iota(jnp.int32, (256, 128), 1)
    pick = jnp.where(at_row == 64 * (at_col // 32) + at_col % 32, 1.0, 0.0)
    small_ref[40:41, 0:256] = small_ref[34:35, pl.ds(start, 256)]
    small_ref[40:41, 256:384] = dot(jnp.broadcast_to(chunk, (8, 256)), pick, ((1,), (0,)), precision=highest)[0:1]


def project(at, pieces, mine, theirs):
    return call(
        project_kernel,
        "project",
        [
            sds(1024, 512),
            sds(512, 512, dtype=f32),
            sds(512, 256),
            sds(16, 8, 128, dtype=f32),
            sds(48, 1024, dtype=f32),
            sds(1024, 512),
            sds(1024, 256),
        ],
        at,
        *pieces,
        mine,
        theirs,
        flops=8 * 10**9,
        scratch=[pltpu.VMEM((8, 128), f32)],
    )


def document_of(places, at):
    found = jnp.zeros(places.shape, f32)
    for i in range(4):
        found = found + jnp.where(places >= at[3 + i], 1.0, 0.0)
    return jnp.where((places >= 0) & (places < 2048), found, -1.0)


def mark_documents(at, docs):
    docs[...] = document_of(at[0] * 512 - HALF + lax.broadcasted_iota(jnp.int32, (1536, 128), 0), at)
    apart = lax.broadcasted_iota(jnp.int32, (1152, 128), 0) - lax.broadcasted_iota(jnp.int32, (1152, 128), 1)
    return jnp.where((apart >= 0) & (apart < 2 * HALF), 0.0, -1e30)


def seen_bias(at, b, docs, near):
    first = at[0] * 512 + 128 * b
    query_doc = document_of(first + lax.broadcasted_iota(jnp.int32, (1, 128), 1), at)
    return jnp.where(docs[128 * b : 128 * b + 1152, :] == query_doc, near, -1e30)


def stacked_heads(tile, kh):
    lane = lax.broadcasted_iota(jnp.int32, (128, 128), 1)
    mine = (lane < 64) if kh == 0 else (lane >= 64)
    other = pltpu.roll(tile, 64, 1)
    first, second = (tile, other) if kh == 0 else (other, tile)
    return jnp.concatenate([jnp.where(mine, first, 0.0), jnp.where(mine, second, 0.0)], axis=0).astype(bf16)


def attend_kernel(at, raw, kv0, kv1, kv2, parts, small, cos, sin, p0, p1, p2, p3, attn, qb, kb, vb, lse, uq, uk, qinv, kinv, vt, docs):
    d = at[0]
    near = mark_documents(at, docs)
    for i in range(12):
        there = jnp.clip(d - 1 + i // 4, 0, 3)
        row = parts[4 * there][4 + i % 4 : 5 + i % 4]
        for s in range(1, 4):
            row = row + parts[4 * there + s][4 + i % 4 : 5 + i % 4]
        inverse = column(lax.rsqrt(row * (1.0 / 512) + epsilon))
        span = slice(128 * i, 128 * (i + 1))
        part = slice(128 * (i % 4), 128 * (i % 4 + 1))
        kv = (kv0, kv1, kv2)[i // 4]
        unit = kv[part, :128].astype(f32) * inverse
        key = unit * small[40:41, 256:384]
        uk[span, :] = unit
        kb[span, :] = (key * cos[span, :] + partner(key) * sin[span, :]).astype(bf16)
        value = kv[part, 128:]
        vb[span, :] = value
        vt[:, span] = value.T
        if i // 4 == 1:
            kinv[part, :] = inverse
            row = parts[4 * d][i % 4 : i % 4 + 1]
            for s in range(1, 4):
                row = row + parts[4 * d + s][i % 4 : i % 4 + 1]
            inverse = column(lax.rsqrt(row * (1.0 / 1024) + epsilon))
            qinv[part, :] = inverse
            for m in range(2):
                lanes = slice(128 * m, 128 * (m + 1))
                unit = raw[part, lanes] * inverse
                uq[part, lanes] = unit
                query = unit * small[40:41, lanes]
                qb[part, lanes] = (query * cos[span, :] + partner(query) * sin[span, :]).astype(bf16)
    for b in range(4):
        bias = seen_bias(at, b, docs, near)
        bias = jnp.concatenate([bias, bias], axis=1)
        window = slice(128 * b, 128 * b + 1152)
        for kh in range(2):
            lanes = slice(128 * kh, 128 * (kh + 1))
            heads = stacked_heads(qb[128 * b : 128 * (b + 1), lanes].astype(f32), kh)
            scores = dot(kb[window, :], heads, ((1,), (1,))) * 0.125 + bias
            top = jnp.max(scores, axis=0, keepdims=True)
            weights = jnp.exp(scores - top)
            total = jnp.sum(weights, axis=0, keepdims=True)
            lse[2 * b + kh : 2 * b + kh + 1, :] = top + jnp.log(total)
            mixed = dot(vt[64 * kh : 64 * kh + 64, window], weights.astype(bf16), ((1,), (0,))) / total
            tile = jnp.concatenate([mixed[:, :128], mixed[:, 128:]], axis=0).T
            attn[b, :, lanes] = tile.astype(bf16)
    for k, ref in enumerate((p0, p1, p2, p3)):
        ref[...] = attn[lax.rem(at[1] + k, 4)]


def attend(at, raw, kvs, parts, small, cos, sin):
    return call(
        attend_kernel,
        "attend",
        [sds(128, 256)] * 4
        + [
            sds(4, 128, 256),
            sds(512, 256),
            sds(1536, 128),
            sds(1536, 128),
            sds(8, 256, dtype=f32),
            sds(512, 256, dtype=f32),
            sds(1536, 128, dtype=f32),
            sds(512, 128, dtype=f32),
            sds(512, 128, dtype=f32),
        ],
        at,
        raw,
        *kvs,
        parts,
        small,
        cos,
        sin,
        flops=15 * 10**9,
        scratch=[pltpu.VMEM((128, 1536), bf16), pltpu.VMEM((1536, 128), f32)],
    )


def attend_back_kernel(
    at, g0, g1, g2, g3, qb, kb, vb, lse, uq, uk, cos, sin, base, wq, dkv_own, dkv_up, dkv_down, sums, kt, dk, dv, qgain, qrows, got, docs
):
    near = mark_documents(at, docs)
    for k, ref in enumerate((g0, g1, g2, g3)):
        got[lax.rem(at[1] - k + 4, 4)] = ref[...]
    for i in range(12):
        span = slice(128 * i, 128 * (i + 1))
        kt[:, span] = kb[span, :].T
    dk[...] = jnp.zeros_like(dk)
    dv[...] = jnp.zeros_like(dv)
    qgain[...] = jnp.zeros_like(qgain)
    for b in range(4):
        bias = seen_bias(at, b, docs, near)
        bias = jnp.concatenate([bias, bias], axis=1)
        window = slice(128 * b, 128 * b + 1152)
        own = slice(128 * b, 128 * (b + 1))
        table = slice(HALF + 128 * b, HALF + 128 * (b + 1))
        total = jnp.zeros((128, 1), f32)
        for kh in range(2):
            lanes = slice(128 * kh, 128 * (kh + 1))
            query = qb[own, lanes].astype(f32)
            heads = stacked_heads(query, kh)
            grads = stacked_heads(got[b, :, lanes].astype(f32), kh)
            scores = dot(kb[window, :], heads, ((1,), (1,))) * 0.125 + bias
            probs = jnp.exp(scores - lse[2 * b + kh : 2 * b + kh + 1, :])
            prob_grad = dot(vb[window, :], grads, ((1,), (1,)))
            centre = jnp.sum(probs * prob_grad, axis=0, keepdims=True)
            score_grad = (probs * (prob_grad - centre)).astype(bf16)
            dv[window, :] += dot(probs.astype(bf16), grads, ((1,), (0,)))
            dk[window, :] += dot(score_grad, heads, ((1,), (0,))) * 0.125
            flat = dot(kt[64 * kh : 64 * kh + 64, window], score_grad, ((1,), (0,))) * 0.125
            dq = jnp.concatenate([flat[:, :128], flat[:, 128:]], axis=0).T.astype(bf16).astype(f32)
            total = total + jnp.sum(dq * query, axis=1, keepdims=True)
            turned = dq * cos[table, :] - partner(dq) * sin[table, :]
            wq[own, lanes] = turned
            qgain[0:1, lanes] += jnp.sum(turned * uq[own, lanes], axis=0, keepdims=True)
        qrows[b : b + 1, :] = jnp.broadcast_to(total, (128, 128)).T[0:1]
    kgain = jnp.zeros((1, 128), f32)
    krows = []
    for i in range(12):
        span = slice(128 * i, 128 * (i + 1))
        part = slice(128 * (i % 4), 128 * (i % 4 + 1))
        grad = dk[span, :]
        spot = jnp.sum(grad * kb[span, :].astype(f32), axis=1, keepdims=True)
        krows.append(jnp.broadcast_to(spot, (128, 128)).T[0:1])
        turned = grad * cos[span, :] - partner(grad) * sin[span, :]
        kgain = kgain + jnp.sum(turned * uk[span, :], axis=0, keepdims=True)
        target = (dkv_down, dkv_own, dkv_up)[i // 4]
        target[part, :128] = grad.astype(target.dtype)
        target[part, 128:] = dv[span, :].astype(target.dtype)
    lane = lax.broadcasted_iota(jnp.int32, (1, 128), 1)
    none = jnp.zeros((6, 128), f32)
    for there in range(4):
        here = jnp.where(at[0] == there, 1.0, 0.0)
        mine = jnp.where(at[1] == there, 1.0, 0.0)
        rows = [qrows[0:4, :] * here]
        for i in range(4):
            row = jnp.zeros((1, 128), f32)
            for part in range(3):
                row = row + krows[4 * part + i] * jnp.where(at[0] - 1 + part == there, 1.0, 0.0)
            rows.append(row)
        for s in range(4):
            q_tile = qgain[0:1, 128 * (s // 2) : 128 * (s // 2 + 1)]
            if s % 2:
                q_tile = pltpu.roll(q_tile, 64, 1)
            k_tile = pltpu.roll(kgain, (64 - 32 * s) % 128, 1)
            gains = jnp.where(lane < 64, q_tile, jnp.where(lane < 96, k_tile, 0.0)) * mine
            more = base[4 * there + s]
            sums[4 * there + s] = jnp.concatenate(rows + [gains, more[0:1], none, more[8:24]], axis=0).astype(bf16)


def attend_back(at, gots, qb, kb, vb, lse, uq, uk, cos, sin, base):
    return call(
        attend_back_kernel,
        "attend_back",
        [
            sds(512, 256, dtype=f32),
            sds(512, 256, dtype=f32),
            sds(512, 256),
            sds(512, 256),
            sds(16, 32, 128),
        ],
        at,
        *gots,
        qb,
        kb,
        vb,
        lse,
        uq,
        uk,
        cos,
        sin,
        base,
        flops=30 * 10**9,
        scratch=[
            pltpu.VMEM((128, 1536), bf16),
            pltpu.VMEM((1536, 128), f32),
            pltpu.VMEM((1536, 128), f32),
            pltpu.VMEM((8, 256), f32),
            pltpu.VMEM((8, 128), f32),
            pltpu.VMEM((4, 128, 512), bf16),
            pltpu.VMEM((1536, 128), f32),
        ],
    )


def route_kernel(at, *refs):
    place_ref, used_ref, gs_ref = refs[8:]
    ids = lax.broadcasted_iota(jnp.int32, (32, 128), 0) + 4 * at[2]
    ids = jnp.where(ids >= 32, ids - 32, ids).astype(f32)
    slot = lax.broadcasted_iota(jnp.int32, (CAP, 128), 0).astype(f32)
    empty = jnp.zeros((CAP, 128), f32)
    hits = []
    for j, ref in enumerate(refs[:8]):
        meta = ref[:, 1024:].astype(f32)
        turned = meta.T
        used = turned[0:1] == ids
        for k in range(1, TOPK):
            used = used | (turned[k : k + 1] == ids)
        used_ref[j] = jnp.where(used, 1.0, 0.0)
        earlier = jnp.where(meta[:, 8:9] < turned[8:9], 1.0, 0.0).astype(bf16)
        before = dot(jnp.where(used, 1.0, 0.0).astype(bf16), earlier, ((1,), (0,)))
        spot = jnp.where(used & (before < CAP), before, 1000.0)
        hits.append([jnp.where(slot == spot[l : l + 1], 1.0, 0.0) for l in range(4)])
    for p in range(4):
        rows = []
        for l in range(4):
            rows.append(jnp.concatenate([hits[2 * p][l], empty], axis=1))
            rows.append(jnp.concatenate([empty, hits[2 * p + 1][l]], axis=1))
        chosen = jnp.concatenate(rows, axis=0).astype(bf16)
        place_ref[p] = chosen
        both = jnp.concatenate([refs[2 * p][:, :1024], refs[2 * p + 1][:, :1024]], axis=0)
        ups = dot(chosen, both, ((1,), (0,))).astype(bf16)
        for l in range(4):
            gs_ref[l, PAIR * p : PAIR * (p + 1), :] = ups[PAIR * l : PAIR * (l + 1)]


def route(at, cots):
    return call(
        route_kernel,
        "route",
        [sds(4, 4 * PAIR, 256), sds(8, 32, 128, dtype=f32), sds(4, ROWS, 1024)],
        at,
        *cots,
        flops=0,
        moved=0,
    )


def expert_step(where_ref, *refs):
    n2_refs = refs[0:8]
    place, used_ref, gs, small, weights = refs[8:13]
    results, grads_ref = refs[13:17], refs[17]
    xs, gate, ys, dxs, dgs, held = refs[18:24]
    staged, load_sems, store_sems = refs[24:28], refs[28], refs[29]
    dn_refs = tuple(ref.at[i] for ref in staged[:2] for i in range(4))
    out_refs = tuple(ref.at[i] for ref in staged[2:] for i in range(4))
    step = pl.program_id(0)
    slot = lax.rem(step, 2)
    load = lambda l, s: pltpu.make_async_copy(weights.at[:, l], held.at[s], load_sems.at[s])
    stores = [pltpu.make_async_copy(staged[i], results[i], store_sems.at[i]) for i in range(4)]

    @pl.when(step == 0)
    def _():
        load(0, 0).start()
        load(1, 1).start()
        router_t = small[0:32, :].astype(bf16)
        back = lax.rem(32 - 4 * where_ref[0], 32)
        for p in range(4):
            both = jnp.concatenate([n2_refs[2 * p][...], n2_refs[2 * p + 1][...]], axis=0)
            used = jnp.concatenate([used_ref[2 * p], used_ref[2 * p + 1]], axis=1) > 0.5
            logits = pltpu.roll(dot(router_t, both, ((1,), (1,))), back, 0)
            masked = jnp.where(used, logits, -1e30)
            grown = jnp.where(used, jnp.exp(masked - jnp.max(masked, axis=0, keepdims=True)), 0.0)
            gates = grown / jnp.sum(grown, axis=0, keepdims=True)
            chosen = place[p]
            rows = dot(chosen, both, ((1,), (0,))).astype(bf16)
            hit = chosen.astype(f32)
            span = slice(PAIR * p, PAIR * (p + 1))
            for l in range(4):
                part = slice(PAIR * l, PAIR * (l + 1))
                share = jnp.sum(hit[part] * gates[l : l + 1], axis=1, keepdims=True)
                gate[l, span, :] = jnp.broadcast_to(share, (PAIR, 128))
                xs[l, span, :] = rows[part]

    load(step, slot).wait()
    w_in = held[slot, :, :64, :].reshape(1024, 1024)
    w_out = held[slot, :, 64:, :].reshape(512, 1024)
    x = xs[step]
    both = dot(x, w_in, ((1,), (0,)))
    gate_part, up_part = both[:, :512], both[:, 512:]
    sig = jax.nn.sigmoid(gate_part)
    silu = gate_part * sig
    hidden = (silu * up_part).astype(bf16)
    g = gs[0].astype(f32)
    share = gate[step][:, 0:1]
    dy = (g * share).astype(bf16)
    dh = dot(dy, w_out, ((1,), (1,)))
    dgu = jnp.concatenate(
        [dh * up_part * (sig * (1.0 + gate_part * (1.0 - sig))), dh * silu], axis=1
    ).astype(bf16)
    dxs[step] = dot(dgu, w_in, ((1,), (1,))).astype(bf16)
    y = dot(hidden, w_out, ((1,), (0,))).astype(bf16).astype(f32)
    ys[step] = (y * share).astype(bf16)
    lane = lax.broadcasted_iota(jnp.int32, (ROWS, 128), 1)
    dgate = jnp.sum(g * y, axis=1, keepdims=True)
    dgs[step] = jnp.where(lane == 4 * where_ref[0] + step, dgate, 0.0).astype(bf16)

    @pl.when(step == 3)
    def _():
        for p in range(4):
            chosen = place[p]
            span = slice(PAIR * p, PAIR * (p + 1))
            for source, targets, lo, hi in ((dxs, dn_refs, 0, 1024), (dgs, dn_refs, 1024, 1152), (ys, out_refs, 0, 1024)):
                stacked = jnp.concatenate([source[l, span, :] for l in range(4)], axis=0)
                total = dot(chosen, stacked, ((0,), (0,))).astype(bf16)
                targets[2 * p][:, lo:hi] = total[:128]
                targets[2 * p + 1][:, lo:hi] = total[128:]
        for store in stores:
            store.start()

    @pl.when(step < 2)
    def _():
        load(step + 2, slot).start()

    grads_ref[:, 0, :64, :] = dot(x, dgu, ((0,), (0,))).astype(bf16).reshape(16, 64, 1024)
    grads_ref[:, 0, 64:, :] = dot(hidden, dy, ((0,), (0,))).astype(bf16).reshape(16, 32, 1024)

    @pl.when(step == 3)
    def _():
        for store in stores:
            store.wait()


def experts(e_index, n2s, place, used, gs, small, weights):
    whole = lambda *s: pl.BlockSpec(s, lambda i, *_: (0,) * len(s))
    each = lambda cols: pl.BlockSpec((1, ROWS, cols), lambda i, *_: (i, 0, 0))
    owned = pl.BlockSpec((16, 1, 96, 1024), lambda i, *_: (0, i, 0, 0))
    shape = lambda *s: jax.ShapeDtypeStruct(s, bf16)
    return pl.pallas_call(
        expert_step,
        grid_spec=pltpu.PrefetchScalarGridSpec(
            num_scalar_prefetch=1,
            grid=(4,),
            in_specs=[whole(128, 1024)] * 8
            + [
                whole(4, 4 * PAIR, 256),
                whole(8, 32, 128),
                each(1024),
                whole(48, 1024),
                pl.BlockSpec(memory_space=pl.ANY),
            ],
            out_specs=[pl.BlockSpec(memory_space=pl.ANY)] * 4 + [owned],
            scratch_shapes=[
                pltpu.VMEM((4, ROWS, 1024), bf16),
                pltpu.VMEM((4, ROWS, 128), f32),
                pltpu.VMEM((4, ROWS, 1024), bf16),
                pltpu.VMEM((4, ROWS, 1024), bf16),
                pltpu.VMEM((4, ROWS, 128), bf16),
                pltpu.VMEM((2, 16, 96, 1024), bf16),
                pltpu.VMEM((4, 128, 1152), bf16),
                pltpu.VMEM((4, 128, 1152), bf16),
                pltpu.VMEM((4, 128, 1024), bf16),
                pltpu.VMEM((4, 128, 1024), bf16),
                pltpu.SemaphoreType.DMA((2,)),
                pltpu.SemaphoreType.DMA((4,)),
            ],
        ),
        out_shape=[shape(4, 128, 1152)] * 2
        + [shape(4, 128, 1024)] * 2
        + [shape(16, 4, 96, 1024)],
        compiler_params=pltpu.CompilerParams(vmem_limit_bytes=VMEM_BYTES),
        cost_estimate=pl.CostEstimate(flops=28 * 10**9, bytes_accessed=40 * 10**6, transcendentals=10**6),
        name="experts",
    )(e_index, *n2s, place, used, gs, small, weights)


def split(x):
    high = x.astype(bf16)
    return high, (x - high.astype(f32)).astype(bf16)


def o_pieces(at, refs):
    core = lax.rem(at[2], 2)
    for k, ref in enumerate(refs):
        chip = lax.rem(at[2] // 2 - k + 4, 4)
        yield block(2 * chip + core), ref[:, :128]
        yield block(2 * chip + 1 - core), ref[:, 128:]


def quarter(index):
    return pl.ds(pl.multiple_of(256 * index, 256), 256)


def middle_kernel(at, tok, a0, a1, a2, a3, o0, o1, o2, o3, small, middle_ref, low_ref, inverse_ref, rows_ref):
    for k, ref in enumerate((a0, a1, a2, a3)):
        rows_ref[:, quarter(lax.rem(at[1] - k + 4, 4))] = ref[...]
    rows = rows_ref[...]
    for lanes, piece in o_pieces(at, (o0, o1, o2, o3)):
        middle_ref[:, lanes] = tok[:, lanes].astype(f32) + dot(rows, piece, ((1,), (0,)))
    total = middle_ref[...]
    inverse = lax.rsqrt(jnp.mean(total * total, axis=1, keepdims=True) + epsilon)
    low_ref[...] = (total * inverse * small[33:34]).astype(bf16)
    inverse_ref[...] = jnp.broadcast_to(inverse, (128, 128))


def make_middle(at, tok, attns, parts, small):
    return call(
        middle_kernel,
        "middle",
        [sds(128, 1024, dtype=f32), sds(128, 1024), sds(128, 128, dtype=f32)],
        at,
        tok,
        *attns,
        *parts,
        small,
        flops=6 * 10**9,
        scratch=[pltpu.VMEM((128, 1024), bf16)],
    )


def middle_back_kernel(
    at, p0a, p0b, p1, p2, p3, middle, inverse_ref, low, cot, small, o0, o1, o2, o3, grad_ref, s0, s1, s2, s3, sums_ref, branch_ref, back_ref
):
    total = p0a[0].astype(f32) + p0b[0].astype(f32) + p1[...].astype(f32) + p2[...].astype(f32) + p3[...].astype(f32)
    dgates = total[:, 1024:1056]
    router_t = small[0:32].astype(bf16)
    logits = dot(low[...], router_t, ((1,), (1,)))
    ids = lax.broadcasted_iota(jnp.int32, (128, 32), 1).astype(f32)
    named = cot[:, 1024:].astype(f32)
    used = named[:, 0:1] == ids
    for k in range(1, TOPK):
        used = used | (named[:, k : k + 1] == ids)
    masked = jnp.where(used, logits, -1e30)
    grown = jnp.where(used, jnp.exp(masked - jnp.max(masked, axis=1, keepdims=True)), 0.0)
    gates = grown / jnp.sum(grown, axis=1, keepdims=True)
    logit_grad = gates * (dgates - jnp.sum(gates * dgates, axis=1, keepdims=True))
    high, rest = split(logit_grad)
    dn2 = total[:, :1024] + dot(high, router_t, ((1,), (0,))) + dot(rest, router_t, ((1,), (0,)))
    inverse = inverse_ref[:, 0:1]
    unit = middle[...] * inverse
    scaled = dn2 * small[33:34]
    grad = cot[:, :1024].astype(f32) + inverse * (scaled - unit * jnp.mean(scaled * unit, axis=1, keepdims=True))
    grad_ref[...] = grad
    branch = grad.astype(bf16)
    branch_ref[...] = branch
    back = jnp.zeros((128, 1024), f32)
    for lanes, piece in o_pieces(at, (o0, o1, o2, o3)):
        back = back + dot(branch_ref[:, lanes], piece, ((1,), (1,)))
    back_ref[...] = back.astype(bf16)
    for k, ref in enumerate((s0, s1, s2, s3)):
        lanes = quarter(lax.rem(at[1] + k, 4))
        ref[:, 0:256] = back_ref[:, lanes]
        ref[:, 256:512] = branch_ref[:, lanes]
    routers = dot(high, low[...], ((0,), (0,))) + dot(rest, low[...], ((0,), (0,)))
    second = jnp.sum(dn2 * unit, axis=0, keepdims=True)
    lane = lax.broadcasted_iota(jnp.int32, (16, 128), 1)
    for i in range(16):
        lanes = slice(128 * (i // 2), 128 * (i // 2 + 1))
        upper, lower, row = routers[0:16, lanes], routers[16:32, lanes], second[:, lanes]
        if i % 2 == 0:
            tile = jnp.where(lane < 64, upper, pltpu.roll(lower, 64, 1))
        else:
            tile = jnp.where(lane < 64, pltpu.roll(upper, 64, 1), lower)
            row = pltpu.roll(row, 64, 1)
        sums_ref[i] = jnp.concatenate([row, jnp.zeros((7, 128), f32), tile], axis=0)


def middle_back(at, pieces, middle, inverse, low, cot, small, parts):
    return call(
        middle_back_kernel,
        "middle_back",
        [sds(128, 1024, dtype=f32)] + [sds(128, 512)] * 4 + [sds(16, 24, 128, dtype=f32)],
        at,
        *pieces,
        middle,
        inverse,
        low,
        cot,
        small,
        *parts,
        flops=12 * 10**9,
        scratch=[pltpu.VMEM((128, 1024), bf16)] * 2,
    )


def out_grad_kernel(at, a0, a1, a2, a3, g0, g1, g2, g3, out_ref, cols):
    for k, ref in enumerate((g0, g1, g2, g3)):
        cols[block(lax.rem(at[1] - k + 4, 4)), :] = ref[:, 256:512]
    for k, part in enumerate((a0, a1, a2, a3)):
        rows = jnp.concatenate([part[i] for i in range(4)], axis=0)
        out_ref[quarter(lax.rem(at[1] - k + 4, 4)), :] = dot(rows, cols[...], ((0,), (0,))).astype(bf16)


def out_grads(at, attns, gots):
    scratch = [pltpu.VMEM((512, 256), bf16)]
    return call(out_grad_kernel, "out_grads", sds(1024, 256), at, *attns, *gots, flops=0, moved=0, scratch=scratch)


def finish_kernel(
    at, wq, own, up, down, sums, uq, uk, qinv, kinv, small, cos, sin, w_ref,
    dn0, dn1, dn2, dn3, keep_ref, send_ref, sums_ref, dqkv,
):
    got = sums[0].astype(f32)
    for i in range(1, 16):
        got = got + sums[i].astype(f32)
    sums_ref[...] = got
    for i in range(4):
        part = slice(128 * i, 128 * (i + 1))
        q_mean = column(got[i : i + 1]) * (1.0 / 1024)
        for m in range(2):
            lanes = slice(128 * m, 128 * (m + 1))
            grad = wq[part, lanes] * small[40:41, lanes] - uq[part, lanes] * q_mean
            dqkv[part, lanes] = (qinv[part, :] * grad).astype(bf16)
        total = own[part, :] + up[part, :].astype(f32) + down[part, :].astype(f32)
        dk = total[:, :128].astype(bf16).astype(f32)
        turned = dk * cos[part, :] - partner(dk) * sin[part, :]
        k_mean = column(got[4 + i : 5 + i]) * (1.0 / 512)
        grad = turned * small[40:41, 256:384] - uk[part, :] * k_mean
        dqkv[part, 256:384] = (kinv[part, :] * grad).astype(bf16)
        dqkv[part, 384:512] = total[:, 128:].astype(bf16)
    w = w_ref[...]
    for k, ref in enumerate((dn0, dn1, dn2, dn3)):
        ref[...] = dot(dqkv[block(lax.rem(at[1] + k, 4)), :], w, ((1,), (1,))).astype(bf16)
    even = lax.rem(at[2], 2) == 0
    left = dqkv[:, :384]
    right = jnp.concatenate([dqkv[:, 384:], jnp.zeros((512, 256), bf16)], axis=1)
    keep_ref[...] = jnp.where(even, left, right)
    send_ref[...] = jnp.where(even, right, left)


def finish(at, wq, own, up, down, sums, uq, uk, qinv, kinv, small, cos, sin, w_cols):
    return call(
        finish_kernel,
        "finish",
        [sds(128, 1024)] * 4 + [sds(512, 384)] * 2 + [sds(sums.shape[1], 128, dtype=f32)],
        at, wq, own, up, down, sums, uq, uk, qinv, kinv, small, cos, sin, w_cols,
        middle=(7, 11, 12),
        flops=10 * 10**9,
        scratch=[pltpu.VMEM((512, 512), bf16)],
    )


def weight_kernel(at, n1, n1_theirs, keep, got, o_part, o_theirs, r0, r1, r2, r3, grads):
    total = dot(n1[...], keep[...], ((1,), (0,))) + dot(n1_theirs[...], got[...], ((1,), (0,)))
    odd = lax.rem(at[2], 2).astype(f32)
    outs = (o_part[...].astype(f32) + o_theirs[...].astype(f32)) * odd
    grads[:, :, :128] = total[:, :128].astype(bf16).reshape(16, 64, 128)
    grads[:, :, 128:] = (total[:, 128:] + outs).astype(bf16).reshape(16, 64, 256)
    for k, ref in enumerate((r0, r1, r2, r3)):
        ref[...] = grads[:, pl.ds(pl.multiple_of(16 * lax.rem(at[2] // 2 + k, 4), 16), 16), :]


def weight_grads(at, *args):
    return call(
        weight_kernel,
        "weight_grads",
        [sds(16, 16, 384)] * 4,
        at,
        *args,
        flops=8 * 10**9,
        scratch=[pltpu.VMEM((16, 64, 384), bf16)],
    )


def input_kernel(at, p0, p1, p2, p3, tok, grad_ref, small, out_ref):
    dn1 = p0[...].astype(f32) + p1[...].astype(f32) + p2[...].astype(f32) + p3[...].astype(f32)
    x = tok[...].astype(f32)
    inverse = lax.rsqrt(jnp.mean(x * x, axis=1, keepdims=True) + epsilon)
    unit = x * inverse
    scaled = dn1 * small[32:33]
    out_ref[...] = grad_ref[...] + inverse * (scaled - unit * jnp.mean(scaled * unit, axis=1, keepdims=True))


def input_back(at, pieces, tok, grad, small):
    return call(input_kernel, "input_back", sds(128, 1024, dtype=f32), at, *pieces, tok, grad, small, flops=0, moved=0)


def pack_kernel(at, w_ref, o_ref, router_ref, gain_ref, key_ref, in_ref, down_ref, out_ref, moe_ref):
    moe_ref[:, :64, :] = in_ref[...]
    moe_ref[:, 64:, :] = down_ref[...]
    even = lax.rem(at[2], 2) == 0
    piece = o_ref[:, block(at[2])]
    key = jnp.concatenate([key_ref[...].astype(f32), jnp.zeros((1, 32), f32)], axis=1)
    extra = jnp.concatenate(
        [router_ref[...].astype(f32), gain_ref[...].astype(f32), key, jnp.zeros((28, 64), f32)], axis=0
    )
    extra = jnp.concatenate([extra, jnp.zeros((64, 64), f32)], axis=1).astype(bf16)
    for s in range(4):
        queries = w_ref[:, 256 * s : 256 * (s + 1)]
        keys = w_ref[:, 1024 + 128 * s : 1024 + 128 * (s + 1)]
        values = w_ref[:, 1536 + 128 * s : 1536 + 128 * (s + 1)]
        half = jnp.where(even, queries, jnp.concatenate([keys, values], axis=1))
        for d in range(4):
            out_ref[4 * d + s, :, 0:256] = half
            out_ref[4 * d + s, :, 256:384] = extra
            out_ref[4 * d + s, :, 384:512] = piece


def pack(at, *args):
    return call(pack_kernel, "pack", [sds(16, 64, 512), sds(4, 96, 1024)], at, *args, flops=10**9)


def last_kernel(at, *refs):
    pieces, (w_ref, gain_ref, qkv_ref, o_ref, gains_ref, key_ref, router_ref) = refs[:4], refs[4:]
    even = lax.rem(at[2], 2) == 0
    sums = jnp.zeros((16, 256), f32)
    for k in range(4):
        rows = pl.ds(pl.multiple_of(16 * lax.rem(at[2] // 2 - k + 4, 4), 16), 16)
        mine, theirs = pieces[k][:, :1792].astype(f32), pieces[k][:, 1792:].astype(f32)
        sums = sums + mine[:, 1536:] + theirs[:, 1536:]
        first, later = jnp.where(even, mine, theirs), jnp.where(even, theirs, mine)
        for s in range(4):
            lanes = 384 * s
            qkv_ref[rows, 256 * s : 256 * (s + 1)] = first[:, lanes : lanes + 256]
            qkv_ref[rows, 1024 + 128 * s : 1024 + 128 * (s + 1)] = first[:, lanes + 256 : lanes + 384]
            qkv_ref[rows, 1536 + 128 * s : 1536 + 128 * (s + 1)] = later[:, lanes : lanes + 128]
            o_ref[rows, 256 * s : 256 * (s + 1)] = later[:, lanes + 128 : lanes + 384]
    first_gain = row_sums(qkv_ref[...] * w_ref[...].astype(f32)) / gain_ref[...].astype(f32)[0:1, :]
    gains_ref[0:1, :] = first_gain
    gains_ref[1:2, :] = sums[9:10, 128:192]
    gains_ref[2:3, :] = sums[8:9, 128:192]
    key_ref[...] = sums[8:9, 192:224]
    router_ref[...] = jnp.concatenate([sums[:, :64], sums[:, 64:128]], axis=0)


def last(at, pieces, w_qkv, norm_gains):
    return call(
        last_kernel,
        "last",
        [
            sds(64, 2048, dtype=f32),
            sds(64, 1024, dtype=f32),
            sds(3, 64, dtype=f32),
            sds(1, 32, dtype=f32),
            sds(32, 64, dtype=f32),
        ],
        at, *pieces, w_qkv, norm_gains,
    )


def chip_kernel(at, r0, r1, r2, r3, out_ref):
    total = r0[...].astype(f32) + r1[...].astype(f32) + r2[...].astype(f32) + r3[...].astype(f32)
    out_ref[...] = total.astype(bf16)


def chip_sum(at, pieces):
    return call(chip_kernel, "chip_sum", sds(*pieces[0].shape), at, *pieces, flops=0, moved=0)


def rows_kernel(at, got, sums, out_ref):
    for s in range(4):
        total = got[s].astype(f32)
        for d in range(1, 4):
            total = total + got[4 * d + s].astype(f32)
        out_ref[:, 384 * s : 384 * (s + 1)] = total.astype(bf16)
    out_ref[:, 1536:1664] = sums[16:32, :].astype(bf16)
    out_ref[:, 1664:1792] = sums[0:16, :].astype(bf16)


def sum_rows(at, got, sums):
    return call(rows_kernel, "sum_rows", sds(16, 1792), at, got, sums, flops=0, moved=0)


def join_kernel(at, *refs):
    for k in range(3):
        refs[6 + k][...] = (refs[k][0].astype(f32) + refs[3 + k][0].astype(f32)).astype(bf16)


def join(at, mine, theirs):
    shape = mine.shape[1:]
    specs = [pl.BlockSpec((1,) + shape, lambda _, k=k: (k, 0, 0)) for k in range(1, 4)] * 2
    args = [mine] * 3 + [theirs] * 3
    stepped = dict(enumerate(specs, 1))
    return call(join_kernel, "join", [sds(*shape)] * 3, at, *args, stepped=stepped, flops=0, moved=0)


def swap(array, axis):
    return lax.all_to_all(array, axis, split_axis=0, concat_axis=0, tiled=True)


def spread(array, axis, ways):
    return swap(jnp.broadcast_to(array[None], (ways,) + array.shape), axis)


def along_seq(array, k):
    return lax.ppermute(array, "seq", [(i, (i + k) % 4) for i in range(4)])


def along_dp(array, k):
    return lax.ppermute(array, "dp", [(i, (i + k) % 4) for i in range(4)])


def along_x(array, k):
    return lax.ppermute(array, "expert", [(i, (i + 2 * k) % 8) for i in range(8)])


def other_core(array):
    return lax.ppermute(array, "expert", [(i, i ^ 1) for i in range(8)])


def gather_x(array):
    return [array] + [along_x(array, k) for k in range(1, 4)]


def return_x(mine, joined, sums):
    return [mine, joined] + [along_x(sums[k - 1], -k) for k in range(1, 4)]


def after(values, *others):
    return lax.optimization_barrier((values, others))[0]


def shards(tokens, cotangent, doc_lengths, routes, route_rank, w_qkv, w_o, norm_gains, key_gain, w_router, w_in, w_out):
    d_index = lax.axis_index("dp")
    s_index = lax.axis_index("seq")
    e_index = lax.axis_index("expert")
    lengths = doc_lengths[0]
    tok = tokens[0]
    place = jnp.stack([d_index, s_index, e_index]).astype(jnp.int32)
    ends = [lengths[0]]
    for i in range(1, 4):
        ends.append(ends[-1] + lengths[i])
    at = jnp.concatenate([place, jnp.stack(ends)])
    w_send, moe_shard = pack(
        place, w_qkv, w_o, w_router.T, norm_gains, key_gain[None], w_in.reshape(4, 64, 1024), w_out
    )
    w_mine = swap(w_send, GROUP)
    tok_pieces = [tok] + [along_seq(tok, k) for k in range(1, 4)]
    cot = jnp.concatenate(
        [cotangent[0], routes[0].astype(bf16), route_rank[0].astype(bf16)[:, None], jnp.zeros((128, 119), bf16)], axis=1
    )
    cots = gather_x(cot)
    places = d_index * 512 - HALF + jnp.arange(1536, dtype=jnp.int32)
    starts = [jnp.zeros((), jnp.int32)] + ends
    begins = jnp.zeros((1536,), jnp.int32)
    for start in starts:
        begins = jnp.maximum(begins, jnp.where(places >= start, start, 0))
    lane = jnp.arange(128, dtype=jnp.int32)
    frequency = 10000.0 ** (-(lane % 32).astype(f32) / 32)
    angles = (places - begins).astype(f32)[:, None] * frequency[None, :]
    cos = jnp.cos(angles)
    sin = jnp.sin(angles) * jnp.where(lane % 64 < 32, -1.0, 1.0)[None, :]

    moe_shard = after(moe_shard, tok_pieces[1], tok_pieces[3])
    moe_all = lax.all_gather(moe_shard, GROUP, axis=0, tiled=False)
    w_mine, cots = after((w_mine, cots), cos, sin, tok_pieces)
    w_theirs = other_core(w_mine)
    n1, raw, kv, parts, small, w_cols, o_pair = project(at, tok_pieces, w_mine, w_theirs)
    up = [(i, i + 1) for i in range(3)]
    down = [(i + 1, i) for i in range(3)]
    kv_before = lax.ppermute(kv, "dp", up)
    kv_after = lax.ppermute(kv, "dp", down)
    cots = cots + [other_core(c) for c in after(cots, kv_before)]
    parts = swap(parts, GROUP)
    o_parts = gather_x(after(o_pair, kv_before))
    *attn_send, attn, qb, kb, vb, lse, uq, uk, qinv, kinv = attend(at, raw, [kv_before, kv, kv_after], parts, small, cos, sin)
    attn_got = [attn_send[0]] + [along_seq(attn_send[k], k) for k in range(1, 4)]
    middle, n2, inverse = make_middle(at, tok, attn_got, o_parts, small)
    routed = route(at, after(cots, n2))
    n2s = after(gather_x(n2), routed)
    n2s = n2s + [other_core(n) for n in n2s]
    made = experts(e_index[None].astype(jnp.int32), n2s, *routed, small, moe_all)
    attns = [attn] + [along_seq(attn, k) for k in range(1, 4)]
    made = after(made, attns)
    joined = other_core(made[1])
    sums = join(at, made[0], joined)
    n1_theirs = other_core(after(n1, sums))
    out_joined = other_core(after(made[3], sums))
    out_sums = join(at, made[2], out_joined)
    dn_pieces = after(return_x(made[0], joined, sums), n1_theirs, out_sums)
    moe_own = lax.psum_scatter(made[4].reshape(16 * 384, 1024), GROUP, scatter_dimension=0, tiled=True)
    moe_own = moe_own.reshape(4, 96, 1024).astype(f32)
    in_own = moe_own[:, :64].reshape(4, 64, 2, 512)
    down_own = moe_own[:, 64:]
    middle_grad, *grad_send, base = middle_back(at, dn_pieces, middle, inverse, n2, cot, small, o_parts)
    grad_got = [grad_send[0]] + [along_seq(grad_send[k], k) for k in range(1, 4)]
    out_pieces = [along_x(out_sums[k - 1], -k) for k in range(1, 4)]
    wq, dkv_own, dkv_up, dkv_down, sums = attend_back(at, grad_got, qb, kb, vb, lse, uq, uk, cos, sin, base)
    from_before = lax.ppermute(dkv_up, "dp", up)
    from_after = lax.ppermute(dkv_down, "dp", down)
    sums = swap(after(sums, out_pieces), GROUP)
    o_part = out_grads(at, attns, after(grad_got, wq))
    output = middle + made[2][0].astype(f32) + out_joined[0].astype(f32)
    for piece in out_pieces:
        output = output + piece.astype(f32)
    output = output.astype(bf16)
    done = finish(
        at, wq, dkv_own, from_before, from_after, sums, uq, uk, qinv, kinv, small, cos, sin, w_cols
    )
    dn1_pieces = [done[0]] + [along_seq(done[k], k) for k in range(1, 4)]
    keep, send, summed = done[4:]
    o_theirs = other_core(after(o_part, send))
    parts = weight_grads(at, after(n1, output), n1_theirs, keep, other_core(send), o_part, o_theirs)
    halves = chip_sum(at, [parts[0]] + [along_x(parts[k], k) for k in range(1, 4)])
    halves = swap(halves, GROUP)
    input_grad = input_back(at, dn1_pieces, tok, middle_grad, small)
    own = sum_rows(at, after(halves, in_own, down_own, input_grad), summed)
    pieces = gather_x(jnp.concatenate([own, other_core(own)], axis=1))
    qkv_own, o_own, gains_own, key_own, router_own = last(at, pieces, w_qkv, norm_gains)
    return (output[None], input_grad[None], qkv_own, o_own, gains_own, key_own[0], router_own.T, in_own, down_own)


def solution(mesh):
    both = P("expert", GROUP, None)
    rows = P(GROUP, None)
    return jax.shard_map(
        shards,
        mesh=mesh,
        in_specs=(
            both,
            both,
            P("expert", None),
            both,
            P("expert", GROUP),
            rows,
            rows,
            P(None, GROUP),
            P(GROUP),
            rows,
            P("expert", GROUP, None, None),
            P("expert", GROUP, None),
        ),
        out_specs=(
            both,
            both,
            rows,
            rows,
            P(None, GROUP),
            P(GROUP),
            rows,
            P("expert", GROUP, None, None),
            P("expert", GROUP, None),
        ),
        check_vma=False,
    )
```
